128 devices in a mesh: dom: 64 (over z, x, y_lo, core), hid: 2 (over y_hi).
Axes of the slice: x: 4, y: 4 (y_hi: 2, y_lo: 2; y = y_hi * 2 + y_lo), z: 4, core: 2. Of those that a mesh axis runs over, the one named last changes fastest.
Arguments:
- node_latent: bfloat16 [16384, 512], P('dom'), may hold values from -6 to 6
- edge_latent: bfloat16 [65536, 512], P('dom'), may hold values from -6 to 6
- send_rows: int32 [64, 2, 64], P('dom'), may hold values from 0 to 255, as said below
- edge_src: int32 [65536], P('dom'), may hold values from 0 to 383, as said below
- edge_dst: int32 [65536], P('dom'), may hold values from 0 to 255
- edge_live: int32 [64], P('dom'), may hold values from 512 to 1024, as said below
- w_in_blocks: bfloat16 [1536, 1536], P(None, 'hid'), may hold values from -0.15625 to 0.15625
- w_in_scale: float32 [12, 12], P(None, 'hid'), may hold values from 0.25 to 4
- bias_in: float32 [1536], P('hid'), may hold values from -4 to 4
- w_out_blocks: bfloat16 [1536, 512], P('hid'), may hold values from -0.15625 to 0.15625
- w_out_scale: float32 [12, 4], P('hid'), may hold values from 0.25 to 4
- bias_out: float32 [512], replicated, may hold values from -4 to 4
- norm_gain: float32 [512], replicated, may hold values from 0.1 to 1.9
- grad_edge: bfloat16 [65536, 512], P('dom'), may hold values from -6 to 6
- grad_agg: bfloat16 [16384, 512], P('dom'), may hold values from -6 to 6
Outputs:
- grad_edge_in: bfloat16 [65536, 512], P(('dom', 'hid'))
- grad_node: bfloat16 [16384, 512], P('dom', 'hid')
- grad_w_in: float32 [1536, 1536], P(None, 'hid')
- grad_bias_in: float32 [1536], P('hid')
- grad_w_out: float32 [1536, 512], P('hid')
- grad_vectors: float32 [3, 512], replicated
The draws below stay inside these ranges and needn't reach their ends.
Inputs may be any that keep to these rules, and one draw needn't show every extreme that they name: send_rows[p, 0] and send_rows[p, 1] together name 128 distinct nodes of partition p. `edge_src`: rows below 256 are the partition's own nodes, the next 64 rows come from the partition below, the last 64 from the partition above; the first partition names no row of the middle range, the last partition none of the upper range. `edge_live`: live edges come first in each partition's block; at least one partition is full and at least one is half full.
All inputs are finite; a program needn't handle non-finite values.
Results may differ from the reference program's by a relative error of at most 0.007.
Values may be sent and summed in bfloat16 or wider, within the bound.
A program may use at most 128 MiB of HBM per device.

```python
import math
import jax
import jax.numpy as jnp
from jax import lax

L = 512
H = 1536
BLOCK = 128
EDGES_DEV = 1024
NODES_DEV = 256
SEND = 64
PARTITIONS = 64
EDGES = 65536
NODES = 16384


def draw_send_rows(key, part):
    scores = jax.random.randint(key, (PARTITIONS, NODES_DEV), 0, 1 << 20) * NODES_DEV + lax.iota(jnp.int32, NODES_DEV)[None, :]
    order = jnp.argsort(scores, axis=1, stable=True).astype(jnp.int32)
    return order[:, :2 * SEND].reshape(PARTITIONS, 2, SEND)


def draw_edge_src(key, part):
    table_rows = NODES_DEV + 2 * SEND
    picks = jax.random.randint(key, (PARTITIONS, EDGES_DEV), 0, table_rows)
    position = lax.iota(jnp.int32, PARTITIONS)[:, None]
    in_lower = (picks >= NODES_DEV) & (picks < NODES_DEV + SEND)
    in_upper = picks >= NODES_DEV + SEND
    picks = jnp.where((position == 0) & in_lower, picks - NODES_DEV, picks)
    picks = jnp.where((position == PARTITIONS - 1) & in_upper, picks - NODES_DEV - SEND, picks)
    return picks.reshape(PARTITIONS * EDGES_DEV).astype(jnp.int32)


def draw_edge_live(key, part):
    key_counts, key_full, key_offset = jax.random.split(key, 3)
    counts = jax.random.randint(key_counts, (PARTITIONS,), EDGES_DEV // 2, EDGES_DEV + 1)
    fullest = jax.random.randint(key_full, (), 0, PARTITIONS)
    offset = jax.random.randint(key_offset, (), 1, max(PARTITIONS, 2))
    emptiest = (fullest + offset) % PARTITIONS
    position = lax.iota(jnp.int32, PARTITIONS)
    counts = jnp.where(position == emptiest, EDGES_DEV // 2, counts)
    counts = jnp.where(position == fullest, EDGES_DEV, counts)
    return counts.astype(jnp.int32)


def with_ends(array, key, least, largest):
    shape = array.shape
    place = [jax.random.randint(jax.random.fold_in(key, axis), (), 0, shape[axis]) for axis in range(len(shape))]
    array = array.at[tuple(place)].set(least)
    longest = shape.index(max(shape))
    place[longest] = (place[longest] + 1) % shape[longest]
    return array.at[tuple(place)].set(largest)


def level_of(stream_key, shape, cuts, least, high):
    factor_of = 1.0
    for axis_at, shards_of in cuts:
        steps = jax.random.uniform(jax.random.fold_in(jax.random.fold_in(stream_key, 6), axis_at), (shards_of,), jnp.float32, least / len(cuts), high / len(cuts))
        factor_of = factor_of * jnp.repeat(jnp.exp(steps), shape[axis_at] // shards_of).reshape((-1,) + (1,) * (len(shape) - 1 - axis_at))
    return factor_of


def bell_draw(stream_key, dims, width, most, cuts=(), held_as=jnp.bfloat16):
    drawn = jax.random.normal(stream_key, dims, jnp.float32) * width
    if len(cuts) > 0:
        drawn = level_of(stream_key, dims, cuts, -0.22, 0.18) * drawn
    return jnp.clip(drawn, min=-most, max=most).astype(held_as)


def setup_inputs(seed: int = 0) -> dict:
    arg_keys = jax.random.split(jax.random.key(seed), 16)
    return {
        "node_latent": bell_draw(arg_keys[0], (NODES, L), 1.0, 6.0, ((0, 64),)),
        "edge_latent": bell_draw(arg_keys[1], (EDGES, L), 1.0, 6.0, ((0, 64),)),
        "send_rows": draw_send_rows(jax.random.fold_in(arg_keys[15], 71), 0),
        "edge_src": draw_edge_src(jax.random.fold_in(arg_keys[15], 71), 0),
        "edge_dst": with_ends(jax.random.randint(arg_keys[4], (EDGES,), 0, NODES_DEV), jax.random.fold_in(arg_keys[4], 1), 0, NODES_DEV - 1).astype(jnp.int32),
        "edge_live": draw_edge_live(jax.random.fold_in(arg_keys[15], 71), 0),
        "w_in_blocks": bell_draw(arg_keys[6], (3 * L, H), (3 * L) ** -0.5, 0.15625, ((1, 2),)),
        "w_in_scale": jnp.clip(jnp.exp(math.log(4.0) - 2.7725887 * jax.random.uniform(arg_keys[7], (3 * L // BLOCK, H // BLOCK), jnp.float32) ** level_of(arg_keys[7], (3 * L // BLOCK, H // BLOCK), ((1, 2),), -0.2, 0.2)), 0.25, 4.0),
        "bias_in": bell_draw(arg_keys[8], (H,), 1.0, 4.0, ((0, 2),), jnp.float32),
        "w_out_blocks": bell_draw(arg_keys[9], (H, L), H ** -0.5, 0.15625, ((0, 2),)),
        "w_out_scale": jnp.clip(jnp.exp(math.log(4.0) - 2.7725887 * jax.random.uniform(arg_keys[10], (H // BLOCK, L // BLOCK), jnp.float32) ** level_of(arg_keys[10], (H // BLOCK, L // BLOCK), ((0, 2),), -0.2, 0.2)), 0.25, 4.0),
        "bias_out": bell_draw(arg_keys[11], (L,), 1.0, 4.0, (), jnp.float32),
        "norm_gain": jnp.clip(1.0 + 0.18 * jax.random.normal(arg_keys[12], (L,), jnp.float32), 0.1, 1.9),
        "grad_edge": bell_draw(arg_keys[13], (EDGES, L), 1.0, 6.0, ((0, 64),)),
        "grad_agg": bell_draw(arg_keys[14], (NODES, L), 1.0, 6.0, ((0, 64),)),
    }


EPS = 1e-05

def dequantize(blocks, scales):
    row_repeat = blocks.shape[0] // scales.shape[0]
    col_repeat = blocks.shape[1] // scales.shape[1]
    spread = jnp.repeat(jnp.repeat(scales, row_repeat, axis=0), col_repeat, axis=1)
    return (blocks.astype(jnp.float32) * spread).astype(jnp.bfloat16)

def norm_backward(message, gain, upstream):
    centre = message - lax.optimization_barrier(jnp.mean(message, axis=1, keepdims=True))
    inverse = lax.rsqrt(lax.optimization_barrier(jnp.mean(centre * centre, axis=1, keepdims=True)) + EPS)
    normed = centre * inverse
    scaled = upstream * gain
    grad_message = inverse * (scaled - lax.optimization_barrier(jnp.mean(scaled, axis=1, keepdims=True)) - normed * lax.optimization_barrier(jnp.mean(scaled * normed, axis=1, keepdims=True)))
    return (normed, grad_message)

def silu_slope(pre_act):
    sigma = jax.nn.sigmoid(pre_act)
    return sigma * (1.0 + pre_act * (1.0 - sigma))

def take_rows(table, index):
    return jnp.take(table, index, axis=0)

def add_back(own_rows, up_index, down_index, got_up, got_down):
    return own_rows.at[up_index].add(got_up).at[down_index].add(got_down)

def reference(node_latent, edge_latent, send_rows, edge_src, edge_dst, edge_live, w_in_blocks, w_in_scale, bias_in, w_out_blocks, w_out_scale, bias_out, norm_gain, grad_edge, grad_agg):
    latent_width = node_latent.shape[1]
    table_rows = NODES_DEV + 2 * SEND
    nodes_grid = node_latent.reshape(PARTITIONS, NODES_DEV, latent_width)
    sent_down = jax.vmap(take_rows)(nodes_grid, send_rows[:, 0])
    sent_up = jax.vmap(take_rows)(nodes_grid, send_rows[:, 1])
    blank = jnp.zeros((1, SEND, latent_width), jnp.bfloat16)
    lower_rows = jnp.concatenate([blank, sent_up[:-1]], axis=0)
    upper_rows = jnp.concatenate([sent_down[1:], blank], axis=0)
    extended = jnp.concatenate([nodes_grid, lower_rows, upper_rows], axis=1)
    w_first = dequantize(w_in_blocks, w_in_scale)
    w_second = dequantize(w_out_blocks, w_out_scale)

    def partition(carry, pieces):
        table, own_edges, sources, targets, live_count, edge_cot, node_cot = pieces
        inputs = jnp.concatenate([own_edges, jnp.take(table, sources, axis=0), jnp.take(table, targets, axis=0)], axis=1)
        pre_act = jnp.dot(inputs, w_first, preferred_element_type=jnp.float32) + bias_in
        activated = jax.nn.silu(pre_act).astype(jnp.bfloat16)
        message = jnp.dot(activated, w_second, preferred_element_type=jnp.float32) + bias_out
        live_mask = (lax.iota(jnp.int32, EDGES_DEV) < live_count).astype(jnp.float32)[:, None]
        upstream = (edge_cot.astype(jnp.float32) + jnp.take(node_cot, targets, axis=0).astype(jnp.float32)) * live_mask
        normed, grad_message = norm_backward(message, norm_gain, upstream)
        vectors = jnp.stack([lax.optimization_barrier(jnp.sum(grad_message, axis=0)), lax.optimization_barrier(jnp.sum(upstream * normed, axis=0)), lax.optimization_barrier(jnp.sum(upstream, axis=0))])
        grad_message_low = grad_message.astype(jnp.bfloat16)
        grad_w_second = jnp.dot(activated.T, grad_message_low, preferred_element_type=jnp.float32)
        grad_act = jnp.dot(grad_message_low, w_second.T, preferred_element_type=jnp.float32)
        grad_pre = grad_act * silu_slope(pre_act)
        grad_pre_low = grad_pre.astype(jnp.bfloat16)
        grad_w_first = jnp.dot(inputs.T, grad_pre_low, preferred_element_type=jnp.float32)
        grad_inputs = jnp.dot(grad_pre_low, w_first.T, preferred_element_type=jnp.float32)
        grad_edge_in = (upstream + grad_inputs[:, :latent_width]).astype(jnp.bfloat16)
        node_data = jnp.concatenate([grad_inputs[:, latent_width:2 * latent_width], grad_inputs[:, 2 * latent_width:]], axis=0)
        node_ids = jnp.concatenate([sources, targets], axis=0)
        table_grad = jax.ops.segment_sum(node_data, node_ids, num_segments=table_rows)
        carry = (carry[0] + grad_w_first, carry[1] + lax.optimization_barrier(jnp.sum(grad_pre, axis=0)), carry[2] + grad_w_second, carry[3] + vectors)
        return (carry, (grad_edge_in, table_grad))
    start = (jnp.zeros(w_first.shape, jnp.float32), jnp.zeros((w_first.shape[1],), jnp.float32), jnp.zeros(w_second.shape, jnp.float32), jnp.zeros((3, latent_width), jnp.float32))
    pieces = (extended, edge_latent.reshape(PARTITIONS, EDGES_DEV, latent_width), edge_src.reshape(PARTITIONS, EDGES_DEV), edge_dst.reshape(PARTITIONS, EDGES_DEV), edge_live, grad_edge.reshape(PARTITIONS, EDGES_DEV, latent_width), grad_agg.reshape(PARTITIONS, NODES_DEV, latent_width))
    totals, (edge_grads, table_grad) = lax.scan(partition, start, pieces)
    factor = 1.0 / EDGES_DEV
    ghost_low = table_grad[:, NODES_DEV:NODES_DEV + SEND]
    ghost_high = table_grad[:, NODES_DEV + SEND:]
    zero_rows = jnp.zeros((1, SEND, latent_width), jnp.float32)
    from_upper = jnp.concatenate([ghost_low[1:], zero_rows], axis=0)
    from_lower = jnp.concatenate([zero_rows, ghost_high[:-1]], axis=0)
    grad_node = jax.vmap(add_back)(table_grad[:, :NODES_DEV], send_rows[:, 1], send_rows[:, 0], from_upper, from_lower)
    return (edge_grads.reshape(EDGES, latent_width), grad_node.astype(jnp.bfloat16).reshape(NODES, latent_width), totals[0] * factor, totals[1] * factor, totals[2] * factor, totals[3] * factor)
```

```python
import jax
import jax.numpy as jnp
from jax import lax
from jax.experimental import pallas as pl
from jax.experimental.pallas import tpu as pltpu
from jax.sharding import PartitionSpec as P

EPS = 1e-05
MESH = pl.DeviceIdType.MESH
F32 = jnp.float32
BF16 = jnp.bfloat16
CHUNKS = 6
LIMIT = 60 << 20


class Place:
    def __init__(self):
        dom = lax.axis_index("dom")
        self.hid = lax.axis_index("hid")
        self.dom = dom
        self.z = lax.div(dom, 16)
        self.x = lax.rem(lax.div(dom, 4), 4)
        self.yl = lax.rem(lax.div(dom, 2), 2)
        self.y = 2 * self.hid + self.yl
        self.core = lax.rem(dom, 2)

    def at(self, z=None, x=None, y=None, core=None):
        z = self.z if z is None else z
        x = self.x if x is None else x
        y = self.y if y is None else y
        core = self.core if core is None else core
        return (((z * 4 + x) * 2 + lax.rem(y, 2)) * 2 + core, lax.div(y, 2))

    def ring(self, axis, step):
        return self.at(**{axis: lax.rem(getattr(self, axis) + step, 4)})

    def other_core(self):
        return self.at(core=1 - self.core)

    def cross(self):
        return self.at(y=3 - self.y)

    def pair(self):
        return self.at(y=self.y + 1 - 2 * self.yl)

    def partition(self, step):
        return (lax.rem(self.dom + step, 64), self.hid)


def ready(partners):
    barrier = pltpu.get_barrier_semaphore()
    for partner in partners:
        pl.semaphore_signal(barrier, inc=1, device_id=partner, device_id_type=MESH)
    pl.semaphore_wait(barrier, len(partners))


def remote(src, dst, send_sem, recv_sem, target):
    return pltpu.make_async_remote_copy(
        src_ref=src,
        dst_ref=dst,
        send_sem=send_sem,
        recv_sem=recv_sem,
        device_id=target,
        device_id_type=MESH,
    )


def kind(chunk):
    return chunk % 3


def own_tile(place, chunk, yl=None):
    yl = place.yl if yl is None else yl
    if kind(chunk) == 0:
        return (place.z * 4 + place.x) * 2 + yl
    if kind(chunk) == 1:
        return (place.x * 2 + yl) * 4 + place.z
    return (yl * 4 + place.z) * 4 + place.x


def rows_of(first, count, unit=16):
    return pl.ds(pl.multiple_of(first * unit, unit), count * unit)


def gather_steps(place, chunk):
    z, x, yl = place.z, place.x, place.yl
    z_ring = [place.ring("z", j) for j in (1, 2, 3)]
    x_ring = [place.ring("x", j) for j in (1, 2, 3)]
    pair = [place.pair()]
    if kind(chunk) == 0:
        return [
            ((z * 4 + x) * 2 + yl, 1, pair),
            ((z * 4 + x) * 2, 2, x_ring),
            (z * 8, 8, z_ring),
        ]
    if kind(chunk) == 1:
        return [
            ((x * 2 + yl) * 4 + z, 1, z_ring),
            ((x * 2 + yl) * 4, 4, pair),
            (x * 8, 8, x_ring),
        ]
    return [
        ((yl * 4 + z) * 4 + x, 1, x_ring),
        ((yl * 4 + z) * 4, 4, z_ring),
        (yl * 16, 16, pair),
    ]


class Gather:
    def __init__(self, place, buf, send_sem, recv_sem):
        self.place, self.buf = place, buf
        self.send_sem, self.recv_sem = send_sem, recv_sem
        self.steps = {}
        self.flying = {}

    def start(self, chunk, step):
        place = self.place
        if chunk not in self.steps:
            self.steps[chunk] = gather_steps(place, chunk)
        block = 2 * chunk + place.core
        if step == 3:
            first, count, targets = 0, 32, [place.other_core()]
            base = 7
        else:
            first, count, targets = self.steps[chunk][step]
            base = sum(len(s[2]) for s in self.steps[chunk][:step])
        part = self.buf.at[block, rows_of(first, count)]
        copies = []
        for j, target in enumerate(targets):
            copy = remote(
                part, part, self.send_sem.at[chunk, base + j], self.recv_sem.at[chunk, base + j], target
            )
            copy.start()
            copies.append(copy)
        self.flying[chunk, step] = copies

    def arrived(self, chunk, step):
        for copy in self.flying[chunk, step]:
            copy.wait_recv()

    def sent(self):
        for copies in self.flying.values():
            for copy in copies:
                copy.wait_send()


RING = (1, 2, 3)
REDUCE_AXES = {0: ("z", "x", "y"), 1: ("x", "y", "z"), 2: ("y", "z", "x")}


def dequantize(own, w_in_ref, w_in_scale, w_out_ref, w_out_scale):
    def block(index, _):
        j = lax.div(index, 3)
        r = lax.rem(index, 3)
        for a in range(4):
            for b in range(2):
                scale = w_in_scale[4 * r + a, 2 * j + b]
                rows = pl.ds(pl.multiple_of(512 * r + 128 * a, 128), 128)
                cols = pl.ds(pl.multiple_of(256 * j + 128 * b, 128), 128)
                value = w_in_ref[rows, cols].astype(F32) * scale
                own[3 + index, 128 * a : 128 * a + 128, 128 * b : 128 * b + 128] = value.astype(BF16)
        return 0

    for a in range(6):
        for b in range(4):
            scale = w_out_scale[a, b]
            value = w_out_ref[128 * a : 128 * a + 128, 128 * b : 128 * b + 128].astype(F32) * scale
            if a < 4:
                index, row = b // 2, 128 * a
            else:
                index, row = 2, 128 * (a - 4) + 256 * (b // 2)
            col = 128 * (b % 2)
            own[index, row : row + 128, col : col + 128] = value.astype(BF16)
    lax.fori_loop(0, 9, block, 0)


def weights_kernel(
    w_in_ref,
    w_in_scale,
    w_out_ref,
    w_out_scale,
    bias_ref,
    node_ref,
    send_ref,
    weights,
    bias,
    halo,
    halo_out,
    gather_send,
    gather_recv,
    cross_send,
    cross_recv,
    halo_send,
    halo_recv,
):
    place = Place()
    partners = [place.ring("z", j) for j in RING] + [place.ring("x", j) for j in RING]
    partners += [place.pair(), place.other_core(), place.cross()]
    partners += [place.partition(1), place.partition(63)]
    ready(partners)
    own, other = weights.at[0], weights.at[1]
    dequantize(own, w_in_ref, w_in_scale, w_out_ref, w_out_scale)
    bias[0] = jnp.zeros((8, 256), F32)
    bias[0, 0:3, :] = bias_ref[...]
    copies = []
    crossing = {}
    copy = remote(bias.at[0], bias.at[1], cross_send.at[6], cross_recv.at[6], place.cross())
    copy.start()
    bias_copy = copy
    for chunk in (2, 3, 4, 5, 0, 1):
        block = 2 * chunk + place.core
        if chunk < 2:
            rows = slice(None)
        else:
            rows = rows_of(own_tile(place, chunk, 1 - place.yl), 1)
        copy = remote(
            own.at[block, rows],
            other.at[block, rows],
            cross_send.at[chunk],
            cross_recv.at[chunk],
            place.cross(),
        )
        copy.start()
        crossing[chunk] = copy
    for side in (0, 1):
        picks = (lax.broadcasted_iota(jnp.int32, (256, 64), 0) == send_ref[side : side + 1, :]).astype(F32)
        halo_out[side] = lax.dot_general(
            picks.astype(BF16), node_ref[...], (((0,), (0,)), ((), ())), preferred_element_type=F32
        ).astype(BF16)
    up = remote(halo_out.at[1], halo.at[0], halo_send.at[0], halo_recv.at[0], place.partition(1))
    down = remote(halo_out.at[0], halo.at[1], halo_send.at[1], halo_recv.at[1], place.partition(63))
    up.start()
    down.start()
    gather = Gather(place, other, gather_send, gather_recv)
    for step in range(4):
        for chunk in (2, 3, 4, 5):
            if step == 0:
                crossing[chunk].wait_recv()
            else:
                gather.arrived(chunk, step - 1)
            gather.start(chunk, step)
    for chunk in (0, 1):
        crossing[chunk].wait_recv()
        gather.start(chunk, 3)
    for chunk in range(CHUNKS):
        gather.arrived(chunk, 3)
    bias_copy.wait_recv()
    up.wait_recv()
    down.wait_recv()
    gather.sent()
    for copy in list(crossing.values()) + [bias_copy, up, down]:
        copy.wait_send()


def place_rows(grads, block, first, value, half):
    count = value.shape[0]
    group = {0: 32, 1: 128, 2: 512}[kind(block // 2)]
    for at in range(0, count, min(group, count)):
        row = first + at
        base = (row // group) * 2 * group + row % group
        size = min(group, count)
        grads[block, pl.ds(pl.multiple_of(base + group * half, 32), size), :] = value[at : at + size]


def compute_kernel(
    edge_ref,
    gedge_ref,
    node_ref,
    gagg_ref,
    halo,
    src_ref,
    dst_ref,
    live_ref,
    weights,
    bias,
    bias_out_ref,
    gain_ref,
    grad_edge_ref,
    grads,
    own_table,
    halo_table,
    sums,
    inp,
    inpt,
    ext,
    pick_src,
    pick_dst,
    act,
    slope,
    up,
    msg,
    low,
    pre_low,
    gedge,
    sem,
):
    hid = lax.axis_index("hid")
    dom = lax.axis_index("dom")
    first_edge = pl.multiple_of(hid * 512, 512)
    get_edge = pltpu.make_async_copy(edge_ref.at[pl.ds(first_edge, 512)], inp.at[0], sem.at[0])
    get_cot = pltpu.make_async_copy(gedge_ref.at[pl.ds(first_edge, 512)], gedge, sem.at[1])
    get_edge.start()
    get_cot.start()
    ext[0:256] = node_ref[...]
    ext[256:320] = jnp.where(dom > 0, halo[0], jnp.zeros((64, 512), BF16))
    ext[320:384] = jnp.where(dom < 63, halo[1], jnp.zeros((64, 512), BF16))
    for k in range(4):
        cols = slice(128 * k, 128 * k + 128)
        src_row = src_ref[pl.ds(4 * hid + k, 1), :]
        dst_row = dst_ref[pl.ds(4 * hid + k, 1), :]
        pick_src[:, cols] = (lax.broadcasted_iota(jnp.int32, (384, 128), 0) == src_row).astype(F32).astype(BF16)
        pick_dst[:, cols] = (lax.broadcasted_iota(jnp.int32, (256, 128), 0) == dst_row).astype(F32).astype(BF16)

    def tdot(a, b):
        return lax.dot_general(a, b, (((0,), (0,)), ((), ())), preferred_element_type=F32)

    def ndot(a, b):
        return lax.dot_general(a, b, (((1,), (1,)), ((), ())), preferred_element_type=F32)

    def dot(a, b):
        return jnp.dot(a, b, preferred_element_type=F32)

    inp[1] = tdot(pick_src[...], ext[...]).astype(BF16)
    inp[2] = tdot(pick_dst[...], node_ref[...]).astype(BF16)
    up[...] = tdot(pick_dst[...], gagg_ref[...])
    get_edge.wait()
    get_cot.wait()
    for r in range(3):
        inpt[r] = inp[r].T

    for slot in range(2):

        def forward(j, _):
            pre = bias[slot, pl.ds(j, 1), :]
            for r in range(3):
                pre = pre + dot(inp[r], weights[slot, 3 + 3 * j + r])
            sigma = 1.0 / (1.0 + jnp.exp(-pre))
            value = pre * sigma
            act[3 * slot + j] = value.astype(BF16)
            slope[3 * slot + j] = sigma + value * (1.0 - sigma)
            return 0

        lax.fori_loop(0, 3, forward, 0)

    for side in range(2):
        total = bias_out_ref[:, 256 * side : 256 * side + 256]
        for slot in range(2):
            for j in range(2):
                total = total + dot(act[3 * slot + j], weights[slot, side, 256 * j : 256 * j + 256, :])
            total = total + dot(act[3 * slot + 2], weights[slot, 2, 256 * side : 256 * side + 256, :])
        msg[:, 256 * side : 256 * side + 256] = total

    live = live_ref[0] - hid * 512
    gain = gain_ref[...]

    def norm(i, carry):
        rows = pl.ds(pl.multiple_of(i * 64, 64), 64)
        mask = (lax.broadcasted_iota(jnp.int32, (64, 512), 0) + i * 64) < live
        upstream = jnp.where(mask, gedge[rows, :].astype(F32) + up[rows, :], 0.0)
        up[rows, :] = upstream
        message = msg[rows, :]
        centre = message - jnp.mean(message, axis=1, keepdims=True)
        inverse = lax.rsqrt(jnp.mean(centre * centre, axis=1, keepdims=True) + EPS)
        normed = centre * inverse
        scaled = upstream * gain
        shift = jnp.mean(scaled, axis=1, keepdims=True)
        tilt = jnp.mean(scaled * normed, axis=1, keepdims=True)
        grad = inverse * (scaled - shift - normed * tilt)
        low[rows, :] = grad.astype(BF16)

        def fold(value):
            return jnp.sum(value.reshape(8, 8, 512), axis=0)

        return (carry[0] + fold(grad), carry[1] + fold(upstream * normed), carry[2] + fold(upstream))

    zero = jnp.zeros((8, 512), F32)
    vectors = lax.fori_loop(0, 8, norm, (zero, zero, zero))
    sums[...] = jnp.zeros((16, 256), F32)
    for i in range(3):
        row = jnp.sum(vectors[i], axis=0, keepdims=True)
        sums[6 + 2 * i : 7 + 2 * i, :] = row[:, 0:256]
        sums[7 + 2 * i : 8 + 2 * i, :] = row[:, 256:512]

    for slot in range(2):
        half = hid if slot == 0 else 1 - hid

        for j in range(3):
            if j < 2:
                rows = slice(256 * j, 256 * j + 256)
                grad = ndot(low[:, 0:256], weights[slot, 0, rows, :]) + ndot(
                    low[:, 256:512], weights[slot, 1, rows, :]
                )
            else:
                grad = ndot(low[:, 0:256], weights[slot, 2, 0:256, :]) + ndot(
                    low[:, 256:512], weights[slot, 2, 256:512, :]
                )
            grad = grad * slope[3 * slot + j]
            sums[pl.ds(3 * half + j, 1), :] = jnp.sum(grad, axis=0, keepdims=True)
            pre_low[3 * slot + j] = grad.astype(BF16)

        for j in range(3):
            part = tdot(act[3 * slot + j], low[...]).astype(BF16)
            if j < 2:
                place_rows(grads, 0, 256 * j, part[:, 0:256], half)
                place_rows(grads, 1, 256 * j, part[:, 256:512], half)
            else:
                place_rows(grads, 2, 0, part[:, 0:256], half)
                place_rows(grads, 2, 256, part[:, 256:512], half)

    for m in range(9):
        for slot in range(2):
            half = hid if slot == 0 else 1 - hid
            part = dot(inpt[m % 3], pre_low[3 * slot + m // 3]).astype(BF16)
            place_rows(grads, 3 + m, 0, part, half)

    for r in range(3):
        total = jnp.zeros((512, 512), F32)
        for slot in range(2):
            for j in range(3):
                total = total + ndot(pre_low[3 * slot + j], weights[slot, 3 + 3 * j + r])
        if r == 0:
            grad_edge_ref[...] = (total + up[...]).astype(BF16)
        elif r == 1:
            table = dot(pick_src[...], total.astype(BF16))
            own_table[...] = table[0:256]
            halo_table[...] = table[256:384].astype(BF16)
        else:
            own_table[...] += dot(pick_dst[...], total.astype(BF16))


def reduce_kernel(
    grads,
    sums,
    own_table,
    halo_table,
    send_ref,
    total,
    grad_node,
    summed,
    core_in,
    stage,
    first_in,
    first_out,
    second_in,
    second_out,
    third_in,
    sum_core,
    sum_ring,
    halo_in,
    node_out,
    node_in,
    reduce_send,
    reduce_recv,
    gather_send,
    gather_recv,
    sum_send,
    sum_recv,
    node_send,
    node_recv,
):
    place = Place()
    core = place.core
    partners = [place.ring(axis, j) for axis in "zxy" for j in RING]
    partners += [place.other_core(), place.partition(1), place.partition(63)]
    ready(partners)
    flying = []

    def go(src, dst, send_sem, recv_sem, target):
        copy = remote(src, dst, send_sem, recv_sem, target)
        copy.start()
        flying.append(copy)
        return copy

    up = go(halo_table.at[64:128], halo_in.at[0], node_send.at[0], node_recv.at[0], place.partition(1))
    down = go(halo_table.at[0:64], halo_in.at[1], node_send.at[1], node_recv.at[1], place.partition(63))
    sum_copy = go(sums, sum_core.at[0], sum_send.at[0, 0], sum_recv.at[0, 0], place.other_core())
    between = {}
    for chunk in range(CHUNKS):
        between[chunk] = go(
            grads.at[2 * chunk + 1 - core],
            core_in.at[chunk],
            reduce_send.at[chunk, 0],
            reduce_recv.at[chunk, 0],
            place.other_core(),
        )

    def spread(chunk, level, src, dst, unit):
        axis = REDUCE_AXES[kind(chunk)][level]
        mine = getattr(place, axis)
        copies = []
        for j in RING:
            at = lax.rem(mine + j, 4)
            sem = 1 + 3 * level + j - 1
            copies.append(
                go(
                    src.at[rows_of(at, 1, unit)],
                    dst.at[j - 1],
                    reduce_send.at[chunk, sem],
                    reduce_recv.at[chunk, sem],
                    place.ring(axis, j),
                )
            )
        return copies

    def kept(chunk, level, src, unit):
        mine = getattr(place, REDUCE_AXES[kind(chunk)][level])
        return src[rows_of(mine, 1, unit), :].astype(F32)

    def add_core(chunk):
        between[chunk].wait_recv()

        def part(i, _):
            rows = pl.ds(pl.multiple_of(i * 128, 128), 128)
            mine = grads[2 * chunk + core, rows, :].astype(F32)
            stage[chunk, rows, :] = (mine + core_in[chunk, rows, :].astype(F32)).astype(BF16)
            return 0

        lax.fori_loop(0, 8, part, 0)

    def sums_ring(level, axis, value):
        mine = getattr(place, axis)
        sum_ring[level, mine] = value
        return [
            go(
                sum_ring.at[level, mine],
                sum_ring.at[level, mine],
                sum_send.at[1 + level, j],
                sum_recv.at[1 + level, j],
                place.ring(axis, j),
            )
            for j in RING
        ]

    waiting = {}
    for chunk in range(CHUNKS):
        add_core(chunk)
        waiting[chunk] = spread(chunk, 0, stage.at[chunk], first_in.at[chunk], 256)
    sum_copy.wait_recv()
    ring_copies = sums_ring(0, "z", sums[...] + sum_core[0])

    up.wait_recv()
    down.wait_recv()
    node = own_table[...]
    for side in (0, 1):
        picks = (lax.broadcasted_iota(jnp.int32, (256, 64), 0) == send_ref[side : side + 1, :]).astype(F32)
        got = halo_in[side]
        there = (place.dom < 63) if side == 1 else (place.dom > 0)
        picks = jnp.where(there, picks, 0.0).astype(BF16)
        node = node + jnp.dot(picks, got, preferred_element_type=F32)
    node_keep = jnp.where(place.hid == 0, node[:, 0:256], node[:, 256:512])
    node_out[...] = jnp.where(place.hid == 0, node[:, 256:512], node[:, 0:256]).astype(BF16)
    swap = go(node_out, node_in, node_send.at[2], node_recv.at[2], (place.dom, 1 - place.hid))

    for chunk in range(CHUNKS):
        for copy in waiting[chunk]:
            copy.wait_recv()
        value = kept(chunk, 0, stage.at[chunk], 256)
        for j in range(3):
            value = value + first_in[chunk, j].astype(F32)
        first_out[chunk] = value.astype(BF16)
        waiting[chunk] = spread(chunk, 1, first_out.at[chunk], second_in.at[chunk], 64)
    for copy in ring_copies:
        copy.wait_recv()
    ring_copies = sums_ring(1, "x", sum_ring[0, 0] + sum_ring[0, 1] + sum_ring[0, 2] + sum_ring[0, 3])
    for chunk in range(CHUNKS):
        for copy in waiting[chunk]:
            copy.wait_recv()
        value = kept(chunk, 1, first_out.at[chunk], 64)
        for j in range(3):
            value = value + second_in[chunk, j].astype(F32)
        second_out[chunk] = value.astype(BF16)
        waiting[chunk] = spread(chunk, 2, second_out.at[chunk], third_in.at[chunk], 16)
    for copy in ring_copies:
        copy.wait_recv()
    ring_copies = sums_ring(2, "y", sum_ring[1, 0] + sum_ring[1, 1] + sum_ring[1, 2] + sum_ring[1, 3])
    gather = Gather(place, total, gather_send, gather_recv)
    for chunk in range(CHUNKS):
        for copy in waiting[chunk]:
            copy.wait_recv()
        value = kept(chunk, 2, second_out.at[chunk], 16)
        for j in range(3):
            value = value + third_in[chunk, j].astype(F32)
        value = value * (1.0 / 1024)
        total[2 * chunk + core, rows_of(own_tile(place, chunk), 1), :] = value.astype(BF16)
        gather.start(chunk, 0)
    swap.wait_recv()
    grad_node[...] = (node_keep + node_in[...].astype(F32)).astype(BF16)
    for step in (1, 2, 3):
        for chunk in range(CHUNKS):
            gather.arrived(chunk, step - 1)
            gather.start(chunk, step)
    for copy in ring_copies:
        copy.wait_recv()
    summed[...] = (sum_ring[2, 0] + sum_ring[2, 1] + sum_ring[2, 2] + sum_ring[2, 3]) * (1.0 / 1024)
    for chunk in range(CHUNKS):
        gather.arrived(chunk, 3)
    gather.sent()
    for copy in flying:
        copy.wait_send()


def widen_kernel(total, w_out, w_in):
    step = pl.program_id(0)

    @pl.when(step == 0)
    def _():
        w_out[0:512, 0:256] = total[0].astype(F32)

    @pl.when(step == 1)
    def _():
        w_out[0:512, 256:512] = total[0].astype(F32)

    @pl.when(step == 2)
    def _():
        w_out[512:768, 0:256] = total[0, 0:256].astype(F32)
        w_out[512:768, 256:512] = total[0, 256:512].astype(F32)

    @pl.when(step >= 3)
    def _():
        w_in[...] = total[0].astype(F32)


def vmem():
    return pl.BlockSpec(memory_space=pltpu.VMEM)


def smem():
    return pl.BlockSpec(memory_space=pltpu.SMEM)


def anywhere():
    return pl.BlockSpec(memory_space=pl.ANY)


def shape(dims, dtype):
    return jax.ShapeDtypeStruct(dims, dtype)


def dma(*dims):
    return pltpu.SemaphoreType.DMA(dims)


def per_device(
    node_latent,
    edge_latent,
    send_rows,
    edge_src,
    edge_dst,
    edge_live,
    w_in_blocks,
    w_in_scale,
    bias_in,
    w_out_blocks,
    w_out_scale,
    bias_out,
    norm_gain,
    grad_edge,
    grad_agg,
):
    lists = send_rows[0]
    weights, bias, halo = pl.pallas_call(
        weights_kernel,
        out_shape=(
            shape((2, 12, 512, 256), BF16),
            shape((2, 8, 256), F32),
            shape((2, 64, 512), BF16),
        ),
        in_specs=[vmem(), smem(), vmem(), smem(), vmem(), vmem(), vmem()],
        out_specs=(vmem(), vmem(), vmem()),
        scratch_shapes=[
            pltpu.VMEM((2, 64, 512), BF16),
            dma(6, 8),
            dma(6, 8),
            dma(7),
            dma(7),
            dma(2),
            dma(2),
        ],
        compiler_params=pltpu.CompilerParams(
            collective_id=0, has_side_effects=True, vmem_limit_bytes=LIMIT
        ),
        name="spread_weights",
    )(w_in_blocks, w_in_scale, w_out_blocks, w_out_scale, bias_in.reshape(3, 256), node_latent, lists)
    grad_edge_in, grads, own_table, halo_table, sums = pl.pallas_call(
        compute_kernel,
        out_shape=(
            shape((512, 512), BF16),
            shape((12, 1024, 256), BF16),
            shape((256, 512), F32),
            shape((128, 512), BF16),
            shape((16, 256), F32),
        ),
        in_specs=[
            anywhere(),
            anywhere(),
            vmem(),
            vmem(),
            vmem(),
            vmem(),
            vmem(),
            smem(),
            vmem(),
            vmem(),
            vmem(),
            vmem(),
        ],
        out_specs=(vmem(),) * 5,
        scratch_shapes=[
            pltpu.VMEM((3, 512, 512), BF16),
            pltpu.VMEM((3, 512, 512), BF16),
            pltpu.VMEM((384, 512), BF16),
            pltpu.VMEM((384, 512), BF16),
            pltpu.VMEM((256, 512), BF16),
            pltpu.VMEM((6, 512, 256), BF16),
            pltpu.VMEM((6, 512, 256), F32),
            pltpu.VMEM((512, 512), F32),
            pltpu.VMEM((512, 512), F32),
            pltpu.VMEM((512, 512), BF16),
            pltpu.VMEM((6, 512, 256), BF16),
            pltpu.VMEM((512, 512), BF16),
            dma(2),
        ],
        compiler_params=pltpu.CompilerParams(vmem_limit_bytes=LIMIT),
        name="local_grads",
    )(
        edge_latent,
        grad_edge,
        node_latent,
        grad_agg,
        halo,
        edge_src.reshape(8, 128),
        edge_dst.reshape(8, 128),
        edge_live,
        weights,
        bias,
        bias_out.reshape(1, 512),
        norm_gain.reshape(1, 512),
    )
    total, grad_node, summed = pl.pallas_call(
        reduce_kernel,
        out_shape=(
            shape((12, 512, 256), BF16),
            shape((256, 256), BF16),
            shape((16, 256), F32),
        ),
        in_specs=[vmem()] * 5,
        out_specs=(vmem(),) * 3,
        scratch_shapes=[
            pltpu.VMEM((6, 1024, 256), BF16),
            pltpu.VMEM((6, 1024, 256), BF16),
            pltpu.VMEM((6, 3, 256, 256), BF16),
            pltpu.VMEM((6, 256, 256), BF16),
            pltpu.VMEM((6, 3, 64, 256), BF16),
            pltpu.VMEM((6, 64, 256), BF16),
            pltpu.VMEM((6, 3, 16, 256), BF16),
            pltpu.VMEM((1, 16, 256), F32),
            pltpu.VMEM((3, 4, 16, 256), F32),
            pltpu.VMEM((2, 64, 512), BF16),
            pltpu.VMEM((256, 256), BF16),
            pltpu.VMEM((256, 256), BF16),
            dma(6, 10),
            dma(6, 10),
            dma(6, 8),
            dma(6, 8),
            dma(4, 4),
            dma(4, 4),
            dma(3),
            dma(3),
        ],
        compiler_params=pltpu.CompilerParams(
            collective_id=1, has_side_effects=True, vmem_limit_bytes=LIMIT
        ),
        name="reduce_grads",
    )(grads, sums, own_table, halo_table, lists)
    grad_w_out, grad_w_in = pl.pallas_call(
        widen_kernel,
        grid=(12,),
        out_shape=(shape((768, 512), F32), shape((1536, 768), F32)),
        in_specs=[pl.BlockSpec((1, 512, 256), lambda i: (i, 0, 0))],
        out_specs=(
            pl.BlockSpec((768, 512), lambda i: (0, 0)),
            pl.BlockSpec(
                (512, 256), lambda i: (jnp.maximum(i - 3, 0) % 3, jnp.maximum(i - 3, 0) // 3)
            ),
        ),
        name="widen_grads",
    )(total)
    hid = lax.axis_index("hid")
    grad_bias = jnp.where(hid == 0, summed[0:3], summed[3:6]).reshape(768)
    vectors = summed[6:12].reshape(3, 512)
    return (grad_edge_in, grad_node, grad_w_in, grad_bias, grad_w_out, vectors)


def solution(mesh):
    in_specs = (
        P("dom", None),
        P("dom", None),
        P("dom", None, None),
        P("dom"),
        P("dom"),
        P("dom"),
        P(None, "hid"),
        P(None, "hid"),
        P("hid"),
        P("hid", None),
        P("hid", None),
        P(),
        P(),
        P("dom", None),
        P("dom", None),
    )
    out_specs = (
        P(("dom", "hid"), None),
        P("dom", "hid"),
        P(None, "hid"),
        P("hid"),
        P("hid", None),
        P(),
    )
    return jax.shard_map(
        per_device, mesh=mesh, in_specs=in_specs, out_specs=out_specs, check_vma=False
    )
```

```python
import jax
import jax.numpy as jnp
from jax import lax
from jax.experimental import pallas as pl
from jax.experimental.pallas import tpu as pltpu
from jax.sharding import PartitionSpec as P

EPS = 1e-05
MESH = pl.DeviceIdType.MESH
F32 = jnp.float32
BF16 = jnp.bfloat16
CHUNKS = 6
LIMIT = 60 << 20


class Place:
    def __init__(self):
        dom = lax.axis_index("dom")
        self.hid = lax.axis_index("hid")
        self.dom = dom
        self.z = lax.div(dom, 16)
        self.x = lax.rem(lax.div(dom, 4), 4)
        self.yl = lax.rem(lax.div(dom, 2), 2)
        self.y = 2 * self.hid + self.yl
        self.core = lax.rem(dom, 2)

    def at(self, z=None, x=None, y=None, core=None):
        z = self.z if z is None else z
        x = self.x if x is None else x
        y = self.y if y is None else y
        core = self.core if core is None else core
        return (((z * 4 + x) * 2 + lax.rem(y, 2)) * 2 + core, lax.div(y, 2))

    def ring(self, axis, step):
        return self.at(**{axis: lax.rem(getattr(self, axis) + step, 4)})

    def other_core(self):
        return self.at(core=1 - self.core)

    def cross(self):
        return self.at(y=3 - self.y)

    def pair(self):
        return self.at(y=self.y + 1 - 2 * self.yl)

    def partition(self, step):
        return (lax.rem(self.dom + step, 64), self.hid)


def greet(partners):
    barrier = pltpu.get_barrier_semaphore()
    for partner in partners:
        pl.semaphore_signal(barrier, inc=1, device_id=partner, device_id_type=MESH)
    return lambda: pl.semaphore_wait(barrier, len(partners))


def remote(src, dst, send_sem, recv_sem, target):
    return pltpu.make_async_remote_copy(
        src_ref=src,
        dst_ref=dst,
        send_sem=send_sem,
        recv_sem=recv_sem,
        device_id=target,
        device_id_type=MESH,
    )


def kind(chunk):
    return chunk % 3


def own_tile(place, chunk, yl=None):
    yl = place.yl if yl is None else yl
    if kind(chunk) == 0:
        return (place.z * 4 + place.x) * 2 + yl
    if kind(chunk) == 1:
        return (place.x * 2 + yl) * 4 + place.z
    return (yl * 4 + place.z) * 4 + place.x


def rows_of(first, count, unit=16):
    return pl.ds(pl.multiple_of(first * unit, unit), count * unit)


def gather_steps(place, chunk):
    z, x, yl = place.z, place.x, place.yl
    z_ring = [place.ring("z", j) for j in (1, 2, 3)]
    x_ring = [place.ring("x", j) for j in (1, 2, 3)]
    pair = [place.pair()]
    if kind(chunk) == 0:
        return [
            ((z * 4 + x) * 2 + yl, 1, pair),
            ((z * 4 + x) * 2, 2, x_ring),
            (z * 8, 8, z_ring),
        ]
    if kind(chunk) == 1:
        return [
            ((x * 2 + yl) * 4 + z, 1, z_ring),
            ((x * 2 + yl) * 4, 4, pair),
            (x * 8, 8, x_ring),
        ]
    return [
        ((yl * 4 + z) * 4 + x, 1, x_ring),
        ((yl * 4 + z) * 4, 4, z_ring),
        (yl * 16, 16, pair),
    ]


class Gather:
    def __init__(self, place, buf, send_sem, recv_sem, result):
        self.place, self.buf, self.result = place, buf, result
        self.send_sem, self.recv_sem = send_sem, recv_sem
        self.steps = {}
        self.flying = {}

    def start(self, chunk, step):
        place = self.place
        if chunk not in self.steps:
            self.steps[chunk] = gather_steps(place, chunk)
        block = 2 * chunk + place.core
        if step == 3:
            first, count, targets = 0, 32, [place.other_core()]
            base = 7
        else:
            first, count, targets = self.steps[chunk][step]
            base = sum(len(s[2]) for s in self.steps[chunk][:step])
        part = self.buf.at[block, rows_of(first, count)]
        goal = self.result.at[block] if step == 3 else part
        copies = []
        for j, target in enumerate(targets):
            copy = remote(
                part, goal, self.send_sem.at[chunk, base + j], self.recv_sem.at[chunk, base + j], target
            )
            copy.start()
            copies.append(copy)
        self.flying[chunk, step] = copies

    def arrived(self, chunk, step):
        for copy in self.flying[chunk, step]:
            copy.wait_recv()

    def sent(self):
        for copies in self.flying.values():
            for copy in copies:
                copy.wait_send()


RING = (1, 2, 3)
REDUCE_AXES = {0: ("z", "x", "y"), 1: ("x", "y", "z"), 2: ("y", "z", "x")}


def tdot(a, b):
    return lax.dot_general(a, b, (((0,), (0,)), ((), ())), preferred_element_type=F32)


def ndot(a, b):
    return lax.dot_general(a, b, (((1,), (1,)), ((), ())), preferred_element_type=F32)


def dot(a, b):
    return jnp.dot(a, b, preferred_element_type=F32)


def dequantize_out(own, w_out_ref, scales):
    for a in range(6):
        for b in range(4):
            value = w_out_ref[128 * a : 128 * a + 128, 128 * b : 128 * b + 128].astype(F32) * scales[b, a]
            if a < 4:
                index, row = b // 2, 128 * a
            else:
                index, row = 2, 128 * (a - 4) + 256 * (b // 2)
            col = 128 * (b % 2)
            own[index, row : row + 128, col : col + 128] = value.astype(BF16)


def dequantize_in(own, w_in_ref, scales, first, last):
    def block(index, _):
        j = lax.div(index, 3)
        r = lax.rem(index, 3)
        for a in range(4):
            for b in range(2):
                scale = scales[2 * j + b, 4 * r + a]
                rows = pl.ds(pl.multiple_of(512 * r + 128 * a, 128), 128)
                cols = pl.ds(pl.multiple_of(256 * j + 128 * b, 128), 128)
                value = w_in_ref[rows, cols].astype(F32) * scale
                own[3 + index, 128 * a : 128 * a + 128, 128 * b : 128 * b + 128] = value.astype(BF16)
        return 0

    lax.fori_loop(first, last, block, 0)


def dequantize_tile(tile, w_in_ref, scales, index, q):
    j = lax.div(index, 3)
    r = lax.rem(index, 3)
    rows = pl.ds(pl.multiple_of(512 * r + 16 * q, 16), 16)
    for b in range(2):
        scale = scales[2 * j + b, 4 * r + lax.div(q, 8)]
        cols = pl.ds(pl.multiple_of(256 * j + 128 * b, 128), 128)
        tile[:, 128 * b : 128 * b + 128] = (w_in_ref[rows, cols].astype(F32) * scale).astype(BF16)


def place_rows(grads, block, first, value, half):
    count = value.shape[0]
    group = {0: 32, 1: 128, 2: 512}[kind(block // 2)]
    size = min(group, count)
    for at in range(0, count, size):
        row = first + at
        base = (row // group) * 2 * group + row % group
        grads[block, pl.ds(pl.multiple_of(base + group * half, 32), size), :] = value[at : at + size]


class Reduce:
    def __init__(self, place, grads, core_in, first_in, first_out, second_in, second_out, third_in, send_sem, recv_sem):
        self.place, self.grads, self.core_in = place, grads, core_in
        self.first_in, self.first_out = first_in, first_out
        self.second_in, self.second_out, self.third_in = second_in, second_out, third_in
        self.send_sem, self.recv_sem = send_sem, recv_sem
        self.flying = {}

    def send(self, chunk, stage, index, src, dst, target):
        copy = remote(src, dst, self.send_sem.at[chunk, index], self.recv_sem.at[chunk, index], target)
        copy.start()
        self.flying.setdefault((chunk, stage), []).append(copy)

    def arrived(self, chunk, stage):
        for copy in self.flying[chunk, stage]:
            copy.wait_recv()

    def sent(self):
        for copies in self.flying.values():
            for copy in copies:
                copy.wait_send()

    def share(self, chunk):
        core = self.place.core
        src = self.grads.at[2 * chunk + 1 - core]
        self.send(chunk, 0, 0, src, self.core_in.at[chunk], self.place.other_core())

    def spread(self, chunk, level, src, dst, unit):
        axis = REDUCE_AXES[kind(chunk)][level]
        mine = getattr(self.place, axis)
        for j in RING:
            at = lax.rem(mine + j, 4)
            part = src.at[rows_of(at, 1, unit)]
            self.send(chunk, level + 1, 3 * level + j, part, dst.at[j - 1], self.place.ring(axis, j))

    def kept(self, chunk, level, src, unit):
        mine = getattr(self.place, REDUCE_AXES[kind(chunk)][level])
        return src[rows_of(mine, 1, unit), :].astype(F32)

    def add_core(self, chunk):
        self.arrived(chunk, 0)
        block = 2 * chunk + self.place.core

        def part(i, _):
            rows = pl.ds(pl.multiple_of(i * 128, 128), 128)
            mine = self.grads[block, rows, :].astype(F32)
            self.grads[block, rows, :] = (mine + self.core_in[chunk, rows, :].astype(F32)).astype(BF16)
            return 0

        lax.fori_loop(0, 8, part, 0)
        self.spread(chunk, 0, self.grads.at[block], self.first_in.at[chunk], 256)

    def add_first(self, chunk):
        self.arrived(chunk, 1)
        value = self.kept(chunk, 0, self.grads.at[2 * chunk + self.place.core], 256)
        for j in range(3):
            value = value + self.first_in[chunk, j].astype(F32)
        self.first_out[chunk] = value.astype(BF16)
        self.spread(chunk, 1, self.first_out.at[chunk], self.second_in.at[chunk], 64)

    def add_second(self, chunk):
        self.arrived(chunk, 2)
        value = self.kept(chunk, 1, self.first_out.at[chunk], 64)
        for j in range(3):
            value = value + self.second_in[chunk, j].astype(F32)
        self.second_out[chunk] = value.astype(BF16)
        self.spread(chunk, 2, self.second_out.at[chunk], self.third_in.at[chunk], 16)

    def add_third(self, chunk):
        self.arrived(chunk, 3)
        value = self.kept(chunk, 2, self.second_out.at[chunk], 16)
        for j in range(3):
            value = value + self.third_in[chunk, j].astype(F32)
        return value


def main_kernel(
    node_hbm,
    edge_hbm,
    send_ref,
    src_ref,
    dst_ref,
    live_ref,
    w_in_hbm,
    w_in_scale,
    bias_ref,
    w_out_hbm,
    w_out_scale,
    bias_out_ref,
    gain_ref,
    gedge_hbm,
    gagg_hbm,
    total_hbm,
    grad_edge,
    grad_node,
    summed,
    node,
    w_in,
    w_out,
    gagg,
    gedge,
    weights,
    bias,
    halo,
    halo_out,
    tiles,
    inp,
    inpt,
    ext,
    pick_src,
    pick_dst,
    act,
    slope,
    up,
    msg,
    low,
    pre_low,
    grads,
    core_in,
    first_in,
    first_out,
    second_in,
    second_out,
    third_in,
    total,
    sums,
    sum_core,
    sum_ring,
    own_table,
    halo_table,
    halo_in,
    node_out,
    node_in,
    local_sem,
    spread_send,
    spread_recv,
    cross_send,
    cross_recv,
    halo_send,
    halo_recv,
    reduce_send,
    reduce_recv,
    gather_send,
    gather_recv,
    sum_send,
    sum_recv,
    node_send,
    node_recv,
    write_sem,
):
    place = Place()
    hid, dom, core = place.hid, place.dom, place.core
    first_edge = pl.multiple_of(hid * 512, 512)

    def fetch(index, src, dst):
        copy = pltpu.make_async_copy(src, dst, local_sem.at[index])
        copy.start()
        return copy

    get_w_in = fetch(1, w_in_hbm, w_in)
    get_w_out = fetch(0, w_out_hbm, w_out)
    get_node = fetch(2, node_hbm, node)
    get_edge = fetch(3, edge_hbm.at[pl.ds(first_edge, 512)], inp.at[0])
    get_agg = fetch(4, gagg_hbm, gagg)
    get_cot = fetch(5, gedge_hbm.at[pl.ds(first_edge, 512)], gedge)
    partners = [place.ring(axis, j) for axis in "zxy" for j in RING]
    partners += [place.other_core(), place.cross(), place.partition(1), place.partition(63)]
    all_here = greet(partners)
    flying = []

    def go(src, dst, send_sem, recv_sem, target):
        copy = remote(src, dst, send_sem, recv_sem, target)
        copy.start()
        flying.append(copy)
        return copy

    own, other = weights.at[0], weights.at[1]
    bias[0] = jnp.zeros((8, 256), F32)
    for j in range(3):
        bias[0, j : j + 1, 0:128] = bias_ref[2 * j : 2 * j + 1, :]
        bias[0, j : j + 1, 128:256] = bias_ref[2 * j + 1 : 2 * j + 2, :]
    get_w_in.wait()
    tile_at = {}
    for chunk in (2, 3, 4, 5):
        tile_at[chunk] = own_tile(place, chunk, 1 - place.yl)
        dequantize_tile(tiles.at[chunk - 2], w_in, w_in_scale, 2 * chunk + core - 3, tile_at[chunk])
    dequantize_in(own, w_in, w_in_scale, 0, 1)
    get_w_out.wait()
    dequantize_out(own, w_out, w_out_scale)
    all_here()
    crossing = {}
    for chunk in (2, 3, 4, 5, 1, 0):
        block = 2 * chunk + core
        if chunk < 2:
            src, dst = own.at[block], other.at[block]
        else:
            src, dst = tiles.at[chunk - 2], other.at[block, rows_of(tile_at[chunk], 1)]
        crossing[chunk] = go(src, dst, cross_send.at[chunk], cross_recv.at[chunk], place.cross())
    bias_copy = go(bias.at[0], bias.at[1], cross_send.at[6], cross_recv.at[6], place.cross())
    get_node.wait()
    for side in (0, 1):
        picks = (lax.broadcasted_iota(jnp.int32, (256, 64), 0) == send_ref[side : side + 1, :]).astype(F32)
        halo_out[side] = tdot(picks.astype(BF16), node[...]).astype(BF16)
    up_rows = go(halo_out.at[1], halo.at[0], halo_send.at[0], halo_recv.at[0], place.partition(1))
    down_rows = go(halo_out.at[0], halo.at[1], halo_send.at[1], halo_recv.at[1], place.partition(63))
    for k in range(4):
        cols = slice(128 * k, 128 * k + 128)
        src_row = src_ref[pl.ds(4 * hid + k, 1), :]
        dst_row = dst_ref[pl.ds(4 * hid + k, 1), :]
        pick_src[:, cols] = (lax.broadcasted_iota(jnp.int32, (384, 128), 0) == src_row).astype(F32).astype(BF16)
        pick_dst[:, cols] = (lax.broadcasted_iota(jnp.int32, (256, 128), 0) == dst_row).astype(F32).astype(BF16)
    spread = Gather(place, other, spread_send, spread_recv, other)
    for chunk in (2, 3, 4, 5):
        crossing[chunk].wait_recv()
        spread.start(chunk, 0)
    dequantize_in(own, w_in, w_in_scale, 1, 9)
    for chunk in (2, 3, 4, 5):
        spread.arrived(chunk, 0)
        spread.start(chunk, 1)
    inp[2] = tdot(pick_dst[...], node[...]).astype(BF16)
    get_agg.wait()
    up[...] = tdot(pick_dst[...], gagg[...])
    ext[0:256] = node[...]
    up_rows.wait_recv()
    down_rows.wait_recv()
    ext[256:320] = jnp.where(dom > 0, halo[0], jnp.zeros((64, 512), BF16))
    ext[320:384] = jnp.where(dom < 63, halo[1], jnp.zeros((64, 512), BF16))
    inp[1] = tdot(pick_src[...], ext[...]).astype(BF16)
    get_edge.wait()
    for chunk in (2, 3, 4, 5):
        spread.arrived(chunk, 1)
        spread.start(chunk, 2)

    def forward(slot, j):
        pre = bias[slot, pl.ds(j, 1), :]
        for r in range(3):
            pre = pre + dot(inp[r], weights[slot, 3 + 3 * j + r])
        sigma = 1.0 / (1.0 + jnp.exp(-pre))
        value = pre * sigma
        act[3 * slot + j] = value.astype(BF16)
        slope[3 * slot + j] = sigma + value * (1.0 - sigma)

    def forward_own(j, _):
        forward(0, j)
        return 0

    lax.fori_loop(0, 3, forward_own, 0)
    crossing[1].wait_recv()
    spread.start(1, 3)
    for chunk in (2, 3, 4, 5):
        spread.arrived(chunk, 2)
        spread.start(chunk, 3)
    crossing[0].wait_recv()
    spread.start(0, 3)
    for r in range(3):
        inpt[r] = inp[r].T
    get_cot.wait()
    bias_copy.wait_recv()
    for chunk in (1, 2):
        spread.arrived(chunk, 3)
    forward(1, 0)
    for chunk in (3, 4):
        spread.arrived(chunk, 3)
    forward(1, 1)
    spread.arrived(5, 3)
    forward(1, 2)
    spread.arrived(0, 3)

    for side in range(2):
        result = bias_out_ref[:, 256 * side : 256 * side + 256]
        for slot in range(2):
            for j in range(2):
                result = result + dot(act[3 * slot + j], weights[slot, side, 256 * j : 256 * j + 256, :])
            result = result + dot(act[3 * slot + 2], weights[slot, 2, 256 * side : 256 * side + 256, :])
        msg[:, 256 * side : 256 * side + 256] = result

    live = live_ref[0] - hid * 512
    gain = gain_ref[...]

    def norm(i, carry):
        rows = pl.ds(pl.multiple_of(i * 64, 64), 64)
        mask = (lax.broadcasted_iota(jnp.int32, (64, 512), 0) + i * 64) < live
        upstream = jnp.where(mask, gedge[rows, :].astype(F32) + up[rows, :], 0.0)
        up[rows, :] = upstream
        message = msg[rows, :]
        centre = message - jnp.mean(message, axis=1, keepdims=True)
        inverse = lax.rsqrt(jnp.mean(centre * centre, axis=1, keepdims=True) + EPS)
        normed = centre * inverse
        scaled = upstream * gain
        shift = jnp.mean(scaled, axis=1, keepdims=True)
        tilt = jnp.mean(scaled * normed, axis=1, keepdims=True)
        grad = inverse * (scaled - shift - normed * tilt)
        low[rows, :] = grad.astype(BF16)

        def fold(value):
            return jnp.sum(value.reshape(8, 8, 512), axis=0)

        return (carry[0] + fold(grad), carry[1] + fold(upstream * normed), carry[2] + fold(upstream))

    zero = jnp.zeros((8, 512), F32)
    vectors = lax.fori_loop(0, 8, norm, (zero, zero, zero))
    sums[...] = jnp.zeros((16, 256), F32)
    for i in range(3):
        row = jnp.sum(vectors[i], axis=0, keepdims=True)
        sums[6 + 2 * i : 7 + 2 * i, :] = row[:, 0:256]
        sums[7 + 2 * i : 8 + 2 * i, :] = row[:, 256:512]

    reduce = Reduce(
        place, grads, core_in, first_in, first_out, second_in, second_out, third_in, reduce_send, reduce_recv
    )
    gather = Gather(place, total, gather_send, gather_recv, total_hbm)
    halves = (hid, 1 - hid)
    for slot in range(2):
        for j in range(3):
            part = tdot(act[3 * slot + j], low[...]).astype(BF16)
            if j < 2:
                place_rows(grads, 0, 256 * j, part[:, 0:256], halves[slot])
                place_rows(grads, 1, 256 * j, part[:, 256:512], halves[slot])
            else:
                place_rows(grads, 2, 0, part[:, 0:256], halves[slot])
                place_rows(grads, 2, 256, part[:, 256:512], halves[slot])
    reduce.share(0)
    for slot in range(2):
        for j in range(3):
            if j < 2:
                rows = slice(256 * j, 256 * j + 256)
                grad = ndot(low[:, 0:256], weights[slot, 0, rows, :])
                grad = grad + ndot(low[:, 256:512], weights[slot, 1, rows, :])
            else:
                grad = ndot(low[:, 0:256], weights[slot, 2, 0:256, :])
                grad = grad + ndot(low[:, 256:512], weights[slot, 2, 256:512, :])
            grad = grad * slope[3 * slot + j]
            sums[pl.ds(3 * halves[slot] + j, 1), :] = jnp.sum(grad, axis=0, keepdims=True)
            pre_low[3 * slot + j] = grad.astype(BF16)
    sum_copy = go(sums, sum_core.at[0], sum_send.at[0, 0], sum_recv.at[0, 0], place.other_core())

    def first_layer(m):
        for slot in range(2):
            part = dot(inpt[m % 3], pre_low[3 * slot + m // 3]).astype(BF16)
            place_rows(grads, 3 + m, 0, part, halves[slot])

    def produce(chunk):
        if chunk > 1:
            first_layer(2 * chunk - 3)
        first_layer(2 * chunk - 2)
        reduce.share(chunk)

    def input_grads(r):
        result = jnp.zeros((512, 512), F32)
        for slot in range(2):
            for j in range(3):
                result = result + ndot(pre_low[3 * slot + j], weights[slot, 3 + 3 * j + r])
        return result

    ring_copies = []

    def sums_ring(level, value):
        axis = "zxy"[level]
        mine = getattr(place, axis)
        sum_ring[level, mine] = value
        ring_copies.clear()
        for j in RING:
            part = sum_ring.at[level, mine]
            ring_copies.append(
                go(part, part, sum_send.at[1 + level, j], sum_recv.at[1 + level, j], place.ring(axis, j))
            )

    def ring_sum(level):
        for copy in ring_copies:
            copy.wait_recv()
        return sum_ring[level, 0] + sum_ring[level, 1] + sum_ring[level, 2] + sum_ring[level, 3]

    def extra_a():
        table = dot(pick_src[...], input_grads(1).astype(BF16))
        own_table[...] = table[0:256]
        halo_table[...] = table[256:384].astype(BF16)
        extra["up"] = go(halo_table.at[64:128], halo_in.at[0], node_send.at[0], node_recv.at[0], place.partition(1))
        extra["down"] = go(halo_table.at[0:64], halo_in.at[1], node_send.at[1], node_recv.at[1], place.partition(63))
        sum_copy.wait_recv()
        sums_ring(0, sums[...] + sum_core[0])

    def extra_b():
        own_table[...] += dot(pick_dst[...], input_grads(2).astype(BF16))

    def extra_c():
        grad_edge[...] = (input_grads(0) + up[...]).astype(BF16)

    def extra_d():
        extra["up"].wait_recv()
        extra["down"].wait_recv()
        value = own_table[...]
        for side in (0, 1):
            picks = (lax.broadcasted_iota(jnp.int32, (256, 64), 0) == send_ref[side : side + 1, :]).astype(F32)
            there = (dom < 63) if side == 1 else (dom > 0)
            picks = jnp.where(there, picks, 0.0).astype(BF16)
            value = value + dot(picks, halo_in[side])
        own_table[...] = value
        node_out[...] = jnp.where(hid == 0, value[:, 256:512], value[:, 0:256]).astype(BF16)
        extra["swap"] = go(node_out, node_in, node_send.at[2], node_recv.at[2], (dom, 1 - hid))
        sums_ring(1, ring_sum(0))

    def extra_e():
        sums_ring(2, ring_sum(1))

    def extra_f():
        extra["swap"].wait_recv()
        keep = jnp.where(hid == 0, own_table[:, 0:256], own_table[:, 256:512])
        grad_node[...] = (keep + node_in[...].astype(F32)).astype(BF16)
        summed[...] = ring_sum(2) * (1.0 / 1024)

    extra = {}
    writes = []

    def write(chunk):
        block = 2 * chunk + core
        copy = pltpu.make_async_copy(total.at[block], total_hbm.at[block], write_sem.at[chunk])
        copy.start()
        writes.append(copy)

    def stage(name, chunk):
        if name == "add":
            reduce.add_core(chunk)
        elif name == "first":
            reduce.add_first(chunk)
        elif name == "second":
            reduce.add_second(chunk)
        elif name == "third":
            value = reduce.add_third(chunk) * (1.0 / 1024)
            total[2 * chunk + core, rows_of(own_tile(place, chunk), 1), :] = value.astype(BF16)
            gather.start(chunk, 0)
        elif name == "gather":
            gather.arrived(chunk, 0)
            gather.start(chunk, 1)
        elif name == "more":
            gather.arrived(chunk, 1)
            gather.start(chunk, 2)
        else:
            gather.arrived(chunk, 2)
            gather.start(chunk, 3)
            write(chunk)

    produce(1)
    stage("add", 0)
    produce(2)
    stage("add", 1)
    produce(3)
    stage("add", 2)
    produce(4)
    stage("add", 3)
    produce(5)
    events = []
    for name, chunk_at in (("add", 2.0), ("first", 9.0), ("second", 13.5), ("third", 17.5)):
        for chunk in range(CHUNKS):
            if name != "add" or chunk > 3:
                events.append((chunk_at + 2.0 * chunk, name, chunk))
    for name, chunk_at in (("gather", 21.5), ("more", 25.5), ("last", 31.5)):
        for chunk in range(CHUNKS):
            events.append((chunk_at + 2.0 * chunk, name, chunk))
    for extra_at, run in ((8.5, extra_a), (10.2, extra_b), (11.2, extra_c), (14.4, extra_d), (19.0, extra_e), (25.0, extra_f)):
        events.append((extra_at, "run", run))
    for _, name, item in sorted(events, key=lambda event: event[0]):
        if name == "run":
            item()
        else:
            stage(name, item)
    for chunk in range(CHUNKS):
        gather.arrived(chunk, 3)
    spread.sent()
    reduce.sent()
    gather.sent()
    for copy in flying:
        copy.wait_send()
    for copy in writes:
        copy.wait()


def finish_kernel(
    total, edge_in, node_in, summed, w_out, w_in, bias, vectors, grad_edge, grad_node, raw, wide, read_sem, write_sem
):
    hid = lax.axis_index("hid")
    moves = [
        pltpu.make_async_copy(total.at[block], raw.at[block], read_sem.at[block]) for block in range(12)
    ]
    for copy in moves:
        copy.start()
    through = [
        pltpu.make_async_copy(edge_in, grad_edge, read_sem.at[12]),
        pltpu.make_async_copy(node_in, grad_node, read_sem.at[13]),
    ]
    for copy in through:
        copy.start()
    for i in range(3):
        vectors[i : i + 1, 0:256] = summed[6 + 2 * i : 7 + 2 * i, :]
        vectors[i : i + 1, 256:512] = summed[7 + 2 * i : 8 + 2 * i, :]
    picked = jnp.where(hid == 0, summed[0:3, :], summed[3:6, :])
    for j in range(3):
        for k in range(2):
            bias[2 * j + k : 2 * j + k + 1, :] = picked[j : j + 1, 128 * k : 128 * k + 128]
    writes = []
    for block in range(12):
        moves[block].wait()

        def part(i, _):
            rows = pl.ds(pl.multiple_of(i * 128, 128), 128)
            wide[block, rows, :] = raw[block, rows, :].astype(F32)
            return 0

        lax.fori_loop(0, 4, part, 0)
        if block < 2:
            parts = [(wide.at[block], w_out.at[0:512, 256 * block : 256 * block + 256])]
        elif block == 2:
            parts = [
                (wide.at[2, 0:256], w_out.at[512:768, 0:256]),
                (wide.at[2, 256:512], w_out.at[512:768, 256:512]),
            ]
        else:
            r, j = (block - 3) % 3, (block - 3) // 3
            parts = [(wide.at[block], w_in.at[512 * r : 512 * r + 512, 256 * j : 256 * j + 256])]
        for src, dst in parts:
            copy = pltpu.make_async_copy(src, dst, write_sem.at[len(writes)])
            copy.start()
            writes.append(copy)
    for copy in writes + through:
        copy.wait()


def vmem():
    return pl.BlockSpec(memory_space=pltpu.VMEM)


def smem():
    return pl.BlockSpec(memory_space=pltpu.SMEM)


def anywhere():
    return pl.BlockSpec(memory_space=pl.ANY)


def shape(dims, dtype):
    return jax.ShapeDtypeStruct(dims, dtype)


def dma(*dims):
    return pltpu.SemaphoreType.DMA(dims)


def per_device(
    node_latent,
    edge_latent,
    send_rows,
    edge_src,
    edge_dst,
    edge_live,
    w_in_blocks,
    w_in_scale,
    bias_in,
    w_out_blocks,
    w_out_scale,
    bias_out,
    norm_gain,
    grad_edge,
    grad_agg,
):
    total, edge_in, node_in, summed = pl.pallas_call(
        main_kernel,
        out_shape=(
            shape((12, 512, 256), BF16),
            shape((512, 512), BF16),
            shape((256, 256), BF16),
            shape((16, 256), F32),
        ),
        in_specs=[
            anywhere(),
            anywhere(),
            vmem(),
            vmem(),
            vmem(),
            smem(),
            anywhere(),
            smem(),
            vmem(),
            anywhere(),
            smem(),
            vmem(),
            vmem(),
            anywhere(),
            anywhere(),
        ],
        out_specs=(anywhere(), vmem(), vmem(), vmem()),
        scratch_shapes=[
            pltpu.VMEM((256, 512), BF16),
            pltpu.VMEM((1536, 768), BF16),
            pltpu.VMEM((768, 512), BF16),
            pltpu.VMEM((256, 512), BF16),
            pltpu.VMEM((512, 512), BF16),
            pltpu.VMEM((2, 12, 512, 256), BF16),
            pltpu.VMEM((2, 8, 256), F32),
            pltpu.VMEM((2, 64, 512), BF16),
            pltpu.VMEM((2, 64, 512), BF16),
            pltpu.VMEM((4, 16, 256), BF16),
            pltpu.VMEM((3, 512, 512), BF16),
            pltpu.VMEM((3, 512, 512), BF16),
            pltpu.VMEM((384, 512), BF16),
            pltpu.VMEM((384, 512), BF16),
            pltpu.VMEM((256, 512), BF16),
            pltpu.VMEM((6, 512, 256), BF16),
            pltpu.VMEM((6, 512, 256), F32),
            pltpu.VMEM((512, 512), F32),
            pltpu.VMEM((512, 512), F32),
            pltpu.VMEM((512, 512), BF16),
            pltpu.VMEM((6, 512, 256), BF16),
            pltpu.VMEM((12, 1024, 256), BF16),
            pltpu.VMEM((6, 1024, 256), BF16),
            pltpu.VMEM((6, 3, 256, 256), BF16),
            pltpu.VMEM((6, 256, 256), BF16),
            pltpu.VMEM((6, 3, 64, 256), BF16),
            pltpu.VMEM((6, 64, 256), BF16),
            pltpu.VMEM((6, 3, 16, 256), BF16),
            pltpu.VMEM((12, 512, 256), BF16),
            pltpu.VMEM((16, 256), F32),
            pltpu.VMEM((1, 16, 256), F32),
            pltpu.VMEM((3, 4, 16, 256), F32),
            pltpu.VMEM((256, 512), F32),
            pltpu.VMEM((128, 512), BF16),
            pltpu.VMEM((2, 64, 512), BF16),
            pltpu.VMEM((256, 256), BF16),
            pltpu.VMEM((256, 256), BF16),
            dma(6),
            dma(6, 8),
            dma(6, 8),
            dma(7),
            dma(7),
            dma(2),
            dma(2),
            dma(6, 10),
            dma(6, 10),
            dma(6, 8),
            dma(6, 8),
            dma(4, 4),
            dma(4, 4),
            dma(3),
            dma(3),
            dma(6),
        ],
        compiler_params=pltpu.CompilerParams(
            collective_id=0, has_side_effects=True, vmem_limit_bytes=LIMIT
        ),
        name="message_grads",
    )(
        node_latent,
        edge_latent,
        send_rows[0],
        edge_src.reshape(8, 128),
        edge_dst.reshape(8, 128),
        edge_live,
        w_in_blocks,
        w_in_scale.T,
        bias_in.reshape(6, 128),
        w_out_blocks,
        w_out_scale.T,
        bias_out.reshape(1, 512),
        norm_gain.reshape(1, 512),
        grad_edge,
        grad_agg,
    )
    grad_w_out, grad_w_in, grad_bias, vectors, grad_edge_in, grad_node = pl.pallas_call(
        finish_kernel,
        out_shape=(
            shape((768, 512), F32),
            shape((1536, 768), F32),
            shape((6, 128), F32),
            shape((3, 512), F32),
            shape((512, 512), BF16),
            shape((256, 256), BF16),
        ),
        in_specs=[anywhere(), anywhere(), anywhere(), vmem()],
        out_specs=(anywhere(), anywhere(), vmem(), vmem(), anywhere(), anywhere()),
        scratch_shapes=[
            pltpu.VMEM((12, 512, 256), BF16),
            pltpu.VMEM((12, 512, 256), F32),
            dma(14),
            dma(13),
        ],
        compiler_params=pltpu.CompilerParams(vmem_limit_bytes=LIMIT),
        name="widen_grads",
    )(total, edge_in, node_in, summed)
    return (grad_edge_in, grad_node, grad_w_in, grad_bias.reshape(768), grad_w_out, vectors)


def solution(mesh):
    in_specs = (
        P("dom", None),
        P("dom", None),
        P("dom", None, None),
        P("dom"),
        P("dom"),
        P("dom"),
        P(None, "hid"),
        P(None, "hid"),
        P("hid"),
        P("hid", None),
        P("hid", None),
        P(),
        P(),
        P("dom", None),
        P("dom", None),
    )
    out_specs = (
        P(("dom", "hid"), None),
        P("dom", "hid"),
        P(None, "hid"),
        P("hid"),
        P("hid", None),
        P(),
    )
    return jax.shard_map(
        per_device, mesh=mesh, in_specs=in_specs, out_specs=out_specs, check_vma=False
    )
```

```python
import jax
import jax.numpy as jnp
from jax import lax
from jax.experimental import pallas as pl
from jax.experimental.pallas import tpu as pltpu
from jax.sharding import PartitionSpec as P

EPS = 1e-05
MESH = pl.DeviceIdType.MESH
F32 = jnp.float32
BF16 = jnp.bfloat16
CHUNKS = 6
LIMIT = 60 << 20


class Place:
    def __init__(self):
        dom = lax.axis_index("dom")
        self.hid = lax.axis_index("hid")
        self.dom = dom
        self.z = lax.div(dom, 16)
        self.x = lax.rem(lax.div(dom, 4), 4)
        self.yl = lax.rem(lax.div(dom, 2), 2)
        self.y = 2 * self.hid + self.yl
        self.core = lax.rem(dom, 2)

    def at(self, z=None, x=None, y=None, core=None):
        z = self.z if z is None else z
        x = self.x if x is None else x
        y = self.y if y is None else y
        core = self.core if core is None else core
        return (((z * 4 + x) * 2 + lax.rem(y, 2)) * 2 + core, lax.div(y, 2))

    def ring(self, axis, step):
        return self.at(**{axis: lax.rem(getattr(self, axis) + step, 4)})

    def other_core(self):
        return self.at(core=1 - self.core)

    def cross(self):
        return self.at(y=3 - self.y)

    def pair(self):
        return self.at(y=self.y + 1 - 2 * self.yl)

    def partition(self, step):
        return (lax.rem(self.dom + step, 64), self.hid)


def greet(partners):
    barrier = pltpu.get_barrier_semaphore()
    for partner in partners:
        pl.semaphore_signal(barrier, inc=1, device_id=partner, device_id_type=MESH)
    return lambda: pl.semaphore_wait(barrier, len(partners))


def remote(src, dst, send_sem, recv_sem, target):
    return pltpu.make_async_remote_copy(
        src_ref=src,
        dst_ref=dst,
        send_sem=send_sem,
        recv_sem=recv_sem,
        device_id=target,
        device_id_type=MESH,
    )


AXES = (
    ("z", "x", "y"),
    ("x", "z", "y"),
    ("y", "z", "x"),
    ("z", "x", "y"),
    ("x", "z", "y"),
    ("y", "x", "z"),
)


def tiles_known(chunk):
    return 2 if AXES[chunk][2] == "y" else 4


def first_tile(place, chunk, yl=None):
    yl = place.yl if yl is None else yl
    a, b, _ = AXES[chunk]
    if a == "y":
        return (yl * 4 + getattr(place, b)) * 4
    return (getattr(place, a) * 4 + getattr(place, b)) * 2


def rows_of(first, count, unit=16):
    return pl.ds(pl.multiple_of(first * unit, unit), count * unit)


def gather_steps(place, chunk):
    a, b, _ = AXES[chunk]
    ring = [place.ring(b, j) for j in (1, 2, 3)]
    known = tiles_known(chunk)
    if a == "y":
        last = (place.yl * 16, 16, [place.pair()])
    else:
        last = (getattr(place, a) * 8, 8, [place.ring(a, j) for j in (1, 2, 3)])
    return [(first_tile(place, chunk), known, ring), last]


class Gather:
    def __init__(self, place, buf, send_sem, recv_sem, result):
        self.place, self.buf, self.result = place, buf, result
        self.send_sem, self.recv_sem = send_sem, recv_sem
        self.steps = {}
        self.flying = {}

    def start(self, chunk, step):
        place = self.place
        if chunk not in self.steps:
            self.steps[chunk] = gather_steps(place, chunk)
        block = 2 * chunk + place.core
        if step == 2:
            first, count, targets = 0, 32, [place.other_core()]
            base = 6
        else:
            first, count, targets = self.steps[chunk][step]
            base = sum(len(s[2]) for s in self.steps[chunk][:step])
        part = self.buf.at[block, rows_of(first, count)]
        goal = self.result.at[block] if step == 2 else part
        copies = []
        for j, target in enumerate(targets):
            copy = remote(
                part, goal, self.send_sem.at[chunk, base + j], self.recv_sem.at[chunk, base + j], target
            )
            copy.start()
            copies.append(copy)
        self.flying[chunk, step] = copies

    def arrived(self, chunk, step):
        for copy in self.flying[chunk, step]:
            copy.wait_recv()

    def sent(self):
        for copies in self.flying.values():
            for copy in copies:
                copy.wait_send()


RING = (1, 2, 3)
GATHERED = (3, 4, 2, 1, 5)
DIRECT = (0,)


def tdot(a, b):
    return lax.dot_general(a, b, (((0,), (0,)), ((), ())), preferred_element_type=F32)


def ndot(a, b):
    return lax.dot_general(a, b, (((1,), (1,)), ((), ())), preferred_element_type=F32)


def dot(a, b):
    return jnp.dot(a, b, preferred_element_type=F32)


def dequantize_out(own, w_out_ref, scales):
    for a in range(6):
        for b in range(4):
            value = w_out_ref[128 * a : 128 * a + 128, 128 * b : 128 * b + 128].astype(F32) * scales[b, a]
            if a < 4:
                index, row = b // 2, 128 * a
            else:
                index, row = 2, 128 * (a - 4) + 256 * (b // 2)
            col = 128 * (b % 2)
            own[index, row : row + 128, col : col + 128] = value.astype(BF16)


def dequantize_in(own, w_in_ref, scales, first, last):
    def block(index, _):
        j = lax.div(index, 3)
        r = lax.rem(index, 3)
        for a in range(4):
            for b in range(2):
                scale = scales[2 * j + b, 4 * r + a]
                rows = pl.ds(pl.multiple_of(512 * r + 128 * a, 128), 128)
                cols = pl.ds(pl.multiple_of(256 * j + 128 * b, 128), 128)
                value = w_in_ref[rows, cols].astype(F32) * scale
                own[3 + index, 128 * a : 128 * a + 128, 128 * b : 128 * b + 128] = value.astype(BF16)
        return 0

    lax.fori_loop(first, last, block, 0)


def dequantize_tiles(tile, w_in_ref, scales, index, q, count):
    j = lax.div(index, 3)
    r = lax.rem(index, 3)
    rows = pl.ds(pl.multiple_of(512 * r + 16 * q, 16), 16 * count)
    for b in range(2):
        scale = scales[2 * j + b, 4 * r + lax.div(q, 8)]
        cols = pl.ds(pl.multiple_of(256 * j + 128 * b, 128), 128)
        tile[0 : 16 * count, 128 * b : 128 * b + 128] = (w_in_ref[rows, cols].astype(F32) * scale).astype(BF16)


def dequantize_out_tiles(tile, w_out_ref, scales, q, wanted):
    side = lax.div(q, 16)
    row = lax.rem(q, 16)
    rows = pl.ds(pl.multiple_of(512 + 16 * row, 16), 32)
    for b in range(2):
        scale = scales[2 * side + b, 4 + lax.div(row, 8)]
        cols = pl.ds(pl.multiple_of(256 * side + 128 * b, 128), 128)
        value = w_out_ref[rows, cols].astype(F32) * scale
        kept = tile[0:32, 128 * b : 128 * b + 128].astype(F32)
        tile[0:32, 128 * b : 128 * b + 128] = jnp.where(wanted, value, kept).astype(BF16)


def place_rows(grads, block, first, value, half):
    count = value.shape[0]
    group = 512 if AXES[block // 2][0] == "y" else 32
    size = min(group, count)
    for at in range(0, count, size):
        row = first + at
        base = (row // group) * 2 * group + row % group
        grads[block, pl.ds(pl.multiple_of(base + group * half, 32), size), :] = value[at : at + size]


class Reduce:
    def __init__(self, place, grads, core_in, first_in, first_out, second_in, second_out, third_in, send_sem, recv_sem):
        self.place, self.grads, self.core_in = place, grads, core_in
        self.first_in, self.first_out = first_in, first_out
        self.second_in, self.second_out, self.third_in = second_in, second_out, third_in
        self.send_sem, self.recv_sem = send_sem, recv_sem
        self.flying = {}

    def send(self, chunk, stage, index, src, dst, target):
        copy = remote(src, dst, self.send_sem.at[chunk, index], self.recv_sem.at[chunk, index], target)
        copy.start()
        self.flying.setdefault((chunk, stage), []).append(copy)

    def arrived(self, chunk, stage):
        for copy in self.flying[chunk, stage]:
            copy.wait_recv()

    def sent(self):
        for copies in self.flying.values():
            for copy in copies:
                copy.wait_send()

    def share(self, chunk):
        core = self.place.core
        src = self.grads.at[2 * chunk + 1 - core]
        self.send(chunk, 0, 0, src, self.core_in.at[chunk], self.place.other_core())

    def spread(self, chunk, level, src, dst, unit):
        axis = AXES[chunk][level]
        mine = getattr(self.place, axis)
        for j in RING:
            at = lax.rem(mine + j, 4)
            part = src.at[rows_of(at, 1, unit)]
            self.send(chunk, level + 1, 3 * level + j, part, dst.at[j - 1], self.place.ring(axis, j))

    def kept(self, chunk, level, src, unit):
        mine = getattr(self.place, AXES[chunk][level])
        return src[rows_of(mine, 1, unit), :].astype(F32)

    def add_core(self, chunk):
        self.arrived(chunk, 0)
        block = 2 * chunk + self.place.core

        def part(i, _):
            rows = pl.ds(pl.multiple_of(i * 128, 128), 128)
            mine = self.grads[block, rows, :].astype(F32)
            self.grads[block, rows, :] = (mine + self.core_in[chunk, rows, :].astype(F32)).astype(BF16)
            return 0

        lax.fori_loop(0, 8, part, 0)
        self.spread(chunk, 0, self.grads.at[block], self.first_in.at[chunk], 256)

    def add_first(self, chunk):
        self.arrived(chunk, 1)
        value = self.kept(chunk, 0, self.grads.at[2 * chunk + self.place.core], 256)
        for j in range(3):
            value = value + self.first_in[chunk, j].astype(F32)
        self.first_out[chunk] = value.astype(BF16)
        self.spread(chunk, 1, self.first_out.at[chunk], self.second_in.at[chunk], 64)

    def add_second(self, chunk):
        self.arrived(chunk, 2)
        value = self.kept(chunk, 1, self.first_out.at[chunk], 64)
        for j in range(3):
            value = value + self.second_in[chunk, j].astype(F32)
        self.second_out[chunk] = value.astype(BF16)
        axis = AXES[chunk][2]
        mine = getattr(self.place, axis)
        rows = 16 * tiles_known(chunk)
        if axis == "y":
            self.third_in[chunk, mine, 0:rows, :] = self.second_out[chunk, rows_of(self.place.hid, 1, 32), :]
        else:
            self.third_in[chunk, mine] = self.second_out[chunk]
        for j in RING:
            if axis == "y":
                half = lax.div(lax.rem(mine + j, 4), 2)
                part = self.second_out.at[chunk, rows_of(half, 1, 32)]
            else:
                part = self.second_out.at[chunk]
            goal = self.third_in.at[chunk, mine, pl.ds(0, rows)]
            self.send(chunk, 3, 6 + j, part, goal, self.place.ring(axis, j))

    def add_third(self, chunk):
        self.arrived(chunk, 3)
        rows = 16 * tiles_known(chunk)
        value = self.third_in[chunk, 0, 0:rows, :].astype(F32)
        for at in range(1, 4):
            value = value + self.third_in[chunk, at, 0:rows, :].astype(F32)
        return value


def main_kernel(
    node_hbm,
    edge_hbm,
    send_ref,
    src_ref,
    dst_ref,
    live_ref,
    w_in_hbm,
    w_in_scale,
    bias_ref,
    w_out_hbm,
    w_out_scale,
    bias_out_ref,
    gain_ref,
    gedge_hbm,
    gagg_hbm,
    total_hbm,
    grad_edge,
    grad_node,
    summed,
    node,
    w_in,
    w_out,
    gagg,
    gedge,
    weights,
    bias,
    halo,
    halo_out,
    tiles,
    inp,
    inpt,
    ext,
    pick_src,
    pick_dst,
    act,
    slope,
    up,
    msg,
    low,
    pre_low,
    grads,
    core_in,
    first_in,
    first_out,
    second_in,
    second_out,
    third_in,
    total,
    sums,
    sum_core,
    sum_ring,
    own_table,
    halo_table,
    halo_in,
    node_out,
    node_in,
    local_sem,
    spread_send,
    spread_recv,
    cross_send,
    cross_recv,
    halo_send,
    halo_recv,
    reduce_send,
    reduce_recv,
    gather_send,
    gather_recv,
    sum_send,
    sum_recv,
    node_send,
    node_recv,
    write_sem,
):
    place = Place()
    hid, dom, core = place.hid, place.dom, place.core
    first_edge = pl.multiple_of(hid * 512, 512)

    def fetch(index, src, dst):
        copy = pltpu.make_async_copy(src, dst, local_sem.at[index])
        copy.start()
        return copy

    get_w_in = fetch(1, w_in_hbm, w_in)
    get_w_out = fetch(0, w_out_hbm, w_out)
    get_node = fetch(2, node_hbm, node)
    get_edge = fetch(3, edge_hbm.at[pl.ds(first_edge, 512)], inp.at[0])
    get_agg = fetch(4, gagg_hbm, gagg)
    get_cot = fetch(5, gedge_hbm.at[pl.ds(first_edge, 512)], gedge)
    partners = [place.ring(axis, j) for axis in "zxy" for j in RING]
    partners += [place.other_core(), place.cross(), place.partition(1), place.partition(63)]
    all_here = greet(partners)
    flying = []

    def go(src, dst, send_sem, recv_sem, target):
        copy = remote(src, dst, send_sem, recv_sem, target)
        copy.start()
        flying.append(copy)
        return copy

    own, other = weights.at[0], weights.at[1]
    bias[0] = jnp.zeros((8, 256), F32)
    for j in range(3):
        bias[0, j : j + 1, 0:128] = bias_ref[2 * j : 2 * j + 1, :]
        bias[0, j : j + 1, 128:256] = bias_ref[2 * j + 1 : 2 * j + 2, :]
    for k in range(4):
        cols = slice(128 * k, 128 * k + 128)
        src_row = src_ref[pl.ds(4 * hid + k, 1), :]
        dst_row = dst_ref[pl.ds(4 * hid + k, 1), :]
        pick_src[:, cols] = (lax.broadcasted_iota(jnp.int32, (384, 128), 0) == src_row).astype(F32).astype(BF16)
        pick_dst[:, cols] = (lax.broadcasted_iota(jnp.int32, (256, 128), 0) == dst_row).astype(F32).astype(BF16)
    get_node.wait()
    for side in (0, 1):
        picks = (lax.broadcasted_iota(jnp.int32, (256, 64), 0) == send_ref[side : side + 1, :]).astype(F32)
        halo_out[side] = tdot(picks.astype(BF16), node[...]).astype(BF16)
    get_w_in.wait()
    tile_at = {}
    for chunk in GATHERED:
        known = tiles_known(chunk)
        index = 2 * chunk + core - 3
        if chunk == 1:
            index = 0
        tile_at[chunk] = first_tile(place, chunk, 1 - place.yl)
        dequantize_tiles(tiles.at[chunk - 1], w_in, w_in_scale, index, tile_at[chunk], known)
    get_w_out.wait()
    dequantize_out_tiles(tiles.at[0], w_out, w_out_scale, tile_at[1], core == 0)
    all_here()
    crossing = {}

    def cross(chunk, src, dst):
        crossing[chunk] = go(src, dst, cross_send.at[chunk], cross_recv.at[chunk], place.cross())

    for chunk in GATHERED:
        rows = 16 * tiles_known(chunk)
        goal = other.at[2 * chunk + core, pl.ds(pl.multiple_of(16 * tile_at[chunk], 16), rows)]
        cross(chunk, tiles.at[chunk - 1, pl.ds(0, rows)], goal)
    up_rows = go(halo_out.at[1], halo.at[0], halo_send.at[0], halo_recv.at[0], place.partition(1))
    down_rows = go(halo_out.at[0], halo.at[1], halo_send.at[1], halo_recv.at[1], place.partition(63))
    bias_copy = go(bias.at[0], bias.at[1], cross_send.at[6], cross_recv.at[6], place.cross())
    dequantize_out(own, w_out, w_out_scale)
    dequantize_in(own, w_in, w_in_scale, 0, 1)
    for chunk in DIRECT:
        cross(chunk, own.at[2 * chunk + core], other.at[2 * chunk + core])
    spread = Gather(place, other, spread_send, spread_recv, other)
    for chunk in GATHERED:
        crossing[chunk].wait_recv()
        spread.start(chunk, 0)
    dequantize_in(own, w_in, w_in_scale, 1, 9)
    inp[2] = tdot(pick_dst[...], node[...]).astype(BF16)
    get_agg.wait()
    up[...] = tdot(pick_dst[...], gagg[...])
    ext[0:256] = node[...]
    for chunk in GATHERED:
        spread.arrived(chunk, 0)
        spread.start(chunk, 1)
    up_rows.wait_recv()
    down_rows.wait_recv()
    ext[256:320] = jnp.where(dom > 0, halo[0], jnp.zeros((64, 512), BF16))
    ext[320:384] = jnp.where(dom < 63, halo[1], jnp.zeros((64, 512), BF16))
    inp[1] = tdot(pick_src[...], ext[...]).astype(BF16)
    get_edge.wait()

    def forward(slot, j):
        pre = bias[slot, pl.ds(j, 1), :]
        for r in range(3):
            pre = pre + dot(inp[r], weights[slot, 3 + 3 * j + r])
        sigma = 1.0 / (1.0 + jnp.exp(-pre))
        value = pre * sigma
        act[3 * slot + j] = value.astype(BF16)
        slope[3 * slot + j] = sigma + value * (1.0 - sigma)

    def forward_own(j, _):
        forward(0, j)
        return 0

    lax.fori_loop(0, 3, forward_own, 0)
    for chunk in DIRECT:
        crossing[chunk].wait_recv()
        spread.start(chunk, 2)
    for chunk in GATHERED:
        spread.arrived(chunk, 1)
        spread.start(chunk, 2)
    for r in range(3):
        inpt[r] = inp[r].T
    get_cot.wait()
    bias_copy.wait_recv()
    for chunk in (3, 4):
        spread.arrived(chunk, 2)
    forward(1, 1)
    for chunk in (1, 2):
        spread.arrived(chunk, 2)
    forward(1, 0)
    spread.arrived(5, 2)
    forward(1, 2)
    spread.arrived(0, 2)

    for side in range(2):
        result = bias_out_ref[:, 256 * side : 256 * side + 256]
        for slot in range(2):
            for j in range(2):
                result = result + dot(act[3 * slot + j], weights[slot, side, 256 * j : 256 * j + 256, :])
            result = result + dot(act[3 * slot + 2], weights[slot, 2, 256 * side : 256 * side + 256, :])
        msg[:, 256 * side : 256 * side + 256] = result

    live = live_ref[0] - hid * 512
    gain = gain_ref[...]

    def norm(i, carry):
        rows = pl.ds(pl.multiple_of(i * 64, 64), 64)
        mask = (lax.broadcasted_iota(jnp.int32, (64, 512), 0) + i * 64) < live
        upstream = jnp.where(mask, gedge[rows, :].astype(F32) + up[rows, :], 0.0)
        up[rows, :] = upstream
        message = msg[rows, :]
        centre = message - jnp.mean(message, axis=1, keepdims=True)
        inverse = lax.rsqrt(jnp.mean(centre * centre, axis=1, keepdims=True) + EPS)
        normed = centre * inverse
        scaled = upstream * gain
        shift = jnp.mean(scaled, axis=1, keepdims=True)
        tilt = jnp.mean(scaled * normed, axis=1, keepdims=True)
        grad = inverse * (scaled - shift - normed * tilt)
        low[rows, :] = grad.astype(BF16)

        def fold(value):
            return jnp.sum(value.reshape(8, 8, 512), axis=0)

        return (carry[0] + fold(grad), carry[1] + fold(upstream * normed), carry[2] + fold(upstream))

    zero = jnp.zeros((8, 512), F32)
    vectors = lax.fori_loop(0, 8, norm, (zero, zero, zero))
    sums[...] = jnp.zeros((16, 256), F32)
    for i in range(3):
        row = jnp.sum(vectors[i], axis=0, keepdims=True)
        sums[6 + 2 * i : 7 + 2 * i, :] = row[:, 0:256]
        sums[7 + 2 * i : 8 + 2 * i, :] = row[:, 256:512]

    reduce = Reduce(
        place, grads, core_in, first_in, first_out, second_in, second_out, third_in, reduce_send, reduce_recv
    )
    gather = Gather(place, total, gather_send, gather_recv, total_hbm)
    halves = (hid, 1 - hid)
    for slot in range(2):
        for j in range(3):
            part = tdot(act[3 * slot + j], low[...]).astype(BF16)
            if j < 2:
                place_rows(grads, 0, 256 * j, part[:, 0:256], halves[slot])
                place_rows(grads, 1, 256 * j, part[:, 256:512], halves[slot])
            else:
                place_rows(grads, 2, 0, part[:, 0:256], halves[slot])
                place_rows(grads, 2, 256, part[:, 256:512], halves[slot])
    reduce.share(0)
    for slot in range(2):
        for j in range(3):
            if j < 2:
                rows = slice(256 * j, 256 * j + 256)
                grad = ndot(low[:, 0:256], weights[slot, 0, rows, :])
                grad = grad + ndot(low[:, 256:512], weights[slot, 1, rows, :])
            else:
                grad = ndot(low[:, 0:256], weights[slot, 2, 0:256, :])
                grad = grad + ndot(low[:, 256:512], weights[slot, 2, 256:512, :])
            grad = grad * slope[3 * slot + j]
            sums[pl.ds(3 * halves[slot] + j, 1), :] = jnp.sum(grad, axis=0, keepdims=True)
            pre_low[3 * slot + j] = grad.astype(BF16)
    sum_copy = go(sums, sum_core.at[0], sum_send.at[0, 0], sum_recv.at[0, 0], place.other_core())

    def first_layer(m):
        for slot in range(2):
            part = dot(inpt[m % 3], pre_low[3 * slot + m // 3]).astype(BF16)
            place_rows(grads, 3 + m, 0, part, halves[slot])

    def produce(chunk):
        if chunk > 1:
            first_layer(2 * chunk - 3)
        first_layer(2 * chunk - 2)
        reduce.share(chunk)

    def input_grads(r):
        result = jnp.zeros((512, 512), F32)
        for slot in range(2):
            for j in range(3):
                result = result + ndot(pre_low[3 * slot + j], weights[slot, 3 + 3 * j + r])
        return result

    ring_copies = []

    def sums_ring(level, value):
        axis = "zxy"[level]
        mine = getattr(place, axis)
        sum_ring[level, mine] = value
        ring_copies.clear()
        for j in RING:
            part = sum_ring.at[level, mine]
            ring_copies.append(
                go(part, part, sum_send.at[1 + level, j], sum_recv.at[1 + level, j], place.ring(axis, j))
            )

    def ring_sum(level):
        for copy in ring_copies:
            copy.wait_recv()
        return sum_ring[level, 0] + sum_ring[level, 1] + sum_ring[level, 2] + sum_ring[level, 3]

    def extra_a():
        table = dot(pick_src[...], input_grads(1).astype(BF16))
        own_table[...] = table[0:256]
        halo_table[...] = table[256:384].astype(BF16)
        extra["up"] = go(halo_table.at[64:128], halo_in.at[0], node_send.at[0], node_recv.at[0], place.partition(1))
        extra["down"] = go(halo_table.at[0:64], halo_in.at[1], node_send.at[1], node_recv.at[1], place.partition(63))
        sum_copy.wait_recv()
        sums_ring(0, sums[...] + sum_core[0])

    def extra_b():
        own_table[...] += dot(pick_dst[...], input_grads(2).astype(BF16))

    def extra_c():
        grad_edge[...] = (input_grads(0) + up[...]).astype(BF16)

    def extra_d():
        extra["up"].wait_recv()
        extra["down"].wait_recv()
        value = own_table[...]
        for side in (0, 1):
            picks = (lax.broadcasted_iota(jnp.int32, (256, 64), 0) == send_ref[side : side + 1, :]).astype(F32)
            there = (dom < 63) if side == 1 else (dom > 0)
            picks = jnp.where(there, picks, 0.0).astype(BF16)
            value = value + dot(picks, halo_in[side])
        own_table[...] = value
        node_out[...] = jnp.where(hid == 0, value[:, 256:512], value[:, 0:256]).astype(BF16)
        extra["swap"] = go(node_out, node_in, node_send.at[2], node_recv.at[2], (dom, 1 - hid))
        sums_ring(1, ring_sum(0))

    def extra_e():
        sums_ring(2, ring_sum(1))

    def extra_f():
        extra["swap"].wait_recv()
        keep = jnp.where(hid == 0, own_table[:, 0:256], own_table[:, 256:512])
        grad_node[...] = (keep + node_in[...].astype(F32)).astype(BF16)
        summed[...] = ring_sum(2) * (1.0 / 1024)

    extra = {}
    writes = []

    def write(chunk):
        block = 2 * chunk + core
        copy = pltpu.make_async_copy(total.at[block], total_hbm.at[block], write_sem.at[chunk])
        copy.start()
        writes.append(copy)

    def stage(name, chunk):
        if name == "add":
            reduce.add_core(chunk)
        elif name == "first":
            reduce.add_first(chunk)
        elif name == "second":
            reduce.add_second(chunk)
        elif name == "third":
            value = reduce.add_third(chunk) * (1.0 / 1024)
            rows = pl.ds(pl.multiple_of(16 * first_tile(place, chunk), 16), 16 * tiles_known(chunk))
            total[2 * chunk + core, rows, :] = value.astype(BF16)
            gather.start(chunk, 0)
        elif name == "gather":
            gather.arrived(chunk, 0)
            gather.start(chunk, 1)
        else:
            gather.arrived(chunk, 1)
            gather.start(chunk, 2)
            write(chunk)

    produce(1)
    stage("add", 0)
    produce(2)
    stage("add", 1)
    produce(3)
    stage("add", 2)
    produce(4)
    stage("add", 3)
    produce(5)
    events = []
    for name, chunk_at in (("add", 2.0), ("first", 9.0), ("second", 13.5), ("third", 17.5), ("gather", 21.5), ("last", 27.5)):
        for chunk in range(CHUNKS):
            if name != "add" or chunk > 3:
                events.append((chunk_at + 2.0 * chunk, name, chunk))
    for extra_at, run in ((8.5, extra_a), (10.2, extra_b), (11.2, extra_c), (14.4, extra_d), (19.0, extra_e), (25.0, extra_f)):
        events.append((extra_at, "run", run))
    for _, name, item in sorted(events, key=lambda event: event[0]):
        if name == "run":
            item()
        else:
            stage(name, item)
    for chunk in range(CHUNKS):
        gather.arrived(chunk, 2)
    spread.sent()
    reduce.sent()
    gather.sent()
    for copy in flying:
        copy.wait_send()
    for copy in writes:
        copy.wait()


def finish_kernel(
    total, edge_in, node_in, summed, w_out, w_in, bias, vectors, grad_edge, grad_node, raw, wide, read_sem, write_sem
):
    hid = lax.axis_index("hid")
    moves = [
        pltpu.make_async_copy(total.at[block], raw.at[block], read_sem.at[block]) for block in range(12)
    ]
    for copy in moves:
        copy.start()
    grad_edge[...] = edge_in[...]
    grad_node[...] = node_in[...]
    for i in range(3):
        vectors[i : i + 1, 0:256] = summed[6 + 2 * i : 7 + 2 * i, :]
        vectors[i : i + 1, 256:512] = summed[7 + 2 * i : 8 + 2 * i, :]
    picked = jnp.where(hid == 0, summed[0:3, :], summed[3:6, :])
    for j in range(3):
        for k in range(2):
            bias[2 * j + k : 2 * j + k + 1, :] = picked[j : j + 1, 128 * k : 128 * k + 128]
    writes = []
    for block in range(12):
        moves[block].wait()

        def part(i, _):
            rows = pl.ds(pl.multiple_of(i * 128, 128), 128)
            wide[block, rows, :] = raw[block, rows, :].astype(F32)
            return 0

        lax.fori_loop(0, 4, part, 0)
        if block < 2:
            parts = [(wide.at[block], w_out.at[0:512, 256 * block : 256 * block + 256])]
        elif block == 2:
            parts = [
                (wide.at[2, 0:256], w_out.at[512:768, 0:256]),
                (wide.at[2, 256:512], w_out.at[512:768, 256:512]),
            ]
        else:
            r, j = (block - 3) % 3, (block - 3) // 3
            parts = [(wide.at[block], w_in.at[512 * r : 512 * r + 512, 256 * j : 256 * j + 256])]
        for src, dst in parts:
            copy = pltpu.make_async_copy(src, dst, write_sem.at[len(writes)])
            copy.start()
            writes.append(copy)
    for copy in writes:
        copy.wait()


def vmem():
    return pl.BlockSpec(memory_space=pltpu.VMEM)


def smem():
    return pl.BlockSpec(memory_space=pltpu.SMEM)


def anywhere():
    return pl.BlockSpec(memory_space=pl.ANY)


def shape(dims, dtype):
    return jax.ShapeDtypeStruct(dims, dtype)


def dma(*dims):
    return pltpu.SemaphoreType.DMA(dims)


def per_device(
    node_latent,
    edge_latent,
    send_rows,
    edge_src,
    edge_dst,
    edge_live,
    w_in_blocks,
    w_in_scale,
    bias_in,
    w_out_blocks,
    w_out_scale,
    bias_out,
    norm_gain,
    grad_edge,
    grad_agg,
):
    total, edge_in, node_in, summed = pl.pallas_call(
        main_kernel,
        out_shape=(
            shape((12, 512, 256), BF16),
            shape((512, 512), BF16),
            shape((256, 256), BF16),
            shape((16, 256), F32),
        ),
        in_specs=[
            anywhere(),
            anywhere(),
            vmem(),
            vmem(),
            vmem(),
            smem(),
            anywhere(),
            smem(),
            vmem(),
            anywhere(),
            smem(),
            vmem(),
            vmem(),
            anywhere(),
            anywhere(),
        ],
        out_specs=(anywhere(), vmem(), vmem(), vmem()),
        scratch_shapes=[
            pltpu.VMEM((256, 512), BF16),
            pltpu.VMEM((1536, 768), BF16),
            pltpu.VMEM((768, 512), BF16),
            pltpu.VMEM((256, 512), BF16),
            pltpu.VMEM((512, 512), BF16),
            pltpu.VMEM((2, 12, 512, 256), BF16),
            pltpu.VMEM((2, 8, 256), F32),
            pltpu.VMEM((2, 64, 512), BF16),
            pltpu.VMEM((2, 64, 512), BF16),
            pltpu.VMEM((5, 64, 256), BF16),
            pltpu.VMEM((3, 512, 512), BF16),
            pltpu.VMEM((3, 512, 512), BF16),
            pltpu.VMEM((384, 512), BF16),
            pltpu.VMEM((384, 512), BF16),
            pltpu.VMEM((256, 512), BF16),
            pltpu.VMEM((6, 512, 256), BF16),
            pltpu.VMEM((6, 512, 256), F32),
            pltpu.VMEM((512, 512), F32),
            pltpu.VMEM((512, 512), F32),
            pltpu.VMEM((512, 512), BF16),
            pltpu.VMEM((6, 512, 256), BF16),
            pltpu.VMEM((12, 1024, 256), BF16),
            pltpu.VMEM((6, 1024, 256), BF16),
            pltpu.VMEM((6, 3, 256, 256), BF16),
            pltpu.VMEM((6, 256, 256), BF16),
            pltpu.VMEM((6, 3, 64, 256), BF16),
            pltpu.VMEM((6, 64, 256), BF16),
            pltpu.VMEM((6, 4, 64, 256), BF16),
            pltpu.VMEM((12, 512, 256), BF16),
            pltpu.VMEM((16, 256), F32),
            pltpu.VMEM((1, 16, 256), F32),
            pltpu.VMEM((3, 4, 16, 256), F32),
            pltpu.VMEM((256, 512), F32),
            pltpu.VMEM((128, 512), BF16),
            pltpu.VMEM((2, 64, 512), BF16),
            pltpu.VMEM((256, 256), BF16),
            pltpu.VMEM((256, 256), BF16),
            dma(6),
            dma(6, 8),
            dma(6, 8),
            dma(7),
            dma(7),
            dma(2),
            dma(2),
            dma(6, 10),
            dma(6, 10),
            dma(6, 8),
            dma(6, 8),
            dma(4, 4),
            dma(4, 4),
            dma(3),
            dma(3),
            dma(6),
        ],
        compiler_params=pltpu.CompilerParams(
            collective_id=0, has_side_effects=True, vmem_limit_bytes=LIMIT
        ),
        name="message_grads",
    )(
        node_latent,
        edge_latent,
        send_rows[0],
        edge_src.reshape(8, 128),
        edge_dst.reshape(8, 128),
        edge_live,
        w_in_blocks,
        w_in_scale.T,
        bias_in.reshape(6, 128),
        w_out_blocks,
        w_out_scale.T,
        bias_out.reshape(1, 512),
        norm_gain.reshape(1, 512),
        grad_edge,
        grad_agg,
    )
    grad_w_out, grad_w_in, grad_bias, vectors, grad_edge_in, grad_node = pl.pallas_call(
        finish_kernel,
        out_shape=(
            shape((768, 512), F32),
            shape((1536, 768), F32),
            shape((6, 128), F32),
            shape((3, 512), F32),
            shape((512, 512), BF16),
            shape((256, 256), BF16),
        ),
        in_specs=[anywhere(), vmem(), vmem(), vmem()],
        out_specs=(anywhere(), anywhere(), vmem(), vmem(), vmem(), vmem()),
        scratch_shapes=[
            pltpu.VMEM((12, 512, 256), BF16),
            pltpu.VMEM((12, 512, 256), F32),
            dma(12),
            dma(13),
        ],
        compiler_params=pltpu.CompilerParams(vmem_limit_bytes=LIMIT),
        name="widen_grads",
    )(total, edge_in, node_in, summed)
    return (grad_edge_in, grad_node, grad_w_in, grad_bias.reshape(768), grad_w_out, vectors)


def solution(mesh):
    in_specs = (
        P("dom", None),
        P("dom", None),
        P("dom", None, None),
        P("dom"),
        P("dom"),
        P("dom"),
        P(None, "hid"),
        P(None, "hid"),
        P("hid"),
        P("hid", None),
        P("hid", None),
        P(),
        P(),
        P("dom", None),
        P("dom", None),
    )
    out_specs = (
        P(("dom", "hid"), None),
        P("dom", "hid"),
        P(None, "hid"),
        P("hid"),
        P("hid", None),
        P(),
    )
    return jax.shard_map(
        per_device, mesh=mesh, in_specs=in_specs, out_specs=out_specs, check_vma=False
    )
```

```python
import jax
import jax.numpy as jnp
from jax import lax
from jax.experimental import pallas as pl
from jax.experimental.pallas import tpu as pltpu
from jax.sharding import PartitionSpec as P

EPS = 1e-05
MESH = pl.DeviceIdType.MESH
F32 = jnp.float32
BF16 = jnp.bfloat16
CHUNKS = 6
LIMIT = 60 << 20


class Place:
    def __init__(self):
        dom = lax.axis_index("dom")
        self.hid = lax.axis_index("hid")
        self.dom = dom
        self.z = lax.div(dom, 16)
        self.x = lax.rem(lax.div(dom, 4), 4)
        self.yl = lax.rem(lax.div(dom, 2), 2)
        self.y = 2 * self.hid + self.yl
        self.core = lax.rem(dom, 2)

    def at(self, z=None, x=None, y=None, core=None):
        z = self.z if z is None else z
        x = self.x if x is None else x
        y = self.y if y is None else y
        core = self.core if core is None else core
        return (((z * 4 + x) * 2 + lax.rem(y, 2)) * 2 + core, lax.div(y, 2))

    def ring(self, axis, step):
        return self.at(**{axis: lax.rem(getattr(self, axis) + step, 4)})

    def other_core(self):
        return self.at(core=1 - self.core)

    def cross(self):
        return self.at(y=3 - self.y)

    def pair(self):
        return self.at(y=self.y + 1 - 2 * self.yl)

    def partition(self, step):
        return (lax.rem(self.dom + step, 64), self.hid)


def greet(partners):
    barrier = pltpu.get_barrier_semaphore()
    for partner in partners:
        pl.semaphore_signal(barrier, inc=1, device_id=partner, device_id_type=MESH)
    return lambda: pl.semaphore_wait(barrier, len(partners))


def remote(src, dst, send_sem, recv_sem, target):
    return pltpu.make_async_remote_copy(
        src_ref=src,
        dst_ref=dst,
        send_sem=send_sem,
        recv_sem=recv_sem,
        device_id=target,
        device_id_type=MESH,
    )


AXES = (
    ("z", "x", "y"),
    ("x", "z", "y"),
    ("y", "z", "x"),
    ("z", "x", "y"),
    ("x", "z", "y"),
    ("y", "x", "z"),
)


def tiles_known(chunk):
    return 2 if AXES[chunk][2] == "y" else 4


def first_tile(place, chunk, yl=None):
    yl = place.yl if yl is None else yl
    a, b, _ = AXES[chunk]
    if a == "y":
        return (yl * 4 + getattr(place, b)) * 4
    return (getattr(place, a) * 4 + getattr(place, b)) * 2


def rows_of(first, count, unit=16):
    return pl.ds(pl.multiple_of(first * unit, unit), count * unit)


def gather_steps(place, chunk):
    a, b, _ = AXES[chunk]
    ring = [place.ring(b, j) for j in (1, 2, 3)]
    known = tiles_known(chunk)
    if a == "y":
        last = (place.yl * 16, 16, [place.pair()])
    else:
        last = (getattr(place, a) * 8, 8, [place.ring(a, j) for j in (1, 2, 3)])
    return [(first_tile(place, chunk), known, ring), last]


class Gather:
    def __init__(self, place, buf, send_sem, recv_sem, result):
        self.place, self.buf, self.result = place, buf, result
        self.send_sem, self.recv_sem = send_sem, recv_sem
        self.steps = {}
        self.flying = {}

    def start(self, chunk, step):
        place = self.place
        if chunk not in self.steps:
            self.steps[chunk] = gather_steps(place, chunk)
        block = 2 * chunk + place.core
        if step == 2:
            first, count, targets = 0, 32, [place.other_core()]
            base = 6
        else:
            first, count, targets = self.steps[chunk][step]
            base = sum(len(s[2]) for s in self.steps[chunk][:step])
        part = self.buf.at[block, rows_of(first, count)]
        goal = self.result.at[block] if step == 2 else part
        copies = []
        for j, target in enumerate(targets):
            copy = remote(
                part, goal, self.send_sem.at[chunk, base + j], self.recv_sem.at[chunk, base + j], target
            )
            copy.start()
            copies.append(copy)
        self.flying[chunk, step] = copies

    def arrived(self, chunk, step):
        for copy in self.flying[chunk, step]:
            copy.wait_recv()

    def sent(self):
        for copies in self.flying.values():
            for copy in copies:
                copy.wait_send()


RING = (1, 2, 3)
GATHERED = (3, 4, 2, 1, 5)
DIRECT = (0,)


def tdot(a, b):
    return lax.dot_general(a, b, (((0,), (0,)), ((), ())), preferred_element_type=F32)


def ndot(a, b):
    return lax.dot_general(a, b, (((1,), (1,)), ((), ())), preferred_element_type=F32)


def dot(a, b):
    return jnp.dot(a, b, preferred_element_type=F32)


def dequantize_out(own, w_out_ref, scales):
    for a in range(6):
        for b in range(4):
            value = w_out_ref[128 * a : 128 * a + 128, 128 * b : 128 * b + 128].astype(F32) * scales[b, a]
            if a < 4:
                index, row = b // 2, 128 * a
            else:
                index, row = 2, 128 * (a - 4) + 256 * (b // 2)
            col = 128 * (b % 2)
            own[index, row : row + 128, col : col + 128] = value.astype(BF16)


def dequantize_in(own, w_in_ref, scales, first, last):
    def block(index, _):
        j = lax.div(index, 3)
        r = lax.rem(index, 3)
        for a in range(4):
            for b in range(2):
                scale = scales[2 * j + b, 4 * r + a]
                rows = pl.ds(pl.multiple_of(512 * r + 128 * a, 128), 128)
                cols = pl.ds(pl.multiple_of(256 * j + 128 * b, 128), 128)
                value = w_in_ref[rows, cols].astype(F32) * scale
                own[3 + index, 128 * a : 128 * a + 128, 128 * b : 128 * b + 128] = value.astype(BF16)
        return 0

    lax.fori_loop(first, last, block, 0)


def dequantize_tiles(tile, w_in_ref, scales, index, q, count):
    j = lax.div(index, 3)
    r = lax.rem(index, 3)
    rows = pl.ds(pl.multiple_of(512 * r + 16 * q, 16), 16 * count)
    for b in range(2):
        scale = scales[2 * j + b, 4 * r + lax.div(q, 8)]
        cols = pl.ds(pl.multiple_of(256 * j + 128 * b, 128), 128)
        tile[0 : 16 * count, 128 * b : 128 * b + 128] = (w_in_ref[rows, cols].astype(F32) * scale).astype(BF16)


def dequantize_out_tiles(tile, w_out_ref, scales, q, wanted):
    side = lax.div(q, 16)
    row = lax.rem(q, 16)
    rows = pl.ds(pl.multiple_of(512 + 16 * row, 16), 32)
    for b in range(2):
        scale = scales[2 * side + b, 4 + lax.div(row, 8)]
        cols = pl.ds(pl.multiple_of(256 * side + 128 * b, 128), 128)
        value = w_out_ref[rows, cols].astype(F32) * scale
        kept = tile[0:32, 128 * b : 128 * b + 128].astype(F32)
        tile[0:32, 128 * b : 128 * b + 128] = jnp.where(wanted, value, kept).astype(BF16)


def place_rows(grads, block, first, value, half):
    count = value.shape[0]
    group = 512 if AXES[block // 2][0] == "y" else 32
    size = min(group, count)
    for at in range(0, count, size):
        row = first + at
        base = (row // group) * 2 * group + row % group
        grads[block, pl.ds(pl.multiple_of(base + group * half, 32), size), :] = value[at : at + size]


ORDER = (
    "P1", "A0", "P2", "A1", "P3", "A2", "P4", "A3", "P5", "A4", "A5", "F0",
    "Xa", "F1", "F2", "F3", "Xb", "S0", "F4", "S1", "F5", "S2", "S3", "Xd",
    "T0", "S4", "T1", "S5", "T2", "Xe", "T3", "T4", "T5", "G0", "G1", "G2",
    "G3", "Xc", "G4", "G5", "Xf", "L0", "L1", "L2", "L3", "L4", "L5",
)


class Reduce:
    def __init__(self, place, grads, core_in, first_in, first_out, second_in, second_out, third_in, send_sem, recv_sem):
        self.place, self.grads, self.core_in = place, grads, core_in
        self.first_in, self.first_out = first_in, first_out
        self.second_in, self.second_out, self.third_in = second_in, second_out, third_in
        self.send_sem, self.recv_sem = send_sem, recv_sem
        self.flying = {}

    def send(self, chunk, stage, index, src, dst, target):
        copy = remote(src, dst, self.send_sem.at[chunk, index], self.recv_sem.at[chunk, index], target)
        copy.start()
        self.flying.setdefault((chunk, stage), []).append(copy)

    def arrived(self, chunk, stage):
        for copy in self.flying[chunk, stage]:
            copy.wait_recv()

    def sent(self):
        for copies in self.flying.values():
            for copy in copies:
                copy.wait_send()

    def share(self, chunk):
        core = self.place.core
        src = self.grads.at[2 * chunk + 1 - core]
        self.send(chunk, 0, 0, src, self.core_in.at[chunk], self.place.other_core())

    def spread(self, chunk, level, src, dst, unit):
        axis = AXES[chunk][level]
        mine = getattr(self.place, axis)
        for j in RING:
            at = lax.rem(mine + j, 4)
            part = src.at[rows_of(at, 1, unit)]
            self.send(chunk, level + 1, 3 * level + j, part, dst.at[j - 1], self.place.ring(axis, j))

    def kept(self, chunk, level, src, unit):
        mine = getattr(self.place, AXES[chunk][level])
        return src[rows_of(mine, 1, unit), :].astype(F32)

    def add_core(self, chunk):
        self.arrived(chunk, 0)
        block = 2 * chunk + self.place.core

        def part(i, _):
            rows = pl.ds(pl.multiple_of(i * 128, 128), 128)
            self.grads[block, rows, :] = self.grads[block, rows, :] + self.core_in[chunk, rows, :]
            return 0

        lax.fori_loop(0, 8, part, 0)
        self.spread(chunk, 0, self.grads.at[block], self.first_in.at[chunk], 256)

    def add_first(self, chunk):
        self.arrived(chunk, 1)
        value = self.kept(chunk, 0, self.grads.at[2 * chunk + self.place.core], 256)
        for j in range(3):
            value = value + self.first_in[chunk, j].astype(F32)
        self.first_out[chunk] = value.astype(BF16)
        self.spread(chunk, 1, self.first_out.at[chunk], self.second_in.at[chunk], 64)

    def add_second(self, chunk):
        self.arrived(chunk, 2)
        value = self.kept(chunk, 1, self.first_out.at[chunk], 64)
        for j in range(3):
            value = value + self.second_in[chunk, j].astype(F32)
        self.second_out[chunk] = value.astype(BF16)
        axis = AXES[chunk][2]
        mine = getattr(self.place, axis)
        rows = 16 * tiles_known(chunk)
        if axis == "y":
            self.third_in[chunk, mine, 0:rows, :] = self.second_out[chunk, rows_of(self.place.hid, 1, 32), :]
        else:
            self.third_in[chunk, mine] = self.second_out[chunk]
        for j in RING:
            if axis == "y":
                half = lax.div(lax.rem(mine + j, 4), 2)
                part = self.second_out.at[chunk, rows_of(half, 1, 32)]
            else:
                part = self.second_out.at[chunk]
            goal = self.third_in.at[chunk, mine, pl.ds(0, rows)]
            self.send(chunk, 3, 6 + j, part, goal, self.place.ring(axis, j))

    def add_third(self, chunk):
        self.arrived(chunk, 3)
        rows = 16 * tiles_known(chunk)
        value = self.third_in[chunk, 0, 0:rows, :].astype(F32)
        for at in range(1, 4):
            value = value + self.third_in[chunk, at, 0:rows, :].astype(F32)
        return value


def main_kernel(
    node_hbm,
    edge_hbm,
    send_ref,
    src_ref,
    dst_ref,
    live_ref,
    w_in_hbm,
    w_in_scale,
    bias_ref,
    w_out_hbm,
    w_out_scale,
    bias_out_ref,
    gain_ref,
    gedge_hbm,
    gagg_hbm,
    total_hbm,
    grad_edge,
    grad_node,
    summed,
    node,
    w_in,
    w_out,
    gagg,
    gedge,
    weights,
    bias,
    halo,
    halo_out,
    tiles,
    inp,
    inpt,
    ext,
    pick_src,
    pick_dst,
    act,
    slope,
    up,
    msg,
    low,
    pre_low,
    grads,
    core_in,
    first_in,
    first_out,
    second_in,
    second_out,
    third_in,
    total,
    sums,
    sum_core,
    sum_ring,
    own_table,
    halo_table,
    halo_in,
    node_out,
    node_in,
    local_sem,
    spread_send,
    spread_recv,
    cross_send,
    cross_recv,
    halo_send,
    halo_recv,
    reduce_send,
    reduce_recv,
    gather_send,
    gather_recv,
    sum_send,
    sum_recv,
    node_send,
    node_recv,
    write_sem,
):
    place = Place()
    hid, dom, core = place.hid, place.dom, place.core
    first_edge = pl.multiple_of(hid * 512, 512)

    def fetch(index, src, dst):
        copy = pltpu.make_async_copy(src, dst, local_sem.at[index])
        copy.start()
        return copy

    get_w_in = fetch(1, w_in_hbm, w_in)
    get_w_out = fetch(0, w_out_hbm, w_out)
    get_node = fetch(2, node_hbm, node)
    get_edge = fetch(3, edge_hbm.at[pl.ds(first_edge, 512)], inp.at[0])
    get_agg = fetch(4, gagg_hbm, gagg)
    get_cot = fetch(5, gedge_hbm.at[pl.ds(first_edge, 512)], gedge)
    partners = [place.ring(axis, j) for axis in "zxy" for j in RING]
    partners += [place.other_core(), place.cross(), place.partition(1), place.partition(63)]
    all_here = greet(partners)
    flying = []

    def go(src, dst, send_sem, recv_sem, target):
        copy = remote(src, dst, send_sem, recv_sem, target)
        copy.start()
        flying.append(copy)
        return copy

    own, other = weights.at[0], weights.at[1]
    bias[0] = jnp.zeros((8, 256), F32)
    for j in range(3):
        bias[0, j : j + 1, 0:128] = bias_ref[2 * j : 2 * j + 1, :]
        bias[0, j : j + 1, 128:256] = bias_ref[2 * j + 1 : 2 * j + 2, :]
    for k in range(4):
        cols = slice(128 * k, 128 * k + 128)
        src_row = src_ref[pl.ds(4 * hid + k, 1), :]
        dst_row = dst_ref[pl.ds(4 * hid + k, 1), :]
        pick_src[:, cols] = (lax.broadcasted_iota(jnp.int32, (384, 128), 0) == src_row).astype(F32).astype(BF16)
        pick_dst[:, cols] = (lax.broadcasted_iota(jnp.int32, (256, 128), 0) == dst_row).astype(F32).astype(BF16)
    get_node.wait()
    for side in (0, 1):
        picks = (lax.broadcasted_iota(jnp.int32, (256, 64), 0) == send_ref[side : side + 1, :]).astype(F32)
        halo_out[side] = tdot(picks.astype(BF16), node[...]).astype(BF16)
    get_w_in.wait()
    tile_at = {}
    for chunk in GATHERED:
        known = tiles_known(chunk)
        index = 2 * chunk + core - 3
        if chunk == 1:
            index = 0
        tile_at[chunk] = first_tile(place, chunk, 1 - place.yl)
        dequantize_tiles(tiles.at[chunk - 1], w_in, w_in_scale, index, tile_at[chunk], known)
    get_w_out.wait()
    dequantize_out_tiles(tiles.at[0], w_out, w_out_scale, tile_at[1], core == 0)
    all_here()
    crossing = {}

    def cross(chunk, src, dst):
        crossing[chunk] = go(src, dst, cross_send.at[chunk], cross_recv.at[chunk], place.cross())

    for chunk in GATHERED:
        rows = 16 * tiles_known(chunk)
        goal = other.at[2 * chunk + core, pl.ds(pl.multiple_of(16 * tile_at[chunk], 16), rows)]
        cross(chunk, tiles.at[chunk - 1, pl.ds(0, rows)], goal)
    up_rows = go(halo_out.at[1], halo.at[0], halo_send.at[0], halo_recv.at[0], place.partition(1))
    down_rows = go(halo_out.at[0], halo.at[1], halo_send.at[1], halo_recv.at[1], place.partition(63))
    bias_copy = go(bias.at[0], bias.at[1], cross_send.at[6], cross_recv.at[6], place.cross())
    dequantize_out(own, w_out, w_out_scale)
    dequantize_in(own, w_in, w_in_scale, 0, 1)
    for chunk in DIRECT:
        cross(chunk, own.at[2 * chunk + core], other.at[2 * chunk + core])
    spread = Gather(place, other, spread_send, spread_recv, other)
    for chunk in GATHERED:
        crossing[chunk].wait_recv()
        spread.start(chunk, 0)
    dequantize_in(own, w_in, w_in_scale, 1, 9)
    inp[2] = tdot(pick_dst[...], node[...]).astype(BF16)
    get_agg.wait()
    up[...] = tdot(pick_dst[...], gagg[...])
    ext[0:256] = node[...]
    for chunk in GATHERED:
        spread.arrived(chunk, 0)
        spread.start(chunk, 1)
    up_rows.wait_recv()
    down_rows.wait_recv()
    ext[256:320] = jnp.where(dom > 0, halo[0], jnp.zeros((64, 512), BF16))
    ext[320:384] = jnp.where(dom < 63, halo[1], jnp.zeros((64, 512), BF16))
    inp[1] = tdot(pick_src[...], ext[...]).astype(BF16)
    get_edge.wait()

    def forward(slot, j):
        pre = bias[slot, pl.ds(j, 1), :]
        for r in range(3):
            pre = pre + dot(inp[r], weights[slot, 3 + 3 * j + r])
        sigma = 1.0 / (1.0 + jnp.exp(-pre))
        value = pre * sigma
        act[3 * slot + j] = value.astype(BF16)
        slope[3 * slot + j] = sigma + value * (1.0 - sigma)

    def forward_own(j, _):
        forward(0, j)
        return 0

    lax.fori_loop(0, 3, forward_own, 0)
    for chunk in DIRECT:
        crossing[chunk].wait_recv()
        spread.start(chunk, 2)
    for chunk in GATHERED:
        spread.arrived(chunk, 1)
        spread.start(chunk, 2)
    for r in range(3):
        inpt[r] = inp[r].T
    get_cot.wait()
    bias_copy.wait_recv()
    for chunk in (3, 4):
        spread.arrived(chunk, 2)
    forward(1, 1)
    for chunk in (1, 2):
        spread.arrived(chunk, 2)
    forward(1, 0)
    spread.arrived(5, 2)
    forward(1, 2)
    spread.arrived(0, 2)

    for side in range(2):
        result = bias_out_ref[:, 256 * side : 256 * side + 256]
        for slot in range(2):
            for j in range(2):
                result = result + dot(act[3 * slot + j], weights[slot, side, 256 * j : 256 * j + 256, :])
            result = result + dot(act[3 * slot + 2], weights[slot, 2, 256 * side : 256 * side + 256, :])
        msg[:, 256 * side : 256 * side + 256] = result

    live = live_ref[0] - hid * 512
    gain = gain_ref[...]

    def norm(i, carry):
        rows = pl.ds(pl.multiple_of(i * 64, 64), 64)
        mask = (lax.broadcasted_iota(jnp.int32, (64, 512), 0) + i * 64) < live
        upstream = jnp.where(mask, gedge[rows, :].astype(F32) + up[rows, :], 0.0)
        up[rows, :] = upstream
        message = msg[rows, :]
        centre = message - jnp.mean(message, axis=1, keepdims=True)
        inverse = lax.rsqrt(jnp.mean(centre * centre, axis=1, keepdims=True) + EPS)
        normed = centre * inverse
        scaled = upstream * gain
        shift = jnp.mean(scaled, axis=1, keepdims=True)
        tilt = jnp.mean(scaled * normed, axis=1, keepdims=True)
        grad = inverse * (scaled - shift - normed * tilt)
        low[rows, :] = grad.astype(BF16)

        def fold(value):
            return jnp.sum(value.reshape(8, 8, 512), axis=0)

        return (carry[0] + fold(grad), carry[1] + fold(upstream * normed), carry[2] + fold(upstream))

    zero = jnp.zeros((8, 512), F32)
    vectors = lax.fori_loop(0, 8, norm, (zero, zero, zero))
    sums[...] = jnp.zeros((16, 256), F32)
    for i in range(3):
        row = jnp.sum(vectors[i], axis=0, keepdims=True)
        sums[6 + 2 * i : 7 + 2 * i, :] = row[:, 0:256]
        sums[7 + 2 * i : 8 + 2 * i, :] = row[:, 256:512]

    reduce = Reduce(
        place, grads, core_in, first_in, first_out, second_in, second_out, third_in, reduce_send, reduce_recv
    )
    gather = Gather(place, total, gather_send, gather_recv, total_hbm)
    halves = (hid, 1 - hid)
    for slot in range(2):
        for j in range(3):
            part = tdot(act[3 * slot + j], low[...]).astype(BF16)
            if j < 2:
                place_rows(grads, 0, 256 * j, part[:, 0:256], halves[slot])
                place_rows(grads, 1, 256 * j, part[:, 256:512], halves[slot])
            else:
                place_rows(grads, 2, 0, part[:, 0:256], halves[slot])
                place_rows(grads, 2, 256, part[:, 256:512], halves[slot])
    reduce.share(0)
    for slot in range(2):
        for j in range(3):
            if j < 2:
                rows = slice(256 * j, 256 * j + 256)
                grad = ndot(low[:, 0:256], weights[slot, 0, rows, :])
                grad = grad + ndot(low[:, 256:512], weights[slot, 1, rows, :])
            else:
                grad = ndot(low[:, 0:256], weights[slot, 2, 0:256, :])
                grad = grad + ndot(low[:, 256:512], weights[slot, 2, 256:512, :])
            grad = grad * slope[3 * slot + j]
            sums[pl.ds(3 * halves[slot] + j, 1), :] = jnp.sum(grad, axis=0, keepdims=True)
            pre_low[3 * slot + j] = grad.astype(BF16)
    sum_copy = go(sums, sum_core.at[0], sum_send.at[0, 0], sum_recv.at[0, 0], place.other_core())

    def first_layer(m):
        for slot in range(2):
            part = dot(inpt[m % 3], pre_low[3 * slot + m // 3]).astype(BF16)
            place_rows(grads, 3 + m, 0, part, halves[slot])

    def produce(chunk):
        if chunk > 1:
            first_layer(2 * chunk - 3)
        first_layer(2 * chunk - 2)
        reduce.share(chunk)

    def input_grads(r):
        result = jnp.zeros((512, 512), F32)
        for slot in range(2):
            for j in range(3):
                result = result + ndot(pre_low[3 * slot + j], weights[slot, 3 + 3 * j + r])
        return result

    ring_copies = []

    def sums_ring(level, value):
        axis = "zxy"[level]
        mine = getattr(place, axis)
        sum_ring[level, mine] = value
        ring_copies.clear()
        for j in RING:
            part = sum_ring.at[level, mine]
            ring_copies.append(
                go(part, part, sum_send.at[1 + level, j], sum_recv.at[1 + level, j], place.ring(axis, j))
            )

    def ring_sum(level):
        for copy in ring_copies:
            copy.wait_recv()
        return sum_ring[level, 0] + sum_ring[level, 1] + sum_ring[level, 2] + sum_ring[level, 3]

    def extra_a():
        table = dot(pick_src[...], input_grads(1).astype(BF16))
        own_table[...] = table[0:256]
        halo_table[...] = table[256:384].astype(BF16)
        extra["up"] = go(halo_table.at[64:128], halo_in.at[0], node_send.at[0], node_recv.at[0], place.partition(1))
        extra["down"] = go(halo_table.at[0:64], halo_in.at[1], node_send.at[1], node_recv.at[1], place.partition(63))
        sum_copy.wait_recv()
        sums_ring(0, sums[...] + sum_core[0])

    def extra_b():
        own_table[...] += dot(pick_dst[...], input_grads(2).astype(BF16))

    def extra_c():
        grad_edge[...] = (input_grads(0) + up[...]).astype(BF16)

    def extra_d():
        extra["up"].wait_recv()
        extra["down"].wait_recv()
        value = own_table[...]
        for side in (0, 1):
            picks = (lax.broadcasted_iota(jnp.int32, (256, 64), 0) == send_ref[side : side + 1, :]).astype(F32)
            there = (dom < 63) if side == 1 else (dom > 0)
            picks = jnp.where(there, picks, 0.0).astype(BF16)
            value = value + dot(picks, halo_in[side])
        own_table[...] = value
        node_out[...] = jnp.where(hid == 0, value[:, 256:512], value[:, 0:256]).astype(BF16)
        extra["swap"] = go(node_out, node_in, node_send.at[2], node_recv.at[2], (dom, 1 - hid))
        sums_ring(1, ring_sum(0))

    def extra_e():
        sums_ring(2, ring_sum(1))

    def extra_f():
        extra["swap"].wait_recv()
        keep = jnp.where(hid == 0, own_table[:, 0:256], own_table[:, 256:512])
        grad_node[...] = (keep + node_in[...].astype(F32)).astype(BF16)
        summed[...] = ring_sum(2) * (1.0 / 1024)

    extra = {}
    writes = []

    def write(chunk):
        block = 2 * chunk + core
        copy = pltpu.make_async_copy(total.at[block], total_hbm.at[block], write_sem.at[chunk])
        copy.start()
        writes.append(copy)

    def stage(name, chunk):
        if name == "A":
            reduce.add_core(chunk)
        elif name == "F":
            reduce.add_first(chunk)
        elif name == "S":
            reduce.add_second(chunk)
        elif name == "T":
            value = reduce.add_third(chunk) * (1.0 / 1024)
            rows = pl.ds(pl.multiple_of(16 * first_tile(place, chunk), 16), 16 * tiles_known(chunk))
            total[2 * chunk + core, rows, :] = value.astype(BF16)
            gather.start(chunk, 0)
        elif name == "G":
            gather.arrived(chunk, 0)
            gather.start(chunk, 1)
        else:
            gather.arrived(chunk, 1)
            gather.start(chunk, 2)
            write(chunk)

    work = {"a": extra_a, "b": extra_b, "c": extra_c, "d": extra_d, "e": extra_e, "f": extra_f}
    for name, item in ORDER:
        if name == "X":
            work[item]()
        elif name == "P":
            produce(int(item))
        else:
            stage(name, int(item))
    for chunk in range(CHUNKS):
        gather.arrived(chunk, 2)
    spread.sent()
    reduce.sent()
    gather.sent()
    for copy in flying:
        copy.wait_send()
    for copy in writes:
        copy.wait()


def finish_kernel(
    total, edge_in, node_in, summed, w_out, w_in, bias, vectors, grad_edge, grad_node, raw, wide, read_sem, write_sem
):
    hid = lax.axis_index("hid")
    moves = [
        pltpu.make_async_copy(total.at[block], raw.at[block], read_sem.at[block]) for block in range(12)
    ]
    for copy in moves:
        copy.start()
    grad_edge[...] = edge_in[...]
    grad_node[...] = node_in[...]
    for i in range(3):
        vectors[i : i + 1, 0:256] = summed[6 + 2 * i : 7 + 2 * i, :]
        vectors[i : i + 1, 256:512] = summed[7 + 2 * i : 8 + 2 * i, :]
    picked = jnp.where(hid == 0, summed[0:3, :], summed[3:6, :])
    for j in range(3):
        for k in range(2):
            bias[2 * j + k : 2 * j + k + 1, :] = picked[j : j + 1, 128 * k : 128 * k + 128]
    writes = []
    for block in range(12):
        moves[block].wait()

        def part(i, _):
            rows = pl.ds(pl.multiple_of(i * 128, 128), 128)
            wide[block, rows, :] = raw[block, rows, :].astype(F32)
            return 0

        lax.fori_loop(0, 4, part, 0)
        if block < 2:
            parts = [(wide.at[block], w_out.at[0:512, 256 * block : 256 * block + 256])]
        elif block == 2:
            parts = [
                (wide.at[2, 0:256], w_out.at[512:768, 0:256]),
                (wide.at[2, 256:512], w_out.at[512:768, 256:512]),
            ]
        else:
            r, j = (block - 3) % 3, (block - 3) // 3
            parts = [(wide.at[block], w_in.at[512 * r : 512 * r + 512, 256 * j : 256 * j + 256])]
        for src, dst in parts:
            copy = pltpu.make_async_copy(src, dst, write_sem.at[len(writes)])
            copy.start()
            writes.append(copy)
    for copy in writes:
        copy.wait()


def vmem():
    return pl.BlockSpec(memory_space=pltpu.VMEM)


def smem():
    return pl.BlockSpec(memory_space=pltpu.SMEM)


def anywhere():
    return pl.BlockSpec(memory_space=pl.ANY)


def shape(dims, dtype):
    return jax.ShapeDtypeStruct(dims, dtype)


def dma(*dims):
    return pltpu.SemaphoreType.DMA(dims)


def per_device(
    node_latent,
    edge_latent,
    send_rows,
    edge_src,
    edge_dst,
    edge_live,
    w_in_blocks,
    w_in_scale,
    bias_in,
    w_out_blocks,
    w_out_scale,
    bias_out,
    norm_gain,
    grad_edge,
    grad_agg,
):
    total, edge_in, node_in, summed = pl.pallas_call(
        main_kernel,
        out_shape=(
            shape((12, 512, 256), BF16),
            shape((512, 512), BF16),
            shape((256, 256), BF16),
            shape((16, 256), F32),
        ),
        in_specs=[
            anywhere(),
            anywhere(),
            vmem(),
            vmem(),
            vmem(),
            smem(),
            anywhere(),
            smem(),
            vmem(),
            anywhere(),
            smem(),
            vmem(),
            vmem(),
            anywhere(),
            anywhere(),
        ],
        out_specs=(anywhere(), vmem(), vmem(), vmem()),
        scratch_shapes=[
            pltpu.VMEM((256, 512), BF16),
            pltpu.VMEM((1536, 768), BF16),
            pltpu.VMEM((768, 512), BF16),
            pltpu.VMEM((256, 512), BF16),
            pltpu.VMEM((512, 512), BF16),
            pltpu.VMEM((2, 12, 512, 256), BF16),
            pltpu.VMEM((2, 8, 256), F32),
            pltpu.VMEM((2, 64, 512), BF16),
            pltpu.VMEM((2, 64, 512), BF16),
            pltpu.VMEM((5, 64, 256), BF16),
            pltpu.VMEM((3, 512, 512), BF16),
            pltpu.VMEM((3, 512, 512), BF16),
            pltpu.VMEM((384, 512), BF16),
            pltpu.VMEM((384, 512), BF16),
            pltpu.VMEM((256, 512), BF16),
            pltpu.VMEM((6, 512, 256), BF16),
            pltpu.VMEM((6, 512, 256), F32),
            pltpu.VMEM((512, 512), F32),
            pltpu.VMEM((512, 512), F32),
            pltpu.VMEM((512, 512), BF16),
            pltpu.VMEM((6, 512, 256), BF16),
            pltpu.VMEM((12, 1024, 256), BF16),
            pltpu.VMEM((6, 1024, 256), BF16),
            pltpu.VMEM((6, 3, 256, 256), BF16),
            pltpu.VMEM((6, 256, 256), BF16),
            pltpu.VMEM((6, 3, 64, 256), BF16),
            pltpu.VMEM((6, 64, 256), BF16),
            pltpu.VMEM((6, 4, 64, 256), BF16),
            pltpu.VMEM((12, 512, 256), BF16),
            pltpu.VMEM((16, 256), F32),
            pltpu.VMEM((1, 16, 256), F32),
            pltpu.VMEM((3, 4, 16, 256), F32),
            pltpu.VMEM((256, 512), F32),
            pltpu.VMEM((128, 512), BF16),
            pltpu.VMEM((2, 64, 512), BF16),
            pltpu.VMEM((256, 256), BF16),
            pltpu.VMEM((256, 256), BF16),
            dma(6),
            dma(6, 8),
            dma(6, 8),
            dma(7),
            dma(7),
            dma(2),
            dma(2),
            dma(6, 10),
            dma(6, 10),
            dma(6, 8),
            dma(6, 8),
            dma(4, 4),
            dma(4, 4),
            dma(3),
            dma(3),
            dma(6),
        ],
        compiler_params=pltpu.CompilerParams(
            collective_id=0, has_side_effects=True, vmem_limit_bytes=LIMIT
        ),
        name="message_grads",
    )(
        node_latent,
        edge_latent,
        send_rows[0],
        edge_src.reshape(8, 128),
        edge_dst.reshape(8, 128),
        edge_live,
        w_in_blocks,
        w_in_scale.T,
        bias_in.reshape(6, 128),
        w_out_blocks,
        w_out_scale.T,
        bias_out.reshape(1, 512),
        norm_gain.reshape(1, 512),
        grad_edge,
        grad_agg,
    )
    grad_w_out, grad_w_in, grad_bias, vectors, grad_edge_in, grad_node = pl.pallas_call(
        finish_kernel,
        out_shape=(
            shape((768, 512), F32),
            shape((1536, 768), F32),
            shape((6, 128), F32),
            shape((3, 512), F32),
            shape((512, 512), BF16),
            shape((256, 256), BF16),
        ),
        in_specs=[anywhere(), vmem(), vmem(), vmem()],
        out_specs=(anywhere(), anywhere(), vmem(), vmem(), vmem(), vmem()),
        scratch_shapes=[
            pltpu.VMEM((12, 512, 256), BF16),
            pltpu.VMEM((12, 512, 256), F32),
            dma(12),
            dma(13),
        ],
        compiler_params=pltpu.CompilerParams(vmem_limit_bytes=LIMIT),
        name="widen_grads",
    )(total, edge_in, node_in, summed)
    return (grad_edge_in, grad_node, grad_w_in, grad_bias.reshape(768), grad_w_out, vectors)


def solution(mesh):
    in_specs = (
        P("dom", None),
        P("dom", None),
        P("dom", None, None),
        P("dom"),
        P("dom"),
        P("dom"),
        P(None, "hid"),
        P(None, "hid"),
        P("hid"),
        P("hid", None),
        P("hid", None),
        P(),
        P(),
        P("dom", None),
        P("dom", None),
    )
    out_specs = (
        P(("dom", "hid"), None),
        P("dom", "hid"),
        P(None, "hid"),
        P("hid"),
        P("hid", None),
        P(),
    )
    return jax.shard_map(
        per_device, mesh=mesh, in_specs=in_specs, out_specs=out_specs, check_vma=False
    )
```

```python
import jax
import jax.numpy as jnp
from jax import lax
from jax.experimental import pallas as pl
from jax.experimental.pallas import tpu as pltpu
from jax.sharding import PartitionSpec as P

EPS = 1e-05
MESH = pl.DeviceIdType.MESH
F32 = jnp.float32
BF16 = jnp.bfloat16
CHUNKS = 6
LIMIT = 60 << 20


class Place:
    def __init__(self):
        dom = lax.axis_index("dom")
        self.hid = lax.axis_index("hid")
        self.dom = dom
        self.z = lax.div(dom, 16)
        self.x = lax.rem(lax.div(dom, 4), 4)
        self.yl = lax.rem(lax.div(dom, 2), 2)
        self.y = 2 * self.hid + self.yl
        self.core = lax.rem(dom, 2)

    def at(self, z=None, x=None, y=None, core=None):
        z = self.z if z is None else z
        x = self.x if x is None else x
        y = self.y if y is None else y
        core = self.core if core is None else core
        return (((z * 4 + x) * 2 + lax.rem(y, 2)) * 2 + core, lax.div(y, 2))

    def ring(self, axis, step):
        return self.at(**{axis: lax.rem(getattr(self, axis) + step, 4)})

    def other_core(self):
        return self.at(core=1 - self.core)

    def cross(self):
        return self.at(y=3 - self.y)

    def pair(self):
        return self.at(y=self.y + 1 - 2 * self.yl)

    def partition(self, step):
        return (lax.rem(self.dom + step, 64), self.hid)


def greet(partners):
    barrier = pltpu.get_barrier_semaphore()
    for partner in partners:
        pl.semaphore_signal(barrier, inc=1, device_id=partner, device_id_type=MESH)
    return lambda: pl.semaphore_wait(barrier, len(partners))


def remote(src, dst, send_sem, recv_sem, target):
    return pltpu.make_async_remote_copy(
        src_ref=src,
        dst_ref=dst,
        send_sem=send_sem,
        recv_sem=recv_sem,
        device_id=target,
        device_id_type=MESH,
    )


AXES = (
    ("z", "x", "y"),
    ("x", "z", "y"),
    ("y", "z", "x"),
    ("z", "x", "y"),
    ("x", "z", "y"),
    ("y", "x", "z"),
)


def tiles_known(chunk):
    return 2 if AXES[chunk][2] == "y" else 4


def first_tile(place, chunk, yl=None):
    yl = place.yl if yl is None else yl
    a, b, _ = AXES[chunk]
    if a == "y":
        return (yl * 4 + getattr(place, b)) * 4
    return (getattr(place, a) * 4 + getattr(place, b)) * 2


def rows_of(first, count, unit=16):
    return pl.ds(pl.multiple_of(first * unit, unit), count * unit)


def gather_steps(place, chunk):
    a, b, _ = AXES[chunk]
    ring = [place.ring(b, j) for j in (2, 1, 3)]
    known = tiles_known(chunk)
    if a == "y":
        last = (place.yl * 16, 16, [place.pair()])
    else:
        last = (getattr(place, a) * 8, 8, [place.ring(a, j) for j in (2, 1, 3)])
    return [(first_tile(place, chunk), known, ring), last]


class Gather:
    def __init__(self, place, buf, send_sem, recv_sem, result):
        self.place, self.buf, self.result = place, buf, result
        self.send_sem, self.recv_sem = send_sem, recv_sem
        self.steps = {}
        self.flying = {}

    def start(self, chunk, step):
        place = self.place
        if chunk not in self.steps:
            self.steps[chunk] = gather_steps(place, chunk)
        halved = AXES[chunk][0] == "y"
        if step == 2:
            first, count = ((1 - place.yl) * 16, 16) if halved else (0, 32)
            self.send(chunk, 2, first, count, 6, place.other_core())
            return
        first, count, targets = self.steps[chunk][step]
        for j, target in enumerate(targets):
            self.send(chunk, step, first, count, 3 * step + j, target)
        if step == 1 and halved:
            self.send(chunk, 2, first, count, 7, place.other_core())

    def send(self, chunk, step, first, count, index, target):
        block = 2 * chunk + self.place.core
        part = self.buf.at[block, rows_of(first, count)]
        goal = self.result.at[block, rows_of(first, count)] if step == 2 else part
        copy = remote(part, goal, self.send_sem.at[chunk, index], self.recv_sem.at[chunk, index], target)
        copy.start()
        self.flying.setdefault((chunk, step), []).append(copy)

    def arrived(self, chunk, step):
        for copy in self.flying[chunk, step]:
            copy.wait_recv()

    def sent(self):
        for copies in self.flying.values():
            for copy in copies:
                copy.wait_send()


RING = (2, 1, 3)
GATHERED = (3, 4, 2, 1, 5)
DIRECT = (0,)


def tdot(a, b):
    return lax.dot_general(a, b, (((0,), (0,)), ((), ())), preferred_element_type=F32)


def ndot(a, b):
    return lax.dot_general(a, b, (((1,), (1,)), ((), ())), preferred_element_type=F32)


def dot(a, b):
    return jnp.dot(a, b, preferred_element_type=F32)


def dequantize_out(own, w_out_ref, scales):
    for a in range(6):
        for b in range(4):
            value = w_out_ref[128 * a : 128 * a + 128, 128 * b : 128 * b + 128].astype(F32) * scales[b, a]
            if a < 4:
                index, row = b // 2, 128 * a
            else:
                index, row = 2, 128 * (a - 4) + 256 * (b // 2)
            col = 128 * (b % 2)
            own[index, row : row + 128, col : col + 128] = value.astype(BF16)


def dequantize_in(own, w_in_ref, scales, first, last):
    def block(index, _):
        j = lax.div(index, 3)
        r = lax.rem(index, 3)
        for a in range(4):
            for b in range(2):
                scale = scales[2 * j + b, 4 * r + a]
                rows = pl.ds(pl.multiple_of(512 * r + 128 * a, 128), 128)
                cols = pl.ds(pl.multiple_of(256 * j + 128 * b, 128), 128)
                value = w_in_ref[rows, cols].astype(F32) * scale
                own[3 + index, 128 * a : 128 * a + 128, 128 * b : 128 * b + 128] = value.astype(BF16)
        return 0

    lax.fori_loop(first, last, block, 0)


def dequantize_tiles(tile, w_in_ref, scales, index, q, count):
    j = lax.div(index, 3)
    r = lax.rem(index, 3)
    rows = pl.ds(pl.multiple_of(512 * r + 16 * q, 16), 16 * count)
    for b in range(2):
        scale = scales[2 * j + b, 4 * r + lax.div(q, 8)]
        cols = pl.ds(pl.multiple_of(256 * j + 128 * b, 128), 128)
        tile[0 : 16 * count, 128 * b : 128 * b + 128] = (w_in_ref[rows, cols].astype(F32) * scale).astype(BF16)


def dequantize_out_tiles(tile, w_out_ref, scales, q, wanted):
    side = lax.div(q, 16)
    row = lax.rem(q, 16)
    rows = pl.ds(pl.multiple_of(512 + 16 * row, 16), 32)
    for b in range(2):
        scale = scales[2 * side + b, 4 + lax.div(row, 8)]
        cols = pl.ds(pl.multiple_of(256 * side + 128 * b, 128), 128)
        value = w_out_ref[rows, cols].astype(F32) * scale
        kept = tile[0:32, 128 * b : 128 * b + 128].astype(F32)
        tile[0:32, 128 * b : 128 * b + 128] = jnp.where(wanted, value, kept).astype(BF16)


def place_rows(grads, block, first, value, half):
    count = value.shape[0]
    group = 512 if AXES[block // 2][0] == "y" else 32
    size = min(group, count)
    for at in range(0, count, size):
        row = first + at
        base = (row // group) * 2 * group + row % group
        grads[block, pl.ds(pl.multiple_of(base + group * half, 32), size), :] = value[at : at + size]


ORDER = (
    "P1", "A0", "P2", "A1", "P3", "A2", "P4", "A3", "P5", "A4", "A5", "F0",
    "Xa", "F1", "F2", "F3", "Xb", "S0", "F4", "S1", "F5", "S2", "S3", "Xd",
    "T0", "S4", "T1", "S5", "T2", "Xe", "T3", "T4", "T5", "G0", "G1", "G2",
    "G3", "Xc", "G4", "G5", "Xf", "L0", "L1", "L2", "L3", "L4", "L5",
)


class Reduce:
    def __init__(self, place, grads, core_in, first_in, first_out, second_in, second_out, third_in, send_sem, recv_sem):
        self.place, self.grads, self.core_in = place, grads, core_in
        self.first_in, self.first_out = first_in, first_out
        self.second_in, self.second_out, self.third_in = second_in, second_out, third_in
        self.send_sem, self.recv_sem = send_sem, recv_sem
        self.flying = {}

    def send(self, chunk, stage, index, src, dst, target):
        copy = remote(src, dst, self.send_sem.at[chunk, index], self.recv_sem.at[chunk, index], target)
        copy.start()
        self.flying.setdefault((chunk, stage), []).append(copy)

    def arrived(self, chunk, stage):
        for copy in self.flying[chunk, stage]:
            copy.wait_recv()

    def sent(self):
        for copies in self.flying.values():
            for copy in copies:
                copy.wait_send()

    def share(self, chunk):
        core = self.place.core
        src = self.grads.at[2 * chunk + 1 - core]
        self.send(chunk, 0, 0, src, self.core_in.at[chunk], self.place.other_core())

    def spread(self, chunk, level, src, dst, unit):
        axis = AXES[chunk][level]
        mine = getattr(self.place, axis)
        for j in RING:
            at = lax.rem(mine + j, 4)
            part = src.at[rows_of(at, 1, unit)]
            self.send(chunk, level + 1, 3 * level + j, part, dst.at[j - 1], self.place.ring(axis, j))

    def kept(self, chunk, level, src, unit):
        mine = getattr(self.place, AXES[chunk][level])
        return src[rows_of(mine, 1, unit), :].astype(F32)

    def add_core(self, chunk):
        self.arrived(chunk, 0)
        block = 2 * chunk + self.place.core

        def part(i, _):
            rows = pl.ds(pl.multiple_of(i * 128, 128), 128)
            self.grads[block, rows, :] = self.grads[block, rows, :] + self.core_in[chunk, rows, :]
            return 0

        lax.fori_loop(0, 8, part, 0)
        self.spread(chunk, 0, self.grads.at[block], self.first_in.at[chunk], 256)

    def add_first(self, chunk):
        self.arrived(chunk, 1)
        value = self.kept(chunk, 0, self.grads.at[2 * chunk + self.place.core], 256)
        for j in range(3):
            value = value + self.first_in[chunk, j].astype(F32)
        self.first_out[chunk] = value.astype(BF16)
        self.spread(chunk, 1, self.first_out.at[chunk], self.second_in.at[chunk], 64)

    def add_second(self, chunk):
        self.arrived(chunk, 2)
        value = self.kept(chunk, 1, self.first_out.at[chunk], 64)
        for j in range(3):
            value = value + self.second_in[chunk, j].astype(F32)
        self.second_out[chunk] = value.astype(BF16)
        axis = AXES[chunk][2]
        mine = getattr(self.place, axis)
        rows = 16 * tiles_known(chunk)
        if axis == "y":
            self.third_in[chunk, mine, 0:rows, :] = self.second_out[chunk, rows_of(self.place.hid, 1, 32), :]
        else:
            self.third_in[chunk, mine] = self.second_out[chunk]
        for j in RING:
            if axis == "y":
                half = lax.div(lax.rem(mine + j, 4), 2)
                part = self.second_out.at[chunk, rows_of(half, 1, 32)]
            else:
                part = self.second_out.at[chunk]
            goal = self.third_in.at[chunk, mine, pl.ds(0, rows)]
            self.send(chunk, 3, 6 + j, part, goal, self.place.ring(axis, j))

    def add_third(self, chunk):
        self.arrived(chunk, 3)
        rows = 16 * tiles_known(chunk)
        value = self.third_in[chunk, 0, 0:rows, :].astype(F32)
        for at in range(1, 4):
            value = value + self.third_in[chunk, at, 0:rows, :].astype(F32)
        return value


def main_kernel(
    node_hbm,
    edge_hbm,
    send_ref,
    src_ref,
    dst_ref,
    live_ref,
    w_in_hbm,
    w_in_scale,
    bias_ref,
    w_out_hbm,
    w_out_scale,
    bias_out_ref,
    gain_ref,
    gedge_hbm,
    gagg_hbm,
    total_hbm,
    grad_edge,
    grad_node,
    summed,
    node,
    w_in,
    w_out,
    gagg,
    gedge,
    weights,
    bias,
    halo,
    halo_out,
    tiles,
    inp,
    inpt,
    ext,
    pick_src,
    pick_dst,
    act,
    slope,
    up,
    msg,
    low,
    pre_low,
    grads,
    core_in,
    first_in,
    first_out,
    second_in,
    second_out,
    third_in,
    total,
    sums,
    sum_core,
    sum_ring,
    own_table,
    halo_table,
    halo_in,
    node_out,
    node_in,
    third_vector,
    act_turned,
    local_sem,
    spread_send,
    spread_recv,
    cross_send,
    cross_recv,
    halo_send,
    halo_recv,
    reduce_send,
    reduce_recv,
    gather_send,
    gather_recv,
    sum_send,
    sum_recv,
    node_send,
    node_recv,
    write_sem,
):
    place = Place()
    hid, dom, core = place.hid, place.dom, place.core
    first_edge = pl.multiple_of(hid * 512, 512)

    def fetch(index, src, dst):
        copy = pltpu.make_async_copy(src, dst, local_sem.at[index])
        copy.start()
        return copy

    get_w_in = fetch(1, w_in_hbm, w_in)
    get_w_out = fetch(0, w_out_hbm, w_out)
    get_node = fetch(2, node_hbm, node)
    get_edge = fetch(3, edge_hbm.at[pl.ds(first_edge, 512)], inp.at[0])
    get_agg = fetch(4, gagg_hbm, gagg)
    get_cot = fetch(5, gedge_hbm.at[pl.ds(first_edge, 512)], gedge)
    partners = [place.ring(axis, j) for axis in "zxy" for j in RING]
    partners += [place.other_core(), place.cross(), place.partition(1), place.partition(63)]
    all_here = greet(partners)
    flying = []

    def go(src, dst, send_sem, recv_sem, target):
        copy = remote(src, dst, send_sem, recv_sem, target)
        copy.start()
        flying.append(copy)
        return copy

    own, other = weights.at[0], weights.at[1]
    bias[0] = jnp.zeros((8, 256), F32)
    for j in range(3):
        bias[0, j : j + 1, 0:128] = bias_ref[2 * j : 2 * j + 1, :]
        bias[0, j : j + 1, 128:256] = bias_ref[2 * j + 1 : 2 * j + 2, :]
    for k in range(4):
        cols = slice(128 * k, 128 * k + 128)
        src_row = src_ref[pl.ds(4 * hid + k, 1), :]
        dst_row = dst_ref[pl.ds(4 * hid + k, 1), :]
        pick_src[:, cols] = (lax.broadcasted_iota(jnp.int32, (384, 128), 0) == src_row).astype(F32).astype(BF16)
        pick_dst[:, cols] = (lax.broadcasted_iota(jnp.int32, (256, 128), 0) == dst_row).astype(F32).astype(BF16)
    get_node.wait()
    for side in (0, 1):
        picks = (lax.broadcasted_iota(jnp.int32, (256, 64), 0) == send_ref[side : side + 1, :]).astype(F32)
        halo_out[side] = tdot(picks.astype(BF16), node[...]).astype(BF16)
    get_w_in.wait()
    tile_at = {}
    for chunk in GATHERED:
        known = tiles_known(chunk)
        index = 2 * chunk + core - 3
        if chunk == 1:
            index = 0
        tile_at[chunk] = first_tile(place, chunk, 1 - place.yl)
        dequantize_tiles(tiles.at[chunk - 1], w_in, w_in_scale, index, tile_at[chunk], known)
    get_w_out.wait()
    dequantize_out_tiles(tiles.at[0], w_out, w_out_scale, tile_at[1], core == 0)
    all_here()
    crossing = {}

    def cross(chunk, src, dst):
        crossing[chunk] = go(src, dst, cross_send.at[chunk], cross_recv.at[chunk], place.cross())

    for chunk in GATHERED:
        rows = 16 * tiles_known(chunk)
        goal = other.at[2 * chunk + core, pl.ds(pl.multiple_of(16 * tile_at[chunk], 16), rows)]
        cross(chunk, tiles.at[chunk - 1, pl.ds(0, rows)], goal)
    up_rows = go(halo_out.at[1], halo.at[0], halo_send.at[0], halo_recv.at[0], place.partition(1))
    down_rows = go(halo_out.at[0], halo.at[1], halo_send.at[1], halo_recv.at[1], place.partition(63))
    bias_copy = go(bias.at[0], bias.at[1], cross_send.at[6], cross_recv.at[6], place.cross())
    dequantize_out(own, w_out, w_out_scale)
    dequantize_in(own, w_in, w_in_scale, 0, 1)
    for chunk in DIRECT:
        cross(chunk, own.at[2 * chunk + core], other.at[2 * chunk + core])
    spread = Gather(place, other, spread_send, spread_recv, other)
    for chunk in GATHERED:
        crossing[chunk].wait_recv()
        spread.start(chunk, 0)
    dequantize_in(own, w_in, w_in_scale, 1, 9)
    inp[2] = tdot(pick_dst[...], node[...]).astype(BF16)
    get_agg.wait()
    up[...] = tdot(pick_dst[...], gagg[...])
    ext[0:256] = node[...]
    for chunk in GATHERED:
        spread.arrived(chunk, 0)
        spread.start(chunk, 1)
    up_rows.wait_recv()
    down_rows.wait_recv()
    ext[256:320] = jnp.where(dom > 0, halo[0], jnp.zeros((64, 512), BF16))
    ext[320:384] = jnp.where(dom < 63, halo[1], jnp.zeros((64, 512), BF16))
    inp[1] = tdot(pick_src[...], ext[...]).astype(BF16)
    get_edge.wait()

    live = live_ref[0] - hid * 512

    def fold(value):
        return jnp.sum(value.reshape(8, 8, 512), axis=0)

    def mask_upstream(i, carry):
        rows = pl.ds(pl.multiple_of(i * 64, 64), 64)
        mask = (lax.broadcasted_iota(jnp.int32, (64, 512), 0) + i * 64) < live
        upstream = jnp.where(mask, gedge[rows, :].astype(F32) + up[rows, :], 0.0)
        up[rows, :] = upstream
        return carry + fold(upstream)

    def message_part(slot, side):
        result = dot(act[3 * slot + 2], weights[slot, 2, 256 * side : 256 * side + 256, :])
        for j in range(2):
            result = result + dot(act[3 * slot + j], weights[slot, side, 256 * j : 256 * j + 256, :])
        return result

    def prepare():
        for side in range(2):
            cols = slice(256 * side, 256 * side + 256)
            msg[:, cols] = bias_out_ref[:, cols] + message_part(0, side)
        get_cot.wait()
        third_vector[...] = lax.fori_loop(0, 8, mask_upstream, jnp.zeros((8, 512), F32))
        for j in range(3):
            act_turned[j] = act[j].T

    def forward(slot, j):
        pre = bias[slot, pl.ds(j, 1), :]
        for r in range(3):
            pre = pre + dot(inp[r], weights[slot, 3 + 3 * j + r])
        sigma = 1.0 / (1.0 + jnp.exp(-pre))
        value = pre * sigma
        act[3 * slot + j] = value.astype(BF16)
        slope[3 * slot + j] = sigma + value * (1.0 - sigma)

    def forward_own(j, _):
        forward(0, j)
        return 0

    lax.fori_loop(0, 3, forward_own, 0)
    for chunk in DIRECT:
        crossing[chunk].wait_recv()
        spread.start(chunk, 2)
    for chunk in GATHERED:
        spread.arrived(chunk, 1)
        spread.start(chunk, 2)
    for r in range(3):
        inpt[r] = inp[r].T
    prepare()
    bias_copy.wait_recv()
    for chunk in (3, 4):
        spread.arrived(chunk, 2)
    forward(1, 1)
    for chunk in (1, 2):
        spread.arrived(chunk, 2)
    forward(1, 0)
    spread.arrived(5, 2)
    forward(1, 2)
    spread.arrived(0, 2)

    for side in range(2):
        cols = slice(256 * side, 256 * side + 256)
        msg[:, cols] = msg[:, cols] + message_part(1, side)

    gain = gain_ref[...]

    def norm(i, carry):
        rows = pl.ds(pl.multiple_of(i * 64, 64), 64)
        upstream = up[rows, :]
        message = msg[rows, :]
        centre = message - jnp.mean(message, axis=1, keepdims=True)
        inverse = lax.rsqrt(jnp.mean(centre * centre, axis=1, keepdims=True) + EPS)
        normed = centre * inverse
        scaled = upstream * gain
        shift = jnp.mean(scaled, axis=1, keepdims=True)
        tilt = jnp.mean(scaled * normed, axis=1, keepdims=True)
        grad = inverse * (scaled - shift - normed * tilt)
        low[rows, :] = grad.astype(BF16)
        return (carry[0] + fold(grad), carry[1] + fold(upstream * normed))

    zero = jnp.zeros((8, 512), F32)
    vectors = lax.fori_loop(0, 8, norm, (zero, zero))
    vectors = (*vectors, third_vector[...])
    sums[...] = jnp.zeros((16, 256), F32)
    for i in range(3):
        row = jnp.sum(vectors[i], axis=0, keepdims=True)
        sums[6 + 2 * i : 7 + 2 * i, :] = row[:, 0:256]
        sums[7 + 2 * i : 8 + 2 * i, :] = row[:, 256:512]

    reduce = Reduce(
        place, grads, core_in, first_in, first_out, second_in, second_out, third_in, reduce_send, reduce_recv
    )
    gather = Gather(place, total, gather_send, gather_recv, total_hbm)
    halves = (hid, 1 - hid)
    for slot in range(2):
        for j in range(3):
            if slot == 0:
                part = dot(act_turned[j], low[...]).astype(BF16)
            else:
                part = tdot(act[3 + j], low[...]).astype(BF16)
            if j < 2:
                place_rows(grads, 0, 256 * j, part[:, 0:256], halves[slot])
                place_rows(grads, 1, 256 * j, part[:, 256:512], halves[slot])
            else:
                place_rows(grads, 2, 0, part[:, 0:256], halves[slot])
                place_rows(grads, 2, 256, part[:, 256:512], halves[slot])
    reduce.share(0)
    for slot in range(2):
        for j in range(3):
            if j < 2:
                rows = slice(256 * j, 256 * j + 256)
                grad = ndot(low[:, 0:256], weights[slot, 0, rows, :])
                grad = grad + ndot(low[:, 256:512], weights[slot, 1, rows, :])
            else:
                grad = ndot(low[:, 0:256], weights[slot, 2, 0:256, :])
                grad = grad + ndot(low[:, 256:512], weights[slot, 2, 256:512, :])
            grad = grad * slope[3 * slot + j]
            sums[pl.ds(3 * halves[slot] + j, 1), :] = jnp.sum(grad, axis=0, keepdims=True)
            pre_low[3 * slot + j] = grad.astype(BF16)
    sum_copy = go(sums, sum_core.at[0], sum_send.at[0, 0], sum_recv.at[0, 0], place.other_core())

    def first_layer(m):
        for slot in range(2):
            part = dot(inpt[m % 3], pre_low[3 * slot + m // 3]).astype(BF16)
            place_rows(grads, 3 + m, 0, part, halves[slot])

    def produce(chunk):
        if chunk > 1:
            first_layer(2 * chunk - 3)
        first_layer(2 * chunk - 2)
        reduce.share(chunk)

    def input_grads(r):
        result = jnp.zeros((512, 512), F32)
        for slot in range(2):
            for j in range(3):
                result = result + ndot(pre_low[3 * slot + j], weights[slot, 3 + 3 * j + r])
        return result

    ring_copies = []

    def sums_ring(level, value):
        axis = "zxy"[level]
        mine = getattr(place, axis)
        sum_ring[level, mine] = value
        ring_copies.clear()
        for j in RING:
            part = sum_ring.at[level, mine]
            ring_copies.append(
                go(part, part, sum_send.at[1 + level, j], sum_recv.at[1 + level, j], place.ring(axis, j))
            )

    def ring_sum(level):
        for copy in ring_copies:
            copy.wait_recv()
        return sum_ring[level, 0] + sum_ring[level, 1] + sum_ring[level, 2] + sum_ring[level, 3]

    def extra_a():
        table = dot(pick_src[...], input_grads(1).astype(BF16))
        own_table[...] = table[0:256]
        halo_table[...] = table[256:384].astype(BF16)
        extra["up"] = go(halo_table.at[64:128], halo_in.at[0], node_send.at[0], node_recv.at[0], place.partition(1))
        extra["down"] = go(halo_table.at[0:64], halo_in.at[1], node_send.at[1], node_recv.at[1], place.partition(63))
        sum_copy.wait_recv()
        sums_ring(0, sums[...] + sum_core[0])

    def extra_b():
        own_table[...] += dot(pick_dst[...], input_grads(2).astype(BF16))

    def extra_c():
        grad_edge[...] = (input_grads(0) + up[...]).astype(BF16)

    def extra_d():
        extra["up"].wait_recv()
        extra["down"].wait_recv()
        value = own_table[...]
        for side in (0, 1):
            picks = (lax.broadcasted_iota(jnp.int32, (256, 64), 0) == send_ref[side : side + 1, :]).astype(F32)
            there = (dom < 63) if side == 1 else (dom > 0)
            picks = jnp.where(there, picks, 0.0).astype(BF16)
            value = value + dot(picks, halo_in[side])
        own_table[...] = value
        node_out[...] = jnp.where(hid == 0, value[:, 256:512], value[:, 0:256]).astype(BF16)
        extra["swap"] = go(node_out, node_in, node_send.at[2], node_recv.at[2], (dom, 1 - hid))
        sums_ring(1, ring_sum(0))

    def extra_e():
        sums_ring(2, ring_sum(1))

    def extra_f():
        extra["swap"].wait_recv()
        keep = jnp.where(hid == 0, own_table[:, 0:256], own_table[:, 256:512])
        grad_node[...] = (keep + node_in[...].astype(F32)).astype(BF16)
        summed[...] = ring_sum(2) * (1.0 / 1024)

    extra = {}
    writes = []

    def write(chunk):
        block = 2 * chunk + core
        copy = pltpu.make_async_copy(total.at[block], total_hbm.at[block], write_sem.at[chunk])
        copy.start()
        writes.append(copy)

    def stage(name, chunk):
        if name == "A":
            reduce.add_core(chunk)
        elif name == "F":
            reduce.add_first(chunk)
        elif name == "S":
            reduce.add_second(chunk)
        elif name == "T":
            value = reduce.add_third(chunk) * (1.0 / 1024)
            rows = pl.ds(pl.multiple_of(16 * first_tile(place, chunk), 16), 16 * tiles_known(chunk))
            total[2 * chunk + core, rows, :] = value.astype(BF16)
            gather.start(chunk, 0)
        elif name == "G":
            gather.arrived(chunk, 0)
            gather.start(chunk, 1)
        else:
            gather.arrived(chunk, 1)
            gather.start(chunk, 2)
            write(chunk)

    work = {"a": extra_a, "b": extra_b, "c": extra_c, "d": extra_d, "e": extra_e, "f": extra_f}
    for name, item in ORDER:
        if name == "X":
            work[item]()
        elif name == "P":
            produce(int(item))
        else:
            stage(name, int(item))
    for chunk in range(CHUNKS):
        gather.arrived(chunk, 2)
    spread.sent()
    reduce.sent()
    gather.sent()
    for copy in flying:
        copy.wait_send()
    for copy in writes:
        copy.wait()


def finish_kernel(
    total, edge_in, node_in, summed, w_out, w_in, bias, vectors, grad_edge, grad_node, raw, wide, read_sem, write_sem
):
    hid = lax.axis_index("hid")
    moves = [
        pltpu.make_async_copy(total.at[block], raw.at[block], read_sem.at[block]) for block in range(12)
    ]
    for copy in moves:
        copy.start()
    grad_edge[...] = edge_in[...]
    grad_node[...] = node_in[...]
    for i in range(3):
        vectors[i : i + 1, 0:256] = summed[6 + 2 * i : 7 + 2 * i, :]
        vectors[i : i + 1, 256:512] = summed[7 + 2 * i : 8 + 2 * i, :]
    picked = jnp.where(hid == 0, summed[0:3, :], summed[3:6, :])
    for j in range(3):
        for k in range(2):
            bias[2 * j + k : 2 * j + k + 1, :] = picked[j : j + 1, 128 * k : 128 * k + 128]
    writes = []
    for block in range(12):
        moves[block].wait()

        def part(i, _):
            rows = pl.ds(pl.multiple_of(i * 128, 128), 128)
            wide[block, rows, :] = raw[block, rows, :].astype(F32)
            return 0

        lax.fori_loop(0, 4, part, 0)
        if block < 2:
            parts = [(wide.at[block], w_out.at[0:512, 256 * block : 256 * block + 256])]
        elif block == 2:
            parts = [
                (wide.at[2, 0:256], w_out.at[512:768, 0:256]),
                (wide.at[2, 256:512], w_out.at[512:768, 256:512]),
            ]
        else:
            r, j = (block - 3) % 3, (block - 3) // 3
            parts = [(wide.at[block], w_in.at[512 * r : 512 * r + 512, 256 * j : 256 * j + 256])]
        for src, dst in parts:
            copy = pltpu.make_async_copy(src, dst, write_sem.at[len(writes)])
            copy.start()
            writes.append(copy)
    for copy in writes:
        copy.wait()


def vmem():
    return pl.BlockSpec(memory_space=pltpu.VMEM)


def smem():
    return pl.BlockSpec(memory_space=pltpu.SMEM)


def anywhere():
    return pl.BlockSpec(memory_space=pl.ANY)


def shape(dims, dtype):
    return jax.ShapeDtypeStruct(dims, dtype)


def dma(*dims):
    return pltpu.SemaphoreType.DMA(dims)


def per_device(
    node_latent,
    edge_latent,
    send_rows,
    edge_src,
    edge_dst,
    edge_live,
    w_in_blocks,
    w_in_scale,
    bias_in,
    w_out_blocks,
    w_out_scale,
    bias_out,
    norm_gain,
    grad_edge,
    grad_agg,
):
    total, edge_in, node_in, summed = pl.pallas_call(
        main_kernel,
        out_shape=(
            shape((12, 512, 256), BF16),
            shape((512, 512), BF16),
            shape((256, 256), BF16),
            shape((16, 256), F32),
        ),
        in_specs=[
            anywhere(),
            anywhere(),
            vmem(),
            vmem(),
            vmem(),
            smem(),
            anywhere(),
            smem(),
            vmem(),
            anywhere(),
            smem(),
            vmem(),
            vmem(),
            anywhere(),
            anywhere(),
        ],
        out_specs=(anywhere(), vmem(), vmem(), vmem()),
        scratch_shapes=[
            pltpu.VMEM((256, 512), BF16),
            pltpu.VMEM((1536, 768), BF16),
            pltpu.VMEM((768, 512), BF16),
            pltpu.VMEM((256, 512), BF16),
            pltpu.VMEM((512, 512), BF16),
            pltpu.VMEM((2, 12, 512, 256), BF16),
            pltpu.VMEM((2, 8, 256), F32),
            pltpu.VMEM((2, 64, 512), BF16),
            pltpu.VMEM((2, 64, 512), BF16),
            pltpu.VMEM((5, 64, 256), BF16),
            pltpu.VMEM((3, 512, 512), BF16),
            pltpu.VMEM((3, 512, 512), BF16),
            pltpu.VMEM((384, 512), BF16),
            pltpu.VMEM((384, 512), BF16),
            pltpu.VMEM((256, 512), BF16),
            pltpu.VMEM((6, 512, 256), BF16),
            pltpu.VMEM((6, 512, 256), F32),
            pltpu.VMEM((512, 512), F32),
            pltpu.VMEM((512, 512), F32),
            pltpu.VMEM((512, 512), BF16),
            pltpu.VMEM((6, 512, 256), BF16),
            pltpu.VMEM((12, 1024, 256), BF16),
            pltpu.VMEM((6, 1024, 256), BF16),
            pltpu.VMEM((6, 3, 256, 256), BF16),
            pltpu.VMEM((6, 256, 256), BF16),
            pltpu.VMEM((6, 3, 64, 256), BF16),
            pltpu.VMEM((6, 64, 256), BF16),
            pltpu.VMEM((6, 4, 64, 256), BF16),
            pltpu.VMEM((12, 512, 256), BF16),
            pltpu.VMEM((16, 256), F32),
            pltpu.VMEM((1, 16, 256), F32),
            pltpu.VMEM((3, 4, 16, 256), F32),
            pltpu.VMEM((256, 512), F32),
            pltpu.VMEM((128, 512), BF16),
            pltpu.VMEM((2, 64, 512), BF16),
            pltpu.VMEM((256, 256), BF16),
            pltpu.VMEM((256, 256), BF16),
            pltpu.VMEM((8, 512), F32),
            pltpu.VMEM((3, 256, 512), BF16),
            dma(6),
            dma(6, 8),
            dma(6, 8),
            dma(7),
            dma(7),
            dma(2),
            dma(2),
            dma(6, 10),
            dma(6, 10),
            dma(6, 8),
            dma(6, 8),
            dma(4, 4),
            dma(4, 4),
            dma(3),
            dma(3),
            dma(6),
        ],
        compiler_params=pltpu.CompilerParams(
            collective_id=0, has_side_effects=True, vmem_limit_bytes=LIMIT
        ),
        name="message_grads",
    )(
        node_latent,
        edge_latent,
        send_rows[0],
        edge_src.reshape(8, 128),
        edge_dst.reshape(8, 128),
        edge_live,
        w_in_blocks,
        w_in_scale.T,
        bias_in.reshape(6, 128),
        w_out_blocks,
        w_out_scale.T,
        bias_out.reshape(1, 512),
        norm_gain.reshape(1, 512),
        grad_edge,
        grad_agg,
    )
    grad_w_out, grad_w_in, grad_bias, vectors, grad_edge_in, grad_node = pl.pallas_call(
        finish_kernel,
        out_shape=(
            shape((768, 512), F32),
            shape((1536, 768), F32),
            shape((6, 128), F32),
            shape((3, 512), F32),
            shape((512, 512), BF16),
            shape((256, 256), BF16),
        ),
        in_specs=[anywhere(), vmem(), vmem(), vmem()],
        out_specs=(anywhere(), anywhere(), vmem(), vmem(), vmem(), vmem()),
        scratch_shapes=[
            pltpu.VMEM((12, 512, 256), BF16),
            pltpu.VMEM((12, 512, 256), F32),
            dma(12),
            dma(13),
        ],
        compiler_params=pltpu.CompilerParams(vmem_limit_bytes=LIMIT),
        name="widen_grads",
    )(total, edge_in, node_in, summed)
    return (grad_edge_in, grad_node, grad_w_in, grad_bias.reshape(768), grad_w_out, vectors)


def solution(mesh):
    in_specs = (
        P("dom", None),
        P("dom", None),
        P("dom", None, None),
        P("dom"),
        P("dom"),
        P("dom"),
        P(None, "hid"),
        P(None, "hid"),
        P("hid"),
        P("hid", None),
        P("hid", None),
        P(),
        P(),
        P("dom", None),
        P("dom", None),
    )
    out_specs = (
        P(("dom", "hid"), None),
        P("dom", "hid"),
        P(None, "hid"),
        P("hid"),
        P("hid", None),
        P(),
    )
    return jax.shard_map(
        per_device, mesh=mesh, in_specs=in_specs, out_specs=out_specs, check_vma=False
    )
```

```python
import jax
import jax.numpy as jnp
from jax import lax
from jax.experimental import pallas as pl
from jax.experimental.pallas import tpu as pltpu
from jax.sharding import PartitionSpec as P

EPS = 1e-05
MESH = pl.DeviceIdType.MESH
F32 = jnp.float32
BF16 = jnp.bfloat16
CHUNKS = 6
LIMIT = 60 << 20


class Place:
    def __init__(self):
        dom = lax.axis_index("dom")
        self.hid = lax.axis_index("hid")
        self.dom = dom
        self.z = lax.div(dom, 16)
        self.x = lax.rem(lax.div(dom, 4), 4)
        self.yl = lax.rem(lax.div(dom, 2), 2)
        self.y = 2 * self.hid + self.yl
        self.core = lax.rem(dom, 2)

    def at(self, z=None, x=None, y=None, core=None):
        z = self.z if z is None else z
        x = self.x if x is None else x
        y = self.y if y is None else y
        core = self.core if core is None else core
        return (((z * 4 + x) * 2 + lax.rem(y, 2)) * 2 + core, lax.div(y, 2))

    def ring(self, axis, step):
        return self.at(**{axis: lax.rem(getattr(self, axis) + step, 4)})

    def other_core(self):
        return self.at(core=1 - self.core)

    def cross(self):
        return self.at(y=3 - self.y)

    def pair(self):
        return self.at(y=self.y + 1 - 2 * self.yl)

    def partition(self, step):
        return (lax.rem(self.dom + step, 64), self.hid)


def greet(partners):
    barrier = pltpu.get_barrier_semaphore()
    for partner in partners:
        pl.semaphore_signal(barrier, inc=1, device_id=partner, device_id_type=MESH)
    return lambda: pl.semaphore_wait(barrier, len(partners))


def remote(src, dst, send_sem, recv_sem, target):
    return pltpu.make_async_remote_copy(
        src_ref=src,
        dst_ref=dst,
        send_sem=send_sem,
        recv_sem=recv_sem,
        device_id=target,
        device_id_type=MESH,
    )


AXES = (
    ("z", "x", "y"),
    ("x", "z", "y"),
    ("y", "z", "x"),
    ("z", "x", "y"),
    ("x", "z", "y"),
    ("y", "x", "z"),
)


def tiles_known(chunk):
    return 2 if AXES[chunk][2] == "y" else 4


def first_tile(place, chunk, yl=None):
    yl = place.yl if yl is None else yl
    a, b, _ = AXES[chunk]
    if a == "y":
        return (yl * 4 + getattr(place, b)) * 4
    return (getattr(place, a) * 4 + getattr(place, b)) * 2


def rows_of(first, count, unit=16):
    return pl.ds(pl.multiple_of(first * unit, unit), count * unit)


def gather_steps(place, chunk):
    a, b, _ = AXES[chunk]
    ring = [place.ring(b, j) for j in (2, 1, 3)]
    known = tiles_known(chunk)
    if a == "y":
        last = (place.yl * 16, 16, [place.pair()])
    else:
        last = (getattr(place, a) * 8, 8, [place.ring(a, j) for j in (2, 1, 3)])
    return [(first_tile(place, chunk), known, ring), last]


class Gather:
    def __init__(self, place, buf, send_sem, recv_sem, result):
        self.place, self.buf, self.result = place, buf, result
        self.send_sem, self.recv_sem = send_sem, recv_sem
        self.steps = {}
        self.flying = {}

    def start(self, chunk, step):
        place = self.place
        if chunk not in self.steps:
            self.steps[chunk] = gather_steps(place, chunk)
        halved = AXES[chunk][0] == "y"
        if step == 2:
            if halved:
                self.send(chunk, 2, (1 - place.yl) * 16, 16, 6, place.other_core())
                return
            if (chunk, 1) not in self.flying:
                self.send(chunk, 2, 0, 32, 6, place.other_core())
                return
            mine = getattr(place, AXES[chunk][0])
            for at, j in enumerate((2, 1, 3)):
                self.flying[chunk, 1][at].wait_recv()
                self.send(chunk, 2, lax.rem(mine + 4 - j, 4) * 8, 8, 6 + at, place.other_core())
            return
        first, count, targets = self.steps[chunk][step]
        for j, target in enumerate(targets):
            self.send(chunk, step, first, count, 3 * step + j, target)
        if step == 1:
            self.send(chunk, 2, first, count, 9, place.other_core())

    def send(self, chunk, step, first, count, index, target):
        block = 2 * chunk + self.place.core
        part = self.buf.at[block, rows_of(first, count)]
        goal = self.result.at[block, rows_of(first, count)] if step == 2 else part
        copy = remote(part, goal, self.send_sem.at[chunk, index], self.recv_sem.at[chunk, index], target)
        copy.start()
        self.flying.setdefault((chunk, step), []).append(copy)

    def arrived(self, chunk, step):
        if step == 1 and AXES[chunk][0] != "y":
            return
        for copy in self.flying[chunk, step]:
            copy.wait_recv()

    def sent(self):
        for copies in self.flying.values():
            for copy in copies:
                copy.wait_send()


RING = (2, 1, 3)
GATHERED = (3, 4, 2, 1, 5)
DIRECT = (0,)


def tdot(a, b):
    return lax.dot_general(a, b, (((0,), (0,)), ((), ())), preferred_element_type=F32)


def ndot(a, b):
    return lax.dot_general(a, b, (((1,), (1,)), ((), ())), preferred_element_type=F32)


def dot(a, b):
    return jnp.dot(a, b, preferred_element_type=F32)


def dequantize_out(own, w_out_ref, scales):
    for a in range(6):
        for b in range(4):
            value = w_out_ref[128 * a : 128 * a + 128, 128 * b : 128 * b + 128].astype(F32) * scales[b, a]
            if a < 4:
                index, row = b // 2, 128 * a
            else:
                index, row = 2, 128 * (a - 4) + 256 * (b // 2)
            col = 128 * (b % 2)
            own[index, row : row + 128, col : col + 128] = value.astype(BF16)


def dequantize_in(own, w_in_ref, scales, first, last):
    def block(index, _):
        j = lax.div(index, 3)
        r = lax.rem(index, 3)
        for a in range(4):
            for b in range(2):
                scale = scales[2 * j + b, 4 * r + a]
                rows = pl.ds(pl.multiple_of(512 * r + 128 * a, 128), 128)
                cols = pl.ds(pl.multiple_of(256 * j + 128 * b, 128), 128)
                value = w_in_ref[rows, cols].astype(F32) * scale
                own[3 + index, 128 * a : 128 * a + 128, 128 * b : 128 * b + 128] = value.astype(BF16)
        return 0

    lax.fori_loop(first, last, block, 0)


def dequantize_tiles(tile, w_in_ref, scales, index, q, count):
    j = lax.div(index, 3)
    r = lax.rem(index, 3)
    rows = pl.ds(pl.multiple_of(512 * r + 16 * q, 16), 16 * count)
    for b in range(2):
        scale = scales[2 * j + b, 4 * r + lax.div(q, 8)]
        cols = pl.ds(pl.multiple_of(256 * j + 128 * b, 128), 128)
        tile[0 : 16 * count, 128 * b : 128 * b + 128] = (w_in_ref[rows, cols].astype(F32) * scale).astype(BF16)


def dequantize_out_tiles(tile, w_out_ref, scales, q, wanted):
    side = lax.div(q, 16)
    row = lax.rem(q, 16)
    rows = pl.ds(pl.multiple_of(512 + 16 * row, 16), 32)
    for b in range(2):
        scale = scales[2 * side + b, 4 + lax.div(row, 8)]
        cols = pl.ds(pl.multiple_of(256 * side + 128 * b, 128), 128)
        value = w_out_ref[rows, cols].astype(F32) * scale
        kept = tile[0:32, 128 * b : 128 * b + 128].astype(F32)
        tile[0:32, 128 * b : 128 * b + 128] = jnp.where(wanted, value, kept).astype(BF16)


def place_rows(grads, block, first, value, half):
    count = value.shape[0]
    group = 512 if AXES[block // 2][0] == "y" else 32
    size = min(group, count)
    for at in range(0, count, size):
        row = first + at
        base = (row // group) * 2 * group + row % group
        grads[block, pl.ds(pl.multiple_of(base + group * half, 32), size), :] = value[at : at + size]


ORDER = (
    "P1", "A0", "P2", "A1", "P3", "A2", "P4", "A3", "P5", "A4", "A5", "F0",
    "Xa", "F1", "F2", "F3", "Xb", "S0", "F4", "S1", "F5", "S2", "S3", "Xd",
    "T0", "S4", "T1", "S5", "T2", "Xe", "T3", "T4", "T5", "G0", "G1", "G2",
    "G3", "Xc", "G4", "G5", "Xf", "L0", "L1", "L2", "L3", "L4", "L5",
)


class Reduce:
    def __init__(self, place, grads, core_in, first_in, first_out, second_in, second_out, third_in, send_sem, recv_sem):
        self.place, self.grads, self.core_in = place, grads, core_in
        self.first_in, self.first_out = first_in, first_out
        self.second_in, self.second_out, self.third_in = second_in, second_out, third_in
        self.send_sem, self.recv_sem = send_sem, recv_sem
        self.flying = {}

    def send(self, chunk, stage, index, src, dst, target):
        copy = remote(src, dst, self.send_sem.at[chunk, index], self.recv_sem.at[chunk, index], target)
        copy.start()
        self.flying.setdefault((chunk, stage), []).append(copy)

    def arrived(self, chunk, stage):
        for copy in self.flying[chunk, stage]:
            copy.wait_recv()

    def sent(self):
        for copies in self.flying.values():
            for copy in copies:
                copy.wait_send()

    def share(self, chunk):
        core = self.place.core
        src = self.grads.at[2 * chunk + 1 - core]
        self.send(chunk, 0, 0, src, self.core_in.at[chunk], self.place.other_core())

    def spread(self, chunk, level, src, dst, unit):
        axis = AXES[chunk][level]
        mine = getattr(self.place, axis)
        for j in RING:
            at = lax.rem(mine + j, 4)
            part = src.at[rows_of(at, 1, unit)]
            self.send(chunk, level + 1, 3 * level + j, part, dst.at[j - 1], self.place.ring(axis, j))

    def kept(self, chunk, level, src, unit):
        mine = getattr(self.place, AXES[chunk][level])
        return src[rows_of(mine, 1, unit), :].astype(F32)

    def add_core(self, chunk):
        self.arrived(chunk, 0)
        block = 2 * chunk + self.place.core

        def part(i, _):
            rows = pl.ds(pl.multiple_of(i * 128, 128), 128)
            self.grads[block, rows, :] = self.grads[block, rows, :] + self.core_in[chunk, rows, :]
            return 0

        lax.fori_loop(0, 8, part, 0)
        self.spread(chunk, 0, self.grads.at[block], self.first_in.at[chunk], 256)

    def add_first(self, chunk):
        self.arrived(chunk, 1)
        value = self.kept(chunk, 0, self.grads.at[2 * chunk + self.place.core], 256)
        for j in range(3):
            value = value + self.first_in[chunk, j].astype(F32)
        self.first_out[chunk] = value.astype(BF16)
        self.spread(chunk, 1, self.first_out.at[chunk], self.second_in.at[chunk], 64)

    def add_second(self, chunk):
        self.arrived(chunk, 2)
        value = self.kept(chunk, 1, self.first_out.at[chunk], 64)
        for j in range(3):
            value = value + self.second_in[chunk, j].astype(F32)
        self.second_out[chunk] = value.astype(BF16)
        axis = AXES[chunk][2]
        mine = getattr(self.place, axis)
        rows = 16 * tiles_known(chunk)
        if axis == "y":
            self.third_in[chunk, mine, 0:rows, :] = self.second_out[chunk, rows_of(self.place.hid, 1, 32), :]
        else:
            self.third_in[chunk, mine] = self.second_out[chunk]
        for j in RING:
            if axis == "y":
                half = lax.div(lax.rem(mine + j, 4), 2)
                part = self.second_out.at[chunk, rows_of(half, 1, 32)]
            else:
                part = self.second_out.at[chunk]
            goal = self.third_in.at[chunk, mine, pl.ds(0, rows)]
            self.send(chunk, 3, 6 + j, part, goal, self.place.ring(axis, j))

    def add_third(self, chunk):
        self.arrived(chunk, 3)
        rows = 16 * tiles_known(chunk)
        value = self.third_in[chunk, 0, 0:rows, :].astype(F32)
        for at in range(1, 4):
            value = value + self.third_in[chunk, at, 0:rows, :].astype(F32)
        return value


def main_kernel(
    node_hbm,
    edge_hbm,
    send_ref,
    src_ref,
    dst_ref,
    live_ref,
    w_in_hbm,
    w_in_scale,
    bias_ref,
    w_out_hbm,
    w_out_scale,
    bias_out_ref,
    gain_ref,
    gedge_hbm,
    gagg_hbm,
    total_hbm,
    grad_edge,
    grad_node,
    summed,
    node,
    w_in,
    w_out,
    gagg,
    gedge,
    weights,
    bias,
    halo,
    halo_out,
    tiles,
    inp,
    inpt,
    ext,
    pick_src,
    pick_dst,
    act,
    slope,
    up,
    msg,
    low,
    pre_low,
    grads,
    core_in,
    first_in,
    first_out,
    second_in,
    second_out,
    third_in,
    total,
    sums,
    sum_core,
    sum_ring,
    own_table,
    halo_table,
    halo_in,
    node_out,
    node_in,
    third_vector,
    act_turned,
    local_sem,
    spread_send,
    spread_recv,
    cross_send,
    cross_recv,
    halo_send,
    halo_recv,
    reduce_send,
    reduce_recv,
    gather_send,
    gather_recv,
    sum_send,
    sum_recv,
    node_send,
    node_recv,
    write_sem,
):
    place = Place()
    hid, dom, core = place.hid, place.dom, place.core
    first_edge = pl.multiple_of(hid * 512, 512)

    def fetch(index, src, dst):
        copy = pltpu.make_async_copy(src, dst, local_sem.at[index])
        copy.start()
        return copy

    get_w_in = fetch(1, w_in_hbm, w_in)
    get_w_out = fetch(0, w_out_hbm, w_out)
    get_node = fetch(2, node_hbm, node)
    get_edge = fetch(3, edge_hbm.at[pl.ds(first_edge, 512)], inp.at[0])
    get_agg = fetch(4, gagg_hbm, gagg)
    get_cot = fetch(5, gedge_hbm.at[pl.ds(first_edge, 512)], gedge)
    partners = [place.ring(axis, j) for axis in "zxy" for j in RING]
    partners += [place.other_core(), place.cross(), place.partition(1), place.partition(63)]
    all_here = greet(partners)
    flying = []

    def go(src, dst, send_sem, recv_sem, target):
        copy = remote(src, dst, send_sem, recv_sem, target)
        copy.start()
        flying.append(copy)
        return copy

    own, other = weights.at[0], weights.at[1]
    bias[0] = jnp.zeros((8, 256), F32)
    for j in range(3):
        bias[0, j : j + 1, 0:128] = bias_ref[2 * j : 2 * j + 1, :]
        bias[0, j : j + 1, 128:256] = bias_ref[2 * j + 1 : 2 * j + 2, :]
    for k in range(4):
        cols = slice(128 * k, 128 * k + 128)
        src_row = src_ref[pl.ds(4 * hid + k, 1), :]
        dst_row = dst_ref[pl.ds(4 * hid + k, 1), :]
        pick_src[:, cols] = (lax.broadcasted_iota(jnp.int32, (384, 128), 0) == src_row).astype(F32).astype(BF16)
        pick_dst[:, cols] = (lax.broadcasted_iota(jnp.int32, (256, 128), 0) == dst_row).astype(F32).astype(BF16)
    get_node.wait()
    for side in (0, 1):
        picks = (lax.broadcasted_iota(jnp.int32, (256, 64), 0) == send_ref[side : side + 1, :]).astype(F32)
        halo_out[side] = tdot(picks.astype(BF16), node[...]).astype(BF16)
    get_w_in.wait()
    tile_at = {}
    for chunk in GATHERED:
        known = tiles_known(chunk)
        index = 2 * chunk + core - 3
        if chunk == 1:
            index = 0
        tile_at[chunk] = first_tile(place, chunk, 1 - place.yl)
        dequantize_tiles(tiles.at[chunk - 1], w_in, w_in_scale, index, tile_at[chunk], known)
    get_w_out.wait()
    dequantize_out_tiles(tiles.at[0], w_out, w_out_scale, tile_at[1], core == 0)
    all_here()
    crossing = {}

    def cross(chunk, src, dst):
        crossing[chunk] = go(src, dst, cross_send.at[chunk], cross_recv.at[chunk], place.cross())

    for chunk in GATHERED:
        rows = 16 * tiles_known(chunk)
        goal = other.at[2 * chunk + core, pl.ds(pl.multiple_of(16 * tile_at[chunk], 16), rows)]
        cross(chunk, tiles.at[chunk - 1, pl.ds(0, rows)], goal)
    up_rows = go(halo_out.at[1], halo.at[0], halo_send.at[0], halo_recv.at[0], place.partition(1))
    down_rows = go(halo_out.at[0], halo.at[1], halo_send.at[1], halo_recv.at[1], place.partition(63))
    bias_copy = go(bias.at[0], bias.at[1], cross_send.at[6], cross_recv.at[6], place.cross())
    dequantize_out(own, w_out, w_out_scale)
    dequantize_in(own, w_in, w_in_scale, 0, 1)
    for chunk in DIRECT:
        cross(chunk, own.at[2 * chunk + core], other.at[2 * chunk + core])
    spread = Gather(place, other, spread_send, spread_recv, other)
    for chunk in GATHERED:
        crossing[chunk].wait_recv()
        spread.start(chunk, 0)
    dequantize_in(own, w_in, w_in_scale, 1, 9)
    inp[2] = tdot(pick_dst[...], node[...]).astype(BF16)
    get_agg.wait()
    up[...] = tdot(pick_dst[...], gagg[...])
    ext[0:256] = node[...]
    for chunk in GATHERED:
        spread.arrived(chunk, 0)
        spread.start(chunk, 1)
    up_rows.wait_recv()
    down_rows.wait_recv()
    ext[256:320] = jnp.where(dom > 0, halo[0], jnp.zeros((64, 512), BF16))
    ext[320:384] = jnp.where(dom < 63, halo[1], jnp.zeros((64, 512), BF16))
    inp[1] = tdot(pick_src[...], ext[...]).astype(BF16)
    get_edge.wait()

    live = live_ref[0] - hid * 512

    def fold(value):
        return jnp.sum(value.reshape(8, 8, 512), axis=0)

    def mask_upstream(i, carry):
        rows = pl.ds(pl.multiple_of(i * 64, 64), 64)
        mask = (lax.broadcasted_iota(jnp.int32, (64, 512), 0) + i * 64) < live
        upstream = jnp.where(mask, gedge[rows, :].astype(F32) + up[rows, :], 0.0)
        up[rows, :] = upstream
        return carry + fold(upstream)

    def message_part(slot, side):
        result = dot(act[3 * slot + 2], weights[slot, 2, 256 * side : 256 * side + 256, :])
        for j in range(2):
            result = result + dot(act[3 * slot + j], weights[slot, side, 256 * j : 256 * j + 256, :])
        return result

    def prepare():
        for side in range(2):
            cols = slice(256 * side, 256 * side + 256)
            msg[:, cols] = bias_out_ref[:, cols] + message_part(0, side)
        get_cot.wait()
        third_vector[...] = lax.fori_loop(0, 8, mask_upstream, jnp.zeros((8, 512), F32))
        for j in range(3):
            act_turned[j] = act[j].T

    def forward(slot, j):
        pre = bias[slot, pl.ds(j, 1), :]
        for r in range(3):
            pre = pre + dot(inp[r], weights[slot, 3 + 3 * j + r])
        sigma = 1.0 / (1.0 + jnp.exp(-pre))
        value = pre * sigma
        act[3 * slot + j] = value.astype(BF16)
        slope[3 * slot + j] = sigma + value * (1.0 - sigma)

    def forward_own(j, _):
        forward(0, j)
        return 0

    lax.fori_loop(0, 3, forward_own, 0)
    for chunk in DIRECT:
        crossing[chunk].wait_recv()
        spread.start(chunk, 2)
    for chunk in GATHERED:
        spread.arrived(chunk, 1)
        spread.start(chunk, 2)
    for r in range(3):
        inpt[r] = inp[r].T
    prepare()
    bias_copy.wait_recv()
    for chunk in (3, 4):
        spread.arrived(chunk, 2)
    forward(1, 1)
    for chunk in (1, 2):
        spread.arrived(chunk, 2)
    forward(1, 0)
    spread.arrived(5, 2)
    forward(1, 2)
    spread.arrived(0, 2)

    for side in range(2):
        cols = slice(256 * side, 256 * side + 256)
        msg[:, cols] = msg[:, cols] + message_part(1, side)

    gain = gain_ref[...]

    def norm(i, carry):
        rows = pl.ds(pl.multiple_of(i * 64, 64), 64)
        upstream = up[rows, :]
        message = msg[rows, :]
        centre = message - jnp.mean(message, axis=1, keepdims=True)
        inverse = lax.rsqrt(jnp.mean(centre * centre, axis=1, keepdims=True) + EPS)
        normed = centre * inverse
        scaled = upstream * gain
        shift = jnp.mean(scaled, axis=1, keepdims=True)
        tilt = jnp.mean(scaled * normed, axis=1, keepdims=True)
        grad = inverse * (scaled - shift - normed * tilt)
        low[rows, :] = grad.astype(BF16)
        return (carry[0] + fold(grad), carry[1] + fold(upstream * normed))

    zero = jnp.zeros((8, 512), F32)
    vectors = lax.fori_loop(0, 8, norm, (zero, zero))
    vectors = (*vectors, third_vector[...])
    sums[...] = jnp.zeros((16, 256), F32)
    for i in range(3):
        row = jnp.sum(vectors[i], axis=0, keepdims=True)
        sums[6 + 2 * i : 7 + 2 * i, :] = row[:, 0:256]
        sums[7 + 2 * i : 8 + 2 * i, :] = row[:, 256:512]

    reduce = Reduce(
        place, grads, core_in, first_in, first_out, second_in, second_out, third_in, reduce_send, reduce_recv
    )
    gather = Gather(place, total, gather_send, gather_recv, total_hbm)
    halves = (hid, 1 - hid)
    for slot in range(2):
        for j in range(3):
            if slot == 0:
                part = dot(act_turned[j], low[...]).astype(BF16)
            else:
                part = tdot(act[3 + j], low[...]).astype(BF16)
            if j < 2:
                place_rows(grads, 0, 256 * j, part[:, 0:256], halves[slot])
                place_rows(grads, 1, 256 * j, part[:, 256:512], halves[slot])
            else:
                place_rows(grads, 2, 0, part[:, 0:256], halves[slot])
                place_rows(grads, 2, 256, part[:, 256:512], halves[slot])
    reduce.share(0)
    for slot in range(2):
        for j in range(3):
            if j < 2:
                rows = slice(256 * j, 256 * j + 256)
                grad = ndot(low[:, 0:256], weights[slot, 0, rows, :])
                grad = grad + ndot(low[:, 256:512], weights[slot, 1, rows, :])
            else:
                grad = ndot(low[:, 0:256], weights[slot, 2, 0:256, :])
                grad = grad + ndot(low[:, 256:512], weights[slot, 2, 256:512, :])
            grad = grad * slope[3 * slot + j]
            sums[pl.ds(3 * halves[slot] + j, 1), :] = jnp.sum(grad, axis=0, keepdims=True)
            pre_low[3 * slot + j] = grad.astype(BF16)
    sum_copy = go(sums, sum_core.at[0], sum_send.at[0, 0], sum_recv.at[0, 0], place.other_core())

    def first_layer(m):
        for slot in range(2):
            part = dot(inpt[m % 3], pre_low[3 * slot + m // 3]).astype(BF16)
            place_rows(grads, 3 + m, 0, part, halves[slot])

    def produce(chunk):
        if chunk > 1:
            first_layer(2 * chunk - 3)
        first_layer(2 * chunk - 2)
        reduce.share(chunk)

    def input_grads(r):
        result = jnp.zeros((512, 512), F32)
        for slot in range(2):
            for j in range(3):
                result = result + ndot(pre_low[3 * slot + j], weights[slot, 3 + 3 * j + r])
        return result

    ring_copies = []

    def sums_ring(level, value):
        axis = "zxy"[level]
        mine = getattr(place, axis)
        sum_ring[level, mine] = value
        ring_copies.clear()
        for j in RING:
            part = sum_ring.at[level, mine]
            ring_copies.append(
                go(part, part, sum_send.at[1 + level, j], sum_recv.at[1 + level, j], place.ring(axis, j))
            )

    def ring_sum(level):
        for copy in ring_copies:
            copy.wait_recv()
        return sum_ring[level, 0] + sum_ring[level, 1] + sum_ring[level, 2] + sum_ring[level, 3]

    def extra_a():
        table = dot(pick_src[...], input_grads(1).astype(BF16))
        own_table[...] = table[0:256]
        halo_table[...] = table[256:384].astype(BF16)
        extra["up"] = go(halo_table.at[64:128], halo_in.at[0], node_send.at[0], node_recv.at[0], place.partition(1))
        extra["down"] = go(halo_table.at[0:64], halo_in.at[1], node_send.at[1], node_recv.at[1], place.partition(63))
        sum_copy.wait_recv()
        sums_ring(0, sums[...] + sum_core[0])

    def extra_b():
        own_table[...] += dot(pick_dst[...], input_grads(2).astype(BF16))

    def extra_c():
        grad_edge[...] = (input_grads(0) + up[...]).astype(BF16)

    def extra_d():
        extra["up"].wait_recv()
        extra["down"].wait_recv()
        value = own_table[...]
        for side in (0, 1):
            picks = (lax.broadcasted_iota(jnp.int32, (256, 64), 0) == send_ref[side : side + 1, :]).astype(F32)
            there = (dom < 63) if side == 1 else (dom > 0)
            picks = jnp.where(there, picks, 0.0).astype(BF16)
            value = value + dot(picks, halo_in[side])
        own_table[...] = value
        node_out[...] = jnp.where(hid == 0, value[:, 256:512], value[:, 0:256]).astype(BF16)
        extra["swap"] = go(node_out, node_in, node_send.at[2], node_recv.at[2], (dom, 1 - hid))
        sums_ring(1, ring_sum(0))

    def extra_e():
        sums_ring(2, ring_sum(1))

    def extra_f():
        extra["swap"].wait_recv()
        keep = jnp.where(hid == 0, own_table[:, 0:256], own_table[:, 256:512])
        grad_node[...] = (keep + node_in[...].astype(F32)).astype(BF16)
        summed[...] = ring_sum(2) * (1.0 / 1024)

    extra = {}
    writes = []

    def write(chunk):
        block = 2 * chunk + core
        copy = pltpu.make_async_copy(total.at[block], total_hbm.at[block], write_sem.at[chunk])
        copy.start()
        writes.append(copy)

    def stage(name, chunk):
        if name == "A":
            reduce.add_core(chunk)
        elif name == "F":
            reduce.add_first(chunk)
        elif name == "S":
            reduce.add_second(chunk)
        elif name == "T":
            value = reduce.add_third(chunk) * (1.0 / 1024)
            rows = pl.ds(pl.multiple_of(16 * first_tile(place, chunk), 16), 16 * tiles_known(chunk))
            total[2 * chunk + core, rows, :] = value.astype(BF16)
            gather.start(chunk, 0)
        elif name == "G":
            gather.arrived(chunk, 0)
            gather.start(chunk, 1)
        else:
            gather.arrived(chunk, 1)
            gather.start(chunk, 2)
            write(chunk)

    work = {"a": extra_a, "b": extra_b, "c": extra_c, "d": extra_d, "e": extra_e, "f": extra_f}
    for name, item in ORDER:
        if name == "X":
            work[item]()
        elif name == "P":
            produce(int(item))
        else:
            stage(name, int(item))
    for chunk in range(CHUNKS):
        gather.arrived(chunk, 2)
    spread.sent()
    reduce.sent()
    gather.sent()
    for copy in flying:
        copy.wait_send()
    for copy in writes:
        copy.wait()


def finish_kernel(
    total, edge_in, node_in, summed, w_out, w_in, bias, vectors, grad_edge, grad_node, raw, wide, read_sem, write_sem
):
    hid = lax.axis_index("hid")
    moves = [
        pltpu.make_async_copy(total.at[block], raw.at[block], read_sem.at[block]) for block in range(12)
    ]
    for copy in moves:
        copy.start()
    grad_edge[...] = edge_in[...]
    grad_node[...] = node_in[...]
    for i in range(3):
        vectors[i : i + 1, 0:256] = summed[6 + 2 * i : 7 + 2 * i, :]
        vectors[i : i + 1, 256:512] = summed[7 + 2 * i : 8 + 2 * i, :]
    picked = jnp.where(hid == 0, summed[0:3, :], summed[3:6, :])
    for j in range(3):
        for k in range(2):
            bias[2 * j + k : 2 * j + k + 1, :] = picked[j : j + 1, 128 * k : 128 * k + 128]
    writes = []
    for block in range(12):
        moves[block].wait()

        def part(i, _):
            rows = pl.ds(pl.multiple_of(i * 128, 128), 128)
            wide[block, rows, :] = raw[block, rows, :].astype(F32)
            return 0

        lax.fori_loop(0, 4, part, 0)
        if block < 2:
            parts = [(wide.at[block], w_out.at[0:512, 256 * block : 256 * block + 256])]
        elif block == 2:
            parts = [
                (wide.at[2, 0:256], w_out.at[512:768, 0:256]),
                (wide.at[2, 256:512], w_out.at[512:768, 256:512]),
            ]
        else:
            r, j = (block - 3) % 3, (block - 3) // 3
            parts = [(wide.at[block], w_in.at[512 * r : 512 * r + 512, 256 * j : 256 * j + 256])]
        for src, dst in parts:
            copy = pltpu.make_async_copy(src, dst, write_sem.at[len(writes)])
            copy.start()
            writes.append(copy)
    for copy in writes:
        copy.wait()


def vmem():
    return pl.BlockSpec(memory_space=pltpu.VMEM)


def smem():
    return pl.BlockSpec(memory_space=pltpu.SMEM)


def anywhere():
    return pl.BlockSpec(memory_space=pl.ANY)


def shape(dims, dtype):
    return jax.ShapeDtypeStruct(dims, dtype)


def dma(*dims):
    return pltpu.SemaphoreType.DMA(dims)


def per_device(
    node_latent,
    edge_latent,
    send_rows,
    edge_src,
    edge_dst,
    edge_live,
    w_in_blocks,
    w_in_scale,
    bias_in,
    w_out_blocks,
    w_out_scale,
    bias_out,
    norm_gain,
    grad_edge,
    grad_agg,
):
    total, edge_in, node_in, summed = pl.pallas_call(
        main_kernel,
        out_shape=(
            shape((12, 512, 256), BF16),
            shape((512, 512), BF16),
            shape((256, 256), BF16),
            shape((16, 256), F32),
        ),
        in_specs=[
            anywhere(),
            anywhere(),
            vmem(),
            vmem(),
            vmem(),
            smem(),
            anywhere(),
            smem(),
            vmem(),
            anywhere(),
            smem(),
            vmem(),
            vmem(),
            anywhere(),
            anywhere(),
        ],
        out_specs=(anywhere(), vmem(), vmem(), vmem()),
        scratch_shapes=[
            pltpu.VMEM((256, 512), BF16),
            pltpu.VMEM((1536, 768), BF16),
            pltpu.VMEM((768, 512), BF16),
            pltpu.VMEM((256, 512), BF16),
            pltpu.VMEM((512, 512), BF16),
            pltpu.VMEM((2, 12, 512, 256), BF16),
            pltpu.VMEM((2, 8, 256), F32),
            pltpu.VMEM((2, 64, 512), BF16),
            pltpu.VMEM((2, 64, 512), BF16),
            pltpu.VMEM((5, 64, 256), BF16),
            pltpu.VMEM((3, 512, 512), BF16),
            pltpu.VMEM((3, 512, 512), BF16),
            pltpu.VMEM((384, 512), BF16),
            pltpu.VMEM((384, 512), BF16),
            pltpu.VMEM((256, 512), BF16),
            pltpu.VMEM((6, 512, 256), BF16),
            pltpu.VMEM((6, 512, 256), F32),
            pltpu.VMEM((512, 512), F32),
            pltpu.VMEM((512, 512), F32),
            pltpu.VMEM((512, 512), BF16),
            pltpu.VMEM((6, 512, 256), BF16),
            pltpu.VMEM((12, 1024, 256), BF16),
            pltpu.VMEM((6, 1024, 256), BF16),
            pltpu.VMEM((6, 3, 256, 256), BF16),
            pltpu.VMEM((6, 256, 256), BF16),
            pltpu.VMEM((6, 3, 64, 256), BF16),
            pltpu.VMEM((6, 64, 256), BF16),
            pltpu.VMEM((6, 4, 64, 256), BF16),
            pltpu.VMEM((12, 512, 256), BF16),
            pltpu.VMEM((16, 256), F32),
            pltpu.VMEM((1, 16, 256), F32),
            pltpu.VMEM((3, 4, 16, 256), F32),
            pltpu.VMEM((256, 512), F32),
            pltpu.VMEM((128, 512), BF16),
            pltpu.VMEM((2, 64, 512), BF16),
            pltpu.VMEM((256, 256), BF16),
            pltpu.VMEM((256, 256), BF16),
            pltpu.VMEM((8, 512), F32),
            pltpu.VMEM((3, 256, 512), BF16),
            dma(6),
            dma(6, 10),
            dma(6, 10),
            dma(7),
            dma(7),
            dma(2),
            dma(2),
            dma(6, 10),
            dma(6, 10),
            dma(6, 10),
            dma(6, 10),
            dma(4, 4),
            dma(4, 4),
            dma(3),
            dma(3),
            dma(6),
        ],
        compiler_params=pltpu.CompilerParams(
            collective_id=0, has_side_effects=True, vmem_limit_bytes=LIMIT
        ),
        name="message_grads",
    )(
        node_latent,
        edge_latent,
        send_rows[0],
        edge_src.reshape(8, 128),
        edge_dst.reshape(8, 128),
        edge_live,
        w_in_blocks,
        w_in_scale.T,
        bias_in.reshape(6, 128),
        w_out_blocks,
        w_out_scale.T,
        bias_out.reshape(1, 512),
        norm_gain.reshape(1, 512),
        grad_edge,
        grad_agg,
    )
    grad_w_out, grad_w_in, grad_bias, vectors, grad_edge_in, grad_node = pl.pallas_call(
        finish_kernel,
        out_shape=(
            shape((768, 512), F32),
            shape((1536, 768), F32),
            shape((6, 128), F32),
            shape((3, 512), F32),
            shape((512, 512), BF16),
            shape((256, 256), BF16),
        ),
        in_specs=[anywhere(), vmem(), vmem(), vmem()],
        out_specs=(anywhere(), anywhere(), vmem(), vmem(), vmem(), vmem()),
        scratch_shapes=[
            pltpu.VMEM((12, 512, 256), BF16),
            pltpu.VMEM((12, 512, 256), F32),
            dma(12),
            dma(13),
        ],
        compiler_params=pltpu.CompilerParams(vmem_limit_bytes=LIMIT),
        name="widen_grads",
    )(total, edge_in, node_in, summed)
    return (grad_edge_in, grad_node, grad_w_in, grad_bias.reshape(768), grad_w_out, vectors)


def solution(mesh):
    in_specs = (
        P("dom", None),
        P("dom", None),
        P("dom", None, None),
        P("dom"),
        P("dom"),
        P("dom"),
        P(None, "hid"),
        P(None, "hid"),
        P("hid"),
        P("hid", None),
        P("hid", None),
        P(),
        P(),
        P("dom", None),
        P("dom", None),
    )
    out_specs = (
        P(("dom", "hid"), None),
        P("dom", "hid"),
        P(None, "hid"),
        P("hid"),
        P("hid", None),
        P(),
    )
    return jax.shard_map(
        per_device, mesh=mesh, in_specs=in_specs, out_specs=out_specs, check_vma=False
    )
```
